32 devices in a mesh: dp: 2 (over core), expert: 4 (over y, x), tensor: 4 (over z).
Axes of the slice: x: 2, y: 2, z: 4, core: 2. Of those that a mesh axis runs over, the one named last changes fastest.
Arguments:
- tokens: bfloat16 [8, 197, 768], P(('dp', 'expert')), may hold values from -6 to 6
- cotangent: bfloat16 [8, 197, 768], P(('dp', 'expert')), may hold values from -6 to 6
- routes: int32 [2, 8, 197, 2], P(None, ('dp', 'expert')), may hold values from 0 to 7, all different within a row; in each aligned block of 197 rows (0 to 196, 197 to 393, ..., all dimensions but the last counted through in order) at most 73 rows name the same one
- norm_gain: float32 [2, 2, 768], replicated, may hold values from 0.25 to 1.75
- norm_bias: float32 [2, 2, 768], replicated, may hold values from -1.25 to 1.25
- w_qkv: bfloat16 [2, 768, 3, 768], P(None, None, None, 'tensor'), may hold values from -0.21875 to 0.21875
- b_qv: float32 [2, 2, 768], P(None, None, 'tensor'), may hold values from -3 to 3
- w_out: bfloat16 [2, 768, 768], P(None, 'tensor'), may hold values from -1.5 to 1.5
- b_out: float32 [2, 768], replicated, may hold values from -1.75 to 1.75
- w_router: float32 [2, 768, 8], replicated, may hold values from -0.15625 to 0.15625
- w_in: bfloat16 [2, 8, 768, 3072], P(None, ('dp', 'expert'), None, 'tensor'), may hold values from -0.21875 to 0.21875
- b_in: float32 [2, 8, 3072], P(None, ('dp', 'expert'), 'tensor'), may hold values from -1.75 to 1.75
- w_exp_out: bfloat16 [2, 8, 3072, 768], P(None, ('dp', 'expert'), 'tensor'), may hold values from -0.875 to 0.875
- b_exp_out: float32 [2, 8, 768], P(None, ('dp', 'expert')), may hold values from -3 to 3
Outputs:
- output: float32 [8, 197, 768], P(('dp', 'expert'))
- grad_tokens: float32 [8, 197, 768], P(('dp', 'expert'))
- grad_norm_gain: float32 [2, 2, 768], replicated
- grad_norm_bias: float32 [2, 2, 768], replicated
- grad_w_qkv: float32 [2, 768, 3, 768], P(None, None, None, 'tensor')
- grad_b_qv: float32 [2, 2, 768], P(None, None, 'tensor')
- grad_w_out: float32 [2, 768, 768], P(None, 'tensor')
- grad_b_out: float32 [2, 768], replicated
- grad_w_router: float32 [2, 768, 8], replicated
- grad_w_in: float32 [2, 8, 768, 3072], P(None, ('dp', 'expert'), None, 'tensor')
- grad_b_in: float32 [2, 8, 3072], P(None, ('dp', 'expert'), 'tensor')
- grad_w_exp_out: float32 [2, 8, 3072, 768], P(None, ('dp', 'expert'), 'tensor')
- grad_b_exp_out: float32 [2, 8, 768], P(None, ('dp', 'expert'))
The draws below stay inside these ranges and needn't reach their ends.
Inputs may be any that keep to these rules, and one draw needn't show every extreme that they name: `routes`: A token's two experts differ; among the tokens of one group in one block no expert is named more than 73 times, a bound that some block reaches.
All inputs are finite; a program needn't handle non-finite values.
Results may differ from the reference program's by a relative error of at most 0.024.
Values may be sent and summed in bfloat16 or wider, within the bound.
No kernel may reach another device: no remote copies, remote signals or barrier semaphores. Data moves between devices by JAX's collectives and lax.ppermute only.
A program may use at most 128 MiB of HBM per device.

```python
import math
import jax
import jax.numpy as jnp
import numpy as np
from jax import lax

D = 768
HEADS = 12
HEAD_DIM = 64
FF = 3072
SEQ = 197
LAYERS = 2
IMG_DEV = 1
HD = 768
TOK_DEV = 197
IMAGES = 8
EXPERTS = 8
CAPACITY = 73
N_DP = 2
N_EXPERT = 4


def shard_levels(rng, extent, cuts, low, top_value):
    factor_of = 1.0
    for axis_at, shards_of in cuts:
        heights = jax.random.uniform(jax.random.fold_in(jax.random.fold_in(rng, 6), axis_at), (shards_of,), jnp.float32, low / len(cuts), top_value / len(cuts))
        factor_of = factor_of * jnp.repeat(jnp.exp(heights), extent[axis_at] // shards_of).reshape((-1,) + (1,) * (len(extent) - 1 - axis_at))
    return factor_of


def shared_out(own_key, own, number, rows, count, top, bound, lean):
    sequence = jax.random.permutation(own_key, count)
    heavy_load, usual = load_shares(count, rows * top, bound, lean, True), load_shares(count, rows * top, bound, lean, False)
    places = jnp.arange(count)

    def named(sizes, offset_by):
        used = int((sizes > 0).sum())
        fixed = max(1, used // 4)
        passed = fixed + (places - fixed + offset_by * (used - fixed)) % max(1, count - fixed)
        return jnp.zeros((count,), jnp.int32).at[sequence[jnp.where(places < fixed, places, passed)]].set(jnp.asarray(sizes, jnp.int32))

    sizes = jnp.where(number % 4 == 0, named(heavy_load, number // 4), named(usual, number - number // 4 - 1))
    mixed = jax.random.permutation(jax.random.fold_in(own, 3), count)
    giver, taker = mixed[0:count // 2 * 2:2], mixed[1:count // 2 * 2:2]
    room = jnp.minimum(sizes[giver] - 1, bound - sizes[taker]) // 2
    room = jnp.where((giver == sequence[0]) | (taker == sequence[0]) | (sizes[taker] == 0), 0, jnp.maximum(room, 0))
    passed = jax.random.randint(jax.random.fold_in(own, 4), (count // 2,), 0, 1 << 20) % (room + 1)
    sizes = sizes.at[giver].add(-passed).at[taker].add(passed)
    items = jnp.searchsorted(jnp.cumsum(sizes), jnp.arange(rows * top), side="right").astype(jnp.int32)
    grid = items.reshape(top, rows).T
    grid = grid[jax.random.permutation(jax.random.fold_in(own, 1), rows)]
    offset_by = jax.random.randint(jax.random.fold_in(own, 2), (rows, 1), 0, top)
    return jnp.take_along_axis(grid, (jnp.arange(top)[None, :] + offset_by) % top, axis=1)


def load_shares(count, total, most, lean, full):
    weights = [(1 << 20) // math.isqrt(standing ** lean) + 1 for standing in range(1, count + 1)]
    largest = most if full else min(most, max(-(-total // count), total * weights[0] // sum(weights)))
    least = 1 if total - largest >= count - 1 else 0
    counts, surplus = [largest] + [least] * (count - 1), total - largest - least * (count - 1)
    while surplus > 0:
        free = [i for i in range(1, count) if counts[i] < largest] or [i for i in range(1, count) if counts[i] < most]
        pool, budget = sum([weights[i] for i in free]), surplus
        for i in free:
            addition = min(most - counts[i], max(1, budget * weights[i] // pool), surplus)
            counts[i] = counts[i] + addition
            surplus = surplus - addition
    return np.array(counts)


def noise(rng, shape, scale, bound, cuts=(), kind=jnp.bfloat16):
    values = jax.random.normal(rng, shape, jnp.float32) * scale
    if len(cuts) > 0:
        values = shard_levels(rng, shape, cuts, -0.22, 0.18) * values
    return jnp.clip(values, min=-bound, max=bound).astype(kind)


def setup_inputs(seed: int = 0) -> dict:
    splits = jax.random.split(jax.random.key(seed), 15)
    tokens = noise(splits[0], (IMAGES, SEQ, D), 1.0, 6.0, ((0, 8),))
    cotangent = noise(splits[1], (IMAGES, SEQ, D), 1.0, 6.0, ((0, 8),))
    routes_keys = jax.random.split(jax.random.fold_in(splits[2], 1), LAYERS * IMAGES * SEQ // TOK_DEV)
    routes_turns = jax.random.permutation(jax.random.fold_in(splits[2], 3), LAYERS * IMAGES * SEQ // TOK_DEV)
    routes = jax.vmap(lambda own, number: shared_out(jax.random.fold_in(splits[2], 2), own, number, TOK_DEV, EXPERTS, 2, CAPACITY, 2))(routes_keys, routes_turns).reshape((LAYERS, IMAGES, SEQ, 2))
    norm_gain = jnp.clip(1.0 + 0.15 * jax.random.normal(splits[3], (LAYERS, 2, D), jnp.float32), 0.25, 1.75)
    norm_bias = noise(splits[4], (LAYERS, 2, D), 0.2, 1.25, (), jnp.float32)
    w_qkv = noise(splits[5], (LAYERS, D, 3, HD), D ** -0.5, 0.21875, ((3, 4),))
    b_qv = noise(splits[6], (LAYERS, 2, HD), 0.5, 3.0, ((2, 4),), jnp.float32)
    w_out = noise(splits[7], (LAYERS, HD, D), (4 * HD // SEQ) ** -0.5, 1.5, ((1, 4),))
    b_out = noise(splits[8], (LAYERS, D), 0.3, 1.75, (), jnp.float32)
    w_router = noise(splits[9], (LAYERS, D, EXPERTS), (2 * D) ** -0.5, 0.15625, (), jnp.float32)
    w_in = noise(splits[10], (LAYERS, EXPERTS, D, FF), D ** -0.5, 0.21875, ((1, 8), (3, 4)))
    b_in = noise(splits[11], (LAYERS, EXPERTS, FF), 0.3, 1.75, ((1, 8), (2, 4)), jnp.float32)
    w_exp_out = noise(splits[12], (LAYERS, EXPERTS, FF, D), (max(FF // (EXPERTS * EXPERTS), 1)) ** -0.5, 0.875, ((1, 8), (2, 4)))
    b_exp_out = noise(splits[13], (LAYERS, EXPERTS, D), (0.06 * EXPERTS), 3.0, ((1, 8),), jnp.float32)
    return {"tokens": tokens, "cotangent": cotangent, "routes": routes, "norm_gain": norm_gain, "norm_bias": norm_bias, "w_qkv": w_qkv, "b_qv": b_qv, "w_out": w_out, "b_out": b_out, "w_router": w_router, "w_in": w_in, "b_in": b_in, "w_exp_out": w_exp_out, "b_exp_out": b_exp_out}


epsilon = 1e-06
highest = lax.Precision.HIGHEST

@jax.custom_vjp
def low(v):
    return lax.optimization_barrier(v.astype(jnp.bfloat16)).astype(jnp.float32)

@jax.custom_vjp
def low_back(v):
    return v

def low_keep(v):
    return (low(v), None)

def low_pass(kept, grad):
    return (grad,)

def back_keep(v):
    return (v, None)

def back_low(kept, grad):
    return (low(grad),)
low.defvjp(low_keep, low_pass)
low_back.defvjp(back_keep, back_low)

def layer_norm(stream, gain_row, shift_row):
    row_mean = lax.optimization_barrier(jnp.mean(stream, -1, keepdims=True))
    centered = stream - row_mean
    inv_std = lax.rsqrt(lax.optimization_barrier(jnp.mean(centered * centered, -1, keepdims=True)) + epsilon)
    return centered * inv_std * gain_row + shift_row

def route_index(route_ids, capacity, experts):
    flat_ids = route_ids.reshape(route_ids.shape[:-2] + (-1,)).astype(jnp.int32)
    onehot = (flat_ids[..., None] == jnp.arange(experts, dtype=jnp.int32)).astype(jnp.int32)
    before = (jnp.cumsum(onehot, axis=-2) - onehot).astype(jnp.int32)
    return (flat_ids * capacity + lax.optimization_barrier(jnp.sum(before * onehot, axis=-1))).astype(jnp.int32)

def attend(pieces):
    query_rows, key_rows, value_rows = pieces
    scores = jnp.einsum('shd,thd->hst', query_rows, key_rows, precision=highest) * HEAD_DIM ** (-0.5)
    scores = low_back(scores)
    soft_probs = low(jax.nn.softmax(scores, axis=-1))
    return jnp.einsum('hst,thd->shd', soft_probs, value_rows, precision=highest)

def expert_apply(pieces):
    sent_rows, w_first, b_first, w_second, b_second = pieces
    pre_act = low_back(jnp.einsum('nd,df->nf', sent_rows, w_first, precision=highest) + b_first)
    hidden = low(jax.nn.gelu(pre_act, approximate=False))
    result = jnp.einsum('nf,fd->nd', hidden, w_second, precision=highest) + b_second
    return low_back(low(result))

def one_layer(stream, route_ids, gain_pair, shift_pair, qkv_weight, qv_bias, out_weight, out_bias, router_weight, first_weight, first_bias, second_weight, second_bias):
    images = stream.shape[0]
    model_width = stream.shape[2]
    attn_input = low(layer_norm(stream, gain_pair[0], shift_pair[0]))
    qkv_bias = jnp.stack([qv_bias[0], jnp.zeros_like(qv_bias[0]), qv_bias[1]])
    qkv_proj = jnp.einsum('isd,dje->isje', attn_input, qkv_weight, precision=highest) + qkv_bias
    query_rows = low_back(low(qkv_proj[:, :, 0])).reshape(images, SEQ, HEADS, HEAD_DIM)
    key_rows = low_back(low(qkv_proj[:, :, 1])).reshape(images, SEQ, HEADS, HEAD_DIM)
    value_rows = low_back(low(qkv_proj[:, :, 2])).reshape(images, SEQ, HEADS, HEAD_DIM)
    mixed_heads = lax.map(jax.checkpoint(attend), (query_rows, key_rows, value_rows))
    mixed_heads = low_back(low(mixed_heads.reshape(images, SEQ, HEADS * HEAD_DIM)))
    projected = low_back(jnp.einsum('ise,ed->isd', mixed_heads, out_weight, precision=highest))
    residual = stream + projected + out_bias
    moe_input = low(layer_norm(residual, gain_pair[1], shift_pair[1]))
    gate_probs = jax.nn.softmax(jnp.einsum('isd,de->ise', moe_input, router_weight, precision=highest), axis=-1)
    groups = N_DP * N_EXPERT
    token_count = IMG_DEV * SEQ
    flat_input = moe_input.reshape(groups, token_count, model_width)
    route_pairs = route_ids.reshape(groups, token_count, 2).astype(jnp.int32)
    slot_index = route_index(route_pairs, CAPACITY, EXPERTS)
    group_base = (jnp.arange(groups, dtype=jnp.int32) * (EXPERTS * CAPACITY))[:, None]
    places = (slot_index + group_base).reshape(-1)
    sent_rows = low_back(jnp.repeat(flat_input, 2, axis=1)).reshape(-1, model_width)
    buffer = jnp.zeros((groups * EXPERTS * CAPACITY, model_width), jnp.float32).at[places].add(sent_rows)
    buffer = buffer.reshape(groups, EXPERTS, CAPACITY, model_width).transpose(1, 0, 2, 3)
    buffer = buffer.reshape(EXPERTS, groups * CAPACITY, model_width)
    results = lax.map(jax.checkpoint(expert_apply), (buffer, first_weight, first_bias, second_weight, second_bias))
    results = results.reshape(EXPERTS, groups, CAPACITY, model_width).transpose(1, 0, 2, 3)
    results = results.reshape(-1, model_width)
    chosen = results[places].reshape(groups, token_count, 2, model_width)
    picked = jnp.take_along_axis(gate_probs.reshape(groups, token_count, EXPERTS), route_pairs, axis=2)
    expert_mix = lax.optimization_barrier(jnp.sum(picked[..., None] * chosen, axis=2))
    return residual + expert_mix.reshape(images, SEQ, model_width)

def forward(tokens, routes, norm_gain, norm_bias, w_qkv, b_qv, w_out, b_out, w_router, w_in, b_in, w_exp_out, b_exp_out):
    stream = tokens
    for layer_index in range(LAYERS):
        stream = one_layer(stream, routes[layer_index], norm_gain[layer_index], norm_bias[layer_index], w_qkv[layer_index], b_qv[layer_index], w_out[layer_index], b_out[layer_index], w_router[layer_index], w_in[layer_index], b_in[layer_index], w_exp_out[layer_index], b_exp_out[layer_index])
    return stream

def reference(tokens, cotangent, routes, norm_gain, norm_bias, w_qkv, b_qv, w_out, b_out, w_router, w_in, b_in, w_exp_out, b_exp_out):

    def bound_forward(tokens_f, gain_f, shift_f, qkv_f, qv_f, out_f, outb_f, router_f, first_f, firstb_f, second_f, secondb_f):
        return forward(tokens_f, routes, gain_f, shift_f, qkv_f, qv_f, out_f, outb_f, router_f, first_f, firstb_f, second_f, secondb_f)
    floats = (tokens.astype(jnp.float32), norm_gain.astype(jnp.float32), norm_bias.astype(jnp.float32), w_qkv.astype(jnp.float32), b_qv.astype(jnp.float32), w_out.astype(jnp.float32), b_out.astype(jnp.float32), w_router.astype(jnp.float32), w_in.astype(jnp.float32), b_in.astype(jnp.float32), w_exp_out.astype(jnp.float32), b_exp_out.astype(jnp.float32))
    output, pullback = jax.vjp(bound_forward, *floats)
    gradients = pullback(cotangent.astype(jnp.float32))
    return (output, gradients[0], gradients[1], gradients[2], gradients[3], gradients[4], gradients[5], gradients[6], gradients[7], gradients[8], gradients[9], gradients[10], gradients[11])
```

```python
import functools

import jax
import jax.numpy as jnp
from jax import lax
from jax.experimental import pallas as pl
from jax.experimental.pallas import tpu as pltpu
from jax.sharding import PartitionSpec as P

HEAD_DIM = 64
SCALE = HEAD_DIM ** (-0.5)
LANES = 128
GROUP_AXES = ("dp", "expert")
ALL_AXES = ("dp", "expert", "tensor")

epsilon = 1e-06
root_half = 0.7071067811865476
inv_root_tau = 0.3989422804014327

F32 = jnp.float32
BF16 = jnp.bfloat16
I32 = jnp.int32


def ceil_to(value, step):
    return -(-value // step) * step


def dot(a, b):
    return lax.dot_general(a, b, (((1,), (0,)), ((), ())), preferred_element_type=F32)


def dot_nt(a, b):
    return lax.dot_general(a, b, (((1,), (1,)), ((), ())), preferred_element_type=F32)


def dot_tn(a, b):
    return lax.dot_general(a, b, (((0,), (0,)), ((), ())), preferred_element_type=F32)


def split_two(v):
    high = v.astype(BF16)
    return high, (v - high.astype(F32)).astype(BF16)


class Far:
    def __init__(self, array, index=None):
        self.array, self.index = array, index
        self.shape = array.shape if index is None else array.shape[1:]


class Near:
    def __init__(self, array, index):
        self.array, self.index = array, index


class Fetched:
    def __init__(self, copy, ref):
        self.copy, self.ref, self.shape = copy, ref, ref.shape

    def __getitem__(self, at):
        if self.copy is not None:
            self.copy.wait()
            self.copy = None
        return self.ref[at]


class Kept:
    def __init__(self, ref, far_ref, sems):
        self.ref, self.far_ref, self.sems, self.shape = ref, far_ref, sems, ref.shape
        self.copies = []

    def __setitem__(self, at, value):
        self.ref[at] = value
        if at is Ellipsis:
            pair = self.ref, self.far_ref
        else:
            pair = self.ref.at[at], self.far_ref.at[at]
        copy = pltpu.make_async_copy(*pair, self.sems.at[len(self.copies)])
        copy.start()
        self.copies.append(copy)

    def __getitem__(self, at):
        return self.ref[at]


def kernel_call(body, ins, outs, scratch=(), scalars=0, vmem=16, name=None):
    fars = [i for i, v in enumerate(ins) if isinstance(v, Far)]
    keeps = [i for i, v in enumerate(outs) if len(v) > 2]
    arrays = [
        pltpu.with_memory_space_constraint(v.array, pltpu.HBM)
        if isinstance(v, Far)
        else v.array
        if isinstance(v, Near)
        else v
        for v in ins
    ]
    extra = [pltpu.VMEM(ins[i].shape, ins[i].array.dtype) for i in fars]
    extra += [pltpu.VMEM(outs[i][0], outs[i][1]) for i in keeps]
    extra += [pltpu.SemaphoreType.DMA((1,)) for _ in fars]
    extra += [pltpu.SemaphoreType.DMA((outs[i][2],)) for i in keeps]

    def whole(*refs):
        refs = list(refs)
        own = refs[len(ins) + len(outs) :]
        buffers, sems = own[: len(fars) + len(keeps)], own[len(fars) + len(keeps) :]
        sems, rest = sems[: len(buffers)], sems[len(buffers) :]
        for i, v in enumerate(ins):
            if isinstance(v, Near):
                refs[i] = refs[i].at[v.index]
        for at, i in enumerate(fars):
            source = refs[i] if ins[i].index is None else refs[i].at[ins[i].index]
            copy = pltpu.make_async_copy(source, buffers[at], sems[at].at[0])
            copy.start()
            refs[i] = Fetched(copy, buffers[at])
        for at, i in enumerate(keeps, len(fars)):
            refs[len(ins) + i] = Kept(buffers[at], refs[len(ins) + i], sems[at])
        body(*refs[: len(ins) + len(outs)], *rest)
        for i in fars:
            refs[i][...]
        for i in keeps:
            for copy in refs[len(ins) + i].copies:
                copy.wait()

    def space(i):
        if i < scalars:
            return pltpu.SMEM
        return pltpu.HBM if i in fars else pltpu.VMEM

    return pl.pallas_call(
        whole,
        out_shape=[
            pltpu.HBM(*v[:2]) if len(v) > 2 else jax.ShapeDtypeStruct(*v) for v in outs
        ],
        in_specs=[pl.BlockSpec(memory_space=space(i)) for i in range(len(ins))],
        out_specs=[
            pl.BlockSpec(memory_space=pltpu.HBM if i in keeps else pltpu.VMEM)
            for i in range(len(outs))
        ],
        scratch_shapes=extra + list(scratch),
        compiler_params=pltpu.CompilerParams(vmem_limit_bytes=vmem * 1024 * 1024),
        name=name,
    )(*arrays)


def pinned(array):
    return pltpu.with_memory_space_constraint(array, pltpu.HBM)


def block_call(body, ins, outs, grid, in_specs, out_specs, vmem=28, aliases=None, name=None):
    return pl.pallas_call(
        body,
        out_shape=[pltpu.HBM(shape, dtype) for shape, dtype in outs],
        grid=grid,
        in_specs=in_specs,
        out_specs=out_specs,
        input_output_aliases=aliases or {},
        compiler_params=pltpu.CompilerParams(vmem_limit_bytes=vmem * 1024 * 1024),
        name=name,
    )(*ins)


def load_rows(ref, scratch):
    if ref.shape[0] == scratch.shape[0]:
        return ref[...].astype(F32)
    scratch[...] = jnp.zeros_like(scratch)
    scratch[: ref.shape[0], :] = ref[...].astype(F32)
    return scratch[...]


def norm_parts(stream):
    row_mean = jnp.mean(stream, -1, keepdims=True)
    centered = stream - row_mean
    inv_std = lax.rsqrt(jnp.mean(centered * centered, -1, keepdims=True) + epsilon)
    return centered * inv_std, inv_std


def norm_back(upstream, normed, inv_std, gain_row):
    scaled = upstream * gain_row
    return inv_std * (
        scaled
        - jnp.mean(scaled, -1, keepdims=True)
        - normed * jnp.mean(scaled * normed, -1, keepdims=True)
    )


def head_mask(head, width):
    lane = lax.broadcasted_iota(I32, (1, width), 1)
    return (lane >= head * HEAD_DIM) & (lane < (head + 1) * HEAD_DIM)


def only_head(rows, head):
    return jnp.where(head_mask(head, rows.shape[1]), rows, jnp.zeros_like(rows))


def put_pieces(me_ref, value, scratch, out_refs):
    count = len(out_refs)
    chunk = out_refs[0].shape[0]
    scratch[...] = value
    for step, ref in enumerate(out_refs):
        owner = lax.rem(me_ref[0] + step, count)
        ref[...] = scratch[pl.ds(pl.multiple_of(owner * chunk, 8), chunk), :].astype(BF16)


def take_pieces(me_ref, in_refs, scratch):
    count = len(in_refs)
    chunk = in_refs[0].shape[0]
    for step, ref in enumerate(in_refs):
        owner = lax.rem(me_ref[0] + count - step, count)
        scratch[pl.ds(pl.multiple_of(owner * chunk, 8), chunk), :] = ref[...].astype(F32)
    return scratch[...]


def picked_probs(gate, ids):
    lane = lax.broadcasted_iota(I32, gate.shape, 1)
    return [
        jnp.sum(jnp.where(lane == ids[:, k : k + 1], gate, 0.0), -1, keepdims=True) for k in range(2)
    ]


def slot_pick_rows(slot_row, slots):
    tokens = slot_row.shape[1]
    at = lax.broadcasted_iota(I32, (slots, tokens), 0)
    return [jnp.where(at == slot_row[k : k + 1, :], 1.0, 0.0).astype(BF16) for k in range(2)]


def slot_pick_cols(slot_col, slots):
    tokens = slot_col.shape[0]
    at = lax.broadcasted_iota(I32, (tokens, slots), 1)
    return [jnp.where(at == slot_col[:, k : k + 1], 1.0, 0.0).astype(BF16) for k in range(2)]


def gelu_parts(pre_act):
    half = 0.5 * (1.0 + lax.erf(pre_act * root_half))
    return pre_act * half, half


def gelu_slope(pre_act, half):
    return half + pre_act * jnp.exp(-0.5 * pre_act * pre_act) * inv_root_tau


def slots_body(experts, cap, col_ref, row_ref, slot_col_ref, slot_row_ref):
    layers, tokens, _ = col_ref.shape
    down = lax.broadcasted_iota(I32, (tokens, tokens), 0)
    across = lax.broadcasted_iota(I32, (tokens, tokens), 1)
    before_col = jnp.where(across < down, 1.0, 0.0).astype(BF16)
    before_row = jnp.where(down < across, 1.0, 0.0).astype(BF16)
    lane = lax.broadcasted_iota(I32, (tokens, experts), 1)
    sub = lax.broadcasted_iota(I32, (experts, tokens), 0)
    for layer in range(layers):
        ids = col_ref[layer]
        one = [jnp.where(lane == ids[:, k : k + 1], 1.0, 0.0) for k in range(2)]
        earlier = dot(before_col, (one[0] + one[1]).astype(BF16))
        for k in range(2):
            at = jnp.sum(earlier * one[k], -1, keepdims=True).astype(I32)
            own = ids[:, k : k + 1]
            slot_col_ref[layer, :, k : k + 1] = jnp.where(own < 0, -1, own * cap + at)
        ids = row_ref[layer]
        one = [jnp.where(sub == ids[k : k + 1, :], 1.0, 0.0) for k in range(2)]
        earlier = dot((one[0] + one[1]).astype(BF16), before_row)
        for k in range(2):
            at = jnp.sum(earlier * one[k], 0, keepdims=True).astype(I32)
            own = ids[k : k + 1, :]
            slot_row_ref[layer, k : k + 1, :] = jnp.where(own < 0, -1, own * cap + at)


def attend(stream, heads, real, gain_row, shift_row, wqkv_ref, bqv_ref):
    normed, inv_std = norm_parts(stream)
    attn_input = (normed * gain_row + shift_row).astype(BF16)
    width = wqkv_ref.shape[0] // 3
    three = []
    for part in range(3):
        rows = dot_nt(attn_input, wqkv_ref[part * width : (part + 1) * width, :])
        if part != 1:
            rows = rows + bqv_ref[part // 2 : part // 2 + 1, :]
        three.append(rows.astype(BF16))
    query, key, value = three
    tokens = query.shape[0]
    keep = lax.broadcasted_iota(I32, (1, tokens), 1) < real
    mixed = jnp.zeros((tokens, width), F32)
    weights = []
    for head in range(heads):
        scores = dot_nt(only_head(query, head), key) * SCALE
        scores = jnp.where(keep, scores, -1e30)
        row_max = jnp.max(scores, -1, keepdims=True)
        raised = jnp.exp(scores - row_max)
        probs = raised / jnp.sum(raised, -1, keepdims=True)
        weights.append(probs)
        mixed = mixed + dot(probs.astype(BF16), only_head(value, head))
    return normed, attn_input, three, weights, mixed.astype(BF16)


def attn_fwd_body(n, heads, real, from_mix, me_ref, *refs):
    base_ref, *refs = refs
    if from_mix:
        mix_refs, refs = refs[:n], refs[n:]
    gain_ref, shift_ref, wqkv_ref, bqv_ref, wout_ref, *refs = refs
    piece_refs, refs = refs[:n], refs[n:]
    scratch = refs[-1]
    if from_mix:
        stream = take_pieces(me_ref, mix_refs, scratch) + base_ref[...]
        refs[0][...] = stream
    else:
        stream = load_rows(base_ref, scratch)
    mixed = attend(
        stream, heads, real, gain_ref[0:1, :], shift_ref[0:1, :], wqkv_ref, bqv_ref
    )[-1]
    put_pieces(me_ref, dot(mixed, wout_ref[...]), scratch, piece_refs)


def moe_pre_body(n, layer, with_grad, me_ref, base_ref, *refs):
    proj_refs, refs = refs[:n], refs[n:]
    outb_ref, gain_ref, shift_ref, router_ref, ids_ref, slot_row_ref, *refs = refs
    if with_grad:
        up_ref, *refs = refs
    resid_ref, a2_ref, gate_ref, sent_ref, scratch = refs
    residual = load_rows(base_ref, scratch)
    residual = residual + take_pieces(me_ref, proj_refs, scratch) + outb_ref[layer : layer + 1, :]
    resid_ref[...] = residual
    normed, _ = norm_parts(residual)
    moe_input = (normed * gain_ref[1:2, :] + shift_ref[1:2, :]).astype(BF16)
    a2_ref[...] = moe_input
    router = router_ref[...]
    high, rest = split_two(router)
    middle, low = split_two(router - high.astype(F32))
    logits = dot(moe_input, high) + (dot(moe_input, middle) + dot(moe_input, low))
    raised = jnp.exp(logits - jnp.max(logits, -1, keepdims=True))
    gate = raised / jnp.sum(raised, -1, keepdims=True)
    gate_ref[...] = gate
    slots = sent_ref.shape[0] * (sent_ref.shape[1] // 2 if with_grad else 1)
    picks = slot_pick_rows(slot_row_ref[...], slots)
    sent = dot(picks[0] + picks[1], moe_input).astype(BF16)
    if with_grad:
        upstream = load_rows(up_ref, scratch)
        chosen = picked_probs(gate, ids_ref[...])
        sent_grad = (
            dot(picks[0], (chosen[0] * upstream).astype(BF16))
            + dot(picks[1], (chosen[1] * upstream).astype(BF16))
        ).astype(BF16)
        experts, double, width = sent_ref.shape
        sent_ref[:, : double // 2] = sent.reshape(experts, double // 2, width)
        sent_ref[:, double // 2 :] = sent_grad.reshape(experts, double // 2, width)
    else:
        sent_ref[...] = sent


def ffn_fwd_body(share, x_ref, w1_ref, b1_ref, w2_ref, b2_ref, pre_ref, out_ref):
    pre_act = dot(x_ref[...], w1_ref[0, 0]) + b1_ref[0]
    pre_ref[...] = pre_act
    hidden, _ = gelu_parts(pre_act)
    out_ref[...] = (dot(hidden.astype(BF16), w2_ref[0, 0]) + b2_ref[0] * share).astype(BF16)


def ffn_back_body(pre_ref, dy_ref, w1_ref, w2_ref, dx_ref, hid_ref, dpre_ref):
    pre_act = pre_ref[...]
    hidden, half = gelu_parts(pre_act)
    hid_ref[...] = hidden.astype(BF16)
    dpre = (dot_nt(dy_ref[...], w2_ref[0, 0]) * gelu_slope(pre_act, half)).astype(BF16)
    dpre_ref[...] = dpre
    dx_ref[...] = dot_nt(dpre, w1_ref[0, 0]).astype(BF16)


def ffn_both_body(share, x_ref, w1_ref, b1_ref, w2_ref, b2_ref, out_ref, hid_ref, dpre_ref):
    cap = x_ref.shape[1] // 2
    groups = x_ref.shape[0]
    x = x_ref[:, :cap].reshape(groups * cap, x_ref.shape[2])
    dy = x_ref[:, cap:].reshape(groups * cap, x_ref.shape[2])
    pre_act = dot(x, w1_ref[0, 0]) + b1_ref[0]
    hidden, half = gelu_parts(pre_act)
    hidden = hidden.astype(BF16)
    hid_ref[...] = hidden
    result = (dot(hidden, w2_ref[0, 0]) + b2_ref[0] * share).astype(BF16)
    out_ref[:, :cap] = result.reshape(groups, cap, result.shape[1])
    dpre = (dot_nt(dy, w2_ref[0, 0]) * gelu_slope(pre_act, half)).astype(BF16)
    dpre_ref[...] = dpre
    dx = dot_nt(dpre, w1_ref[0, 0]).astype(BF16)
    out_ref[:, cap:] = dx.reshape(groups, cap, dx.shape[1])


def ffn_grads_body(paired, x_ref, dpre_ref, hid_ref, *refs):
    g1_ref, gb1_ref, g2_ref, gb2_ref = refs[-4:]
    if paired:
        groups, double, width = x_ref.shape
        x = x_ref[:, : double // 2].reshape(groups * double // 2, width)
        dy = x_ref[:, double // 2 :].reshape(groups * double // 2, width)
    else:
        x, dy = x_ref[...], refs[0][...]
    g1_ref[0] = dot_tn(x, dpre_ref[...])
    gb1_ref[0] = jnp.sum(dpre_ref[...].astype(F32), 0, keepdims=True)
    g2_ref[0] = dot_tn(hid_ref[...], dy)
    gb2_ref[0] = jnp.sum(dy.astype(F32), 0, keepdims=True)


def combine_body(n, me_ref, ret_ref, gate_ref, ids_ref, slot_col_ref, *refs):
    piece_refs, (y0_ref, y1_ref, scratch) = refs[:n], refs[n:]
    picks = slot_pick_cols(slot_col_ref[...], ret_ref.shape[0])
    chosen = picked_probs(gate_ref[...], ids_ref[...])
    y0 = dot(picks[0], ret_ref[...])
    y1 = dot(picks[1], ret_ref[...])
    y0_ref[...] = y0.astype(BF16)
    y1_ref[...] = y1.astype(BF16)
    put_pieces(me_ref, chosen[0] * y0 + chosen[1] * y1, scratch, piece_refs)


def router_back(upstream, rows, gate, ids, moe_input, router, grad_ref):
    lane = lax.broadcasted_iota(I32, gate.shape, 1)
    prob_grad = jnp.zeros_like(gate)
    for k in range(2):
        choice = jnp.sum(upstream * rows[k], -1, keepdims=True)
        prob_grad = prob_grad + jnp.where(lane == ids[:, k : k + 1], choice, 0.0)
    logit_grad = gate * (prob_grad - jnp.sum(prob_grad * gate, -1, keepdims=True))
    high, low = split_two(logit_grad)
    grad_ref[...] = dot_tn(high, moe_input) + dot_tn(low, moe_input)
    w_high, w_low = split_two(router)
    return dot_nt(high, w_high) + (dot_nt(high, w_low) + dot_nt(low, w_high))


def moe_back_body(
    n, fresh, me_ref, dx_ref, up_ref, gate_ref, ids_ref, slot_col_ref, a2_ref, router_ref, *refs
):
    scratch = refs[-1]
    if fresh:
        groups, double, width = dx_ref.shape
        returned = dx_ref[:, : double // 2].reshape(groups * double // 2, width)
        dx = dx_ref[:, double // 2 :].reshape(groups * double // 2, width)
    else:
        dx = dx_ref[...]
    picks = slot_pick_cols(slot_col_ref[...], dx.shape[0])
    grad = dot(picks[0] + picks[1], dx)
    if fresh:
        rows = [dot(picks[k], returned) for k in range(2)]
    else:
        y0_ref, y1_ref, *refs = refs
        rows = [y0_ref[...].astype(F32), y1_ref[...].astype(F32)]
    upstream = load_rows(up_ref, scratch)
    gate, ids = gate_ref[...], ids_ref[...]
    piece_refs, refs = refs[:n], refs[n:]
    if fresh:
        mix_refs, refs = refs[:n], refs[n:]
    grad_ref, scratch = refs
    grad = grad + router_back(upstream, rows, gate, ids, a2_ref[...], router_ref[...], grad_ref)
    put_pieces(me_ref, grad, scratch, piece_refs)
    if fresh:
        chosen = picked_probs(gate, ids)
        put_pieces(me_ref, chosen[0] * rows[0] + chosen[1] * rows[1], scratch, mix_refs)


def attn_back_body(n, heads, real, place_ref, resid_ref, *refs):
    da2_refs, refs = refs[:n], refs[n:]
    up_ref, gain_ref, shift_ref, wqkv_ref, bqv_ref, wout_ref, stream_ref, router_ref, *refs = refs
    piece_refs, refs = refs[:n], refs[n:]
    dr_ref, keep_ref, send_ref, all_ref, scratch, grad_scratch = refs
    me_ref = place_ref.at[pl.ds(2, 1)]
    normed, attn_input, (query, key, value), weights, mixed = attend(
        load_rows(stream_ref, scratch), heads, real, gain_ref[0:1, :], shift_ref[0:1, :],
        wqkv_ref, bqv_ref,
    )
    upstream = load_rows(up_ref, scratch)
    moe_grad = take_pieces(me_ref, da2_refs, scratch)
    normed_two, inv_std = norm_parts(resid_ref[...])
    share = 1.0 / n
    all_ref[2:3, :] = jnp.sum(moe_grad * normed_two, 0, keepdims=True) * share
    all_ref[3:4, :] = jnp.sum(moe_grad, 0, keepdims=True) * share
    resid_grad = upstream + norm_back(moe_grad, normed_two, inv_std, gain_ref[1:2, :])
    dr_ref[...] = resid_grad
    all_ref[4:5, :] = jnp.sum(resid_grad, 0, keepdims=True) * share
    proj_grad = resid_grad.astype(BF16)
    mixed_grad = dot_nt(proj_grad, wout_ref[...]).astype(BF16)
    width = wout_ref.shape[0]
    dquery = jnp.zeros(query.shape, F32)
    dkey = jnp.zeros(query.shape, F32)
    dvalue = jnp.zeros(query.shape, F32)
    for head in range(heads):
        probs = weights[head]
        own = only_head(mixed_grad, head)
        dvalue = dvalue + dot_tn(probs.astype(BF16), own)
        dot_grad = dot_nt(own, value)
        score_grad = (
            probs * (dot_grad - jnp.sum(dot_grad * probs, -1, keepdims=True))
        ).astype(BF16)
        dquery = dquery + dot(score_grad, only_head(key, head))
        dkey = dkey + dot_tn(score_grad, only_head(query, head))
    attn_grad = None
    three = []
    for part, rows in enumerate((dquery * SCALE, dkey * SCALE, dvalue)):
        three.append(rows.astype(BF16))
        term = dot(three[part], wqkv_ref[part * width : (part + 1) * width, :])
        attn_grad = term if attn_grad is None else attn_grad + term
    put_pieces(me_ref, attn_grad, scratch, piece_refs)
    all_ref[0:1, :] = jnp.sum(attn_grad * normed, 0, keepdims=True)
    all_ref[1:2, :] = jnp.sum(attn_grad, 0, keepdims=True)
    all_ref[5:8, :] = jnp.zeros((3, all_ref.shape[1]), F32)
    for row, part in enumerate((0, 2)):
        sums = jnp.sum(three[part].astype(F32), 0, keepdims=True)
        for block in range(n):
            own = jnp.where(place_ref[2] == block, sums, 0.0)
            all_ref[5 + row : 6 + row, block * width : (block + 1) * width] = own
    all_ref[8:, :] = router_ref[...]
    for part in range(3):
        grad_scratch[part * width : (part + 1) * width, :] = dot_tn(three[part], attn_input)
    grad_scratch[3 * width :, :] = dot_tn(mixed, proj_grad)
    core, half = place_ref[0], keep_ref.shape[0]
    keep_ref[...] = grad_scratch[pl.ds(pl.multiple_of(core * half, 8), half), :].astype(BF16)
    send_ref[...] = grad_scratch[pl.ds(pl.multiple_of((1 - core) * half, 8), half), :].astype(BF16)


def grad_cut_body(count, place_ref, keep_ref, got_ref, *refs):
    piece_refs, scratch = refs[:count], refs[count]
    rows = piece_refs[0].shape[0]
    scratch[...] = keep_ref[...].astype(F32) + got_ref[...].astype(F32)
    for step, ref in enumerate(piece_refs):
        owner = lax.bitwise_xor(place_ref[1], step)
        ref[...] = scratch[pl.ds(pl.multiple_of(owner * rows, 8), rows), :].astype(BF16)


def grad_join_body(layers, count, place_ref, *refs):
    qkv_ref, out_ref, scratch = refs[-3:]
    refs = refs[:-3]
    rows = refs[0].shape[0]
    split = qkv_ref.shape[1]
    for layer in range(layers):
        for side in range(2):
            core = lax.bitwise_xor(place_ref[0], side)
            for step in range(count):
                owner = core * count + lax.bitwise_xor(place_ref[1], step)
                ref = refs[(layer * 2 + side) * count + step]
                scratch[pl.ds(pl.multiple_of(owner * rows, 8), rows), :] = ref[...].astype(F32)
        qkv_ref[layer] = scratch[:split, :]
        out_ref[layer] = scratch[split:, :]


def norm_one_back_body(n, dispatch, me_ref, stream_ref, *refs):
    da1_refs, refs = refs[:n], refs[n:]
    dr_ref, gain_ref, *refs = refs
    if dispatch:
        gate_ref, ids_ref, slot_row_ref, *refs = refs
    gx_ref, *refs = refs
    if dispatch:
        sent_grad_ref, *refs = refs
    (scratch,) = refs
    attn_grad = take_pieces(me_ref, da1_refs, scratch)
    normed, inv_std = norm_parts(load_rows(stream_ref, scratch))
    upstream = dr_ref[...] + norm_back(attn_grad, normed, inv_std, gain_ref[0:1, :])
    gx_ref[...] = upstream[: gx_ref.shape[0]]
    if dispatch:
        picks = slot_pick_rows(slot_row_ref[...], sent_grad_ref.shape[0])
        chosen = picked_probs(gate_ref[...], ids_ref[...])
        sent_grad_ref[...] = (
            dot(picks[0], (chosen[0] * upstream).astype(BF16))
            + dot(picks[1], (chosen[1] * upstream).astype(BF16))
        ).astype(BF16)


def add_out_body(n, me_ref, base_ref, *refs):
    mix_refs, (out_ref, scratch) = refs[:n], refs[n:]
    total = base_ref[...] + take_pieces(me_ref, mix_refs, scratch)
    out_ref[...] = total[: out_ref.shape[0]]


def step_on(rows, step, n):
    return lax.ppermute(rows, "tensor", [(i, (i + step) % n) for i in range(n)])


def add_up(own, arrived):
    total = own.astype(F32)
    for rows in arrived:
        total = total + rows.astype(F32)
    return total.astype(BF16)


def tensor_scatter(pieces):
    return [step_on(pieces[step], step, len(pieces)) for step in range(1, len(pieces))]


def tensor_gather(own, n):
    return [own] + [step_on(own, step, n) for step in range(1, n)]


def tie(first, other):
    flat, tree = jax.tree.flatten((first, other))
    return jax.tree.unflatten(tree, lax.optimization_barrier(tuple(flat)))


def tensor_total(pieces):
    return tensor_gather(add_up(pieces[0], tensor_scatter(pieces)), len(pieces))


def swap(rows, axis, step, size):
    return lax.ppermute(rows, axis, [(i, i ^ step) for i in range(size)])


def group_exchange(rows, groups):
    blocks = rows.reshape(groups, -1, rows.shape[-1])
    moved = lax.all_to_all(blocks, GROUP_AXES, split_axis=0, concat_axis=0, tiled=True)
    return moved.reshape(rows.shape)


def on_device(
    n,
    groups,
    tokens,
    cotangent,
    routes,
    norm_gain,
    norm_bias,
    w_qkv,
    b_qv,
    w_out,
    b_out,
    w_router,
    w_in,
    b_in,
    w_exp_out,
    b_exp_out,
):
    layers = w_qkv.shape[0]
    images, seq_len, model_width = tokens.shape
    real = images * seq_len
    experts = w_router.shape[2]
    capacity = 3 * real // experts
    cap = ceil_to(capacity, 16)
    slots = experts * cap
    local_cols = w_qkv.shape[3]
    heads = local_cols // HEAD_DIM
    hidden = w_in.shape[3]
    chunk = ceil_to(-(-real // n), 8)
    rows = n * chunk
    me = lax.axis_index("tensor").astype(I32).reshape(1)
    place = jnp.stack([lax.axis_index(name) for name in ALL_AXES]).astype(I32)

    tokens_in = tokens.reshape(real, model_width)
    cot = cotangent.reshape(real, model_width)
    ids_col = jnp.pad(
        routes.reshape(layers, real, 2), ((0, 0), (0, rows - real), (0, 0)), constant_values=-1
    )
    ids_row = ids_col.transpose(0, 2, 1)
    qkv_weights = w_qkv.transpose(0, 2, 3, 1).reshape(layers, 3 * local_cols, model_width)

    stage = pltpu.VMEM((rows, model_width), F32)
    piece = ((chunk, model_width), BF16)
    slot_col, slot_row = kernel_call(
        functools.partial(slots_body, experts, cap),
        [ids_col, ids_row],
        [((layers, rows, 2), I32), ((layers, 2, rows), I32)],
        name="slots",
    )

    def norms(layer, near=True):
        wrap = Near if near else Far
        return [wrap(norm_gain, layer), wrap(norm_bias, layer)]

    def attn_weights(layer, near=True):
        wrap = Near if near else Far
        return [wrap(qkv_weights, layer), wrap(b_qv, layer), wrap(w_out, layer)]

    def attn_fwd(layer, base, mix):
        got = kernel_call(
            functools.partial(attn_fwd_body, n, heads, real, bool(mix)),
            [me, Far(base), *mix, *norms(layer, mix), *attn_weights(layer, mix)],
            [piece] * n + ([((rows, model_width), F32, 1)] if mix else []),
            [stage], scalars=1, name="attn_fwd",
        )
        return got[:n], got[n] if mix else base

    def moe_pre(layer, base, proj, upstream):
        ins = [me, Far(base), *proj, b_out, *norms(layer), Near(w_router, layer),
               Near(ids_col, layer), Near(slot_row, layer)]
        outs = [
            ((rows, model_width), F32, 1),
            ((rows, model_width), BF16, 1),
            ((rows, experts), F32, 1),
            ((slots, model_width), BF16),
        ]
        if upstream is not None:
            ins.append(Far(upstream))
            outs[-1] = ((experts, 2 * cap, model_width), BF16)
        return kernel_call(
            functools.partial(moe_pre_body, n, layer, upstream is not None),
            ins, outs, [stage], scalars=1, name="moe_pre",
        )

    parts = 4
    part_rows = slots // parts
    pair_block = (groups // parts, 2 * cap, model_width)

    def row_spec(cols):
        return pl.BlockSpec((part_rows, cols), lambda i: (i, 0))

    def pair_spec():
        return pl.BlockSpec(pair_block, lambda i: (i, 0, 0))

    def entry_spec(array, layer):
        shape = (1,) + array.shape[1:]
        return pl.BlockSpec(shape, lambda i: (layer,) + (0,) * (len(shape) - 1))

    def whole_spec(array):
        return pl.BlockSpec(array.shape, lambda i: (0,) * array.ndim)

    b_first = b_in.reshape(layers, 1, hidden)
    b_second = b_exp_out.reshape(layers, 1, model_width)

    last = layers - 1
    saved = []
    stream, mix = tokens_in, ()
    for layer in range(layers):
        pieces, stream = attn_fwd(layer, stream, mix)
        proj = tensor_total(pieces)
        got = moe_pre(layer, stream, proj, cot if layer == last else None)
        residual, a2, gate, sent = got[:4]
        if layer < last:
            arrived = group_exchange(sent, groups)
            weights = (pinned(w_in), b_first, pinned(w_exp_out), b_second)
            pre_act, result = block_call(
                functools.partial(ffn_fwd_body, 1.0 / n),
                [arrived, *weights],
                [((slots, hidden), F32), ((slots, model_width), BF16)],
                grid=(parts,),
                in_specs=[row_spec(model_width)] + [entry_spec(v, layer) for v in weights],
                out_specs=[row_spec(hidden), row_spec(model_width)],
                name="ffn_fwd",
            )
            returned = group_exchange(result, groups)
            got = kernel_call(
                functools.partial(combine_body, n),
                [me, returned, Far(gate), Near(ids_col, layer), Near(slot_col, layer)],
                [piece] * n + [((rows, model_width), BF16, 1)] * 2,
                [stage], scalars=1, name="combine",
            )
            mix = tensor_total(got[:n])
            saved.append((stream, residual, a2, gate, arrived, pre_act, got[n:]))
            stream = residual
        else:
            saved.append((stream, residual, a2, gate))

    half = (4 * local_cols) // 2
    chips = groups // 2
    joined, cuts = {}, {}

    def group_scatter(layer):
        cut, small = cuts[layer]
        return (
            [swap(cut[step], "expert", step, chips) for step in range(1, chips)],
            [swap(small, "expert", step, chips) for step in range(1, chips)],
        )

    def group_gather(layer, moved):
        cut, small = cuts[layer]
        own = add_up(cut[0], moved[0])
        small = sum(moved[1], small)
        return (
            [own] + [swap(own, "expert", step, chips) for step in range(1, chips)],
            sum([step_on(small, step, n) for step in range(1, n)], small),
        )

    def add_out():
        (total,) = kernel_call(
            functools.partial(add_out_body, n),
            [me, Far(saved[last][1]), *out_chunks],
            [((real, model_width), F32)], [stage], scalars=1, name="add_out",
        )
        return total

    ffn_outs = [
        ((layers, model_width, hidden), F32),
        ((layers, 1, hidden), F32),
        ((layers, hidden, model_width), F32),
        ((layers, 1, model_width), F32),
    ]
    ffn_grads = None
    upstream = cot
    for layer in reversed(range(layers)):
        stream, residual, a2, gate = saved[layer][:4]
        back_ins = [Far(upstream), Far(gate), Near(ids_col, layer), Near(slot_col, layer), Far(a2),
                    Near(w_router, layer)]
        if layer == last:
            arrived = group_exchange(sent, groups)
            weights = (pinned(w_in), b_first, pinned(w_exp_out), b_second)
            result, hid, dpre = block_call(
                functools.partial(ffn_both_body, 1.0 / n),
                [arrived, *weights],
                [((groups, 2 * cap, model_width), BF16)] + [((slots, hidden), BF16)] * 2,
                grid=(parts,),
                in_specs=[pair_spec()] + [entry_spec(v, layer) for v in weights],
                out_specs=[pair_spec()] + [row_spec(hidden)] * 2,
                name="ffn_both",
            )
            returned = group_exchange(result, groups)
            got = kernel_call(
                functools.partial(moe_back_body, n, True),
                [me, returned, *back_ins],
                [piece] * n + [piece + (1,)] * n + [((experts, model_width), F32)],
                [stage], scalars=1, name="moe_back",
            )
            out_mix = got[n : 2 * n]
            router_grad = got[2 * n]
            ffn_ins = [arrived, dpre, hid]
        else:
            arrived, pre_act, (y0, y1) = saved[layer][4:]
            grad_arrived = group_exchange(sent_grad, groups)
            if layer == last - 1:
                grad_arrived, out_arrived = tie(grad_arrived, tensor_scatter(out_mix))
                out_own = add_up(out_mix[0], out_arrived)
            dx, hid, dpre = block_call(
                ffn_back_body,
                [pinned(pre_act), grad_arrived, pinned(w_in), pinned(w_exp_out)],
                [((slots, model_width), BF16)] + [((slots, hidden), BF16)] * 2,
                grid=(parts,),
                in_specs=[row_spec(hidden), row_spec(model_width), entry_spec(w_in, layer),
                          entry_spec(w_exp_out, layer)],
                out_specs=[row_spec(model_width)] + [row_spec(hidden)] * 2,
                name="ffn_back",
            )
            dx = group_exchange(dx, groups)
            if layer == last - 1:
                dx, out_chunks = tie(dx, tensor_gather(out_own, n))
            got = kernel_call(
                functools.partial(moe_back_body, n, False),
                [me, dx, *back_ins, Far(y0), Far(y1)],
                [piece] * n + [((experts, model_width), F32)],
                [stage], scalars=1, name="moe_back",
            )
            router_grad = got[n]
            ffn_ins = [arrived, dpre, hid, grad_arrived]
        ffn_grads = block_call(
            functools.partial(ffn_grads_body, layer == last),
            [pinned(v) for v in ffn_ins] + list(ffn_grads or ()),
            ffn_outs,
            grid=(1,),
            in_specs=[whole_spec(v) for v in ffn_ins]
            + [pl.BlockSpec(memory_space=pl.ANY)] * (4 if ffn_grads else 0),
            out_specs=[
                pl.BlockSpec((1,) + shape[1:], lambda i, layer=layer: (layer, 0, 0))
                for shape, _ in ffn_outs
            ],
            vmem=28,
            aliases={len(ffn_ins) + i: i for i in range(4)} if ffn_grads else None,
            name="ffn_grads",
        )
        if layer == last:
            da2 = tensor_total(got[:n])
        else:
            arrived = tensor_scatter(got[:n])
            ffn_grads, arrived = tie(ffn_grads, arrived)
            arrived, moved = tie(arrived, group_scatter(layer + 1))
            own = add_up(got[0], arrived)
            da2, moved = tie(tensor_gather(own, n), group_gather(layer + 1, moved))
            joined[layer + 1] = moved
            if layer == last - 1:
                da2, output = tie(da2, add_out())
        got = kernel_call(
            functools.partial(attn_back_body, n, heads, real),
            [place, Far(residual), *da2, Far(upstream), *norms(layer), *attn_weights(layer),
             Far(stream), router_grad],
            [piece] * n + [
                ((rows, model_width), F32, 1),
                ((half, model_width), BF16, 1),
                ((half, model_width), BF16),
                ((8 + experts, model_width), F32),
            ],
            [stage, pltpu.VMEM((2 * half, model_width), F32)], scalars=1, name="attn_back",
        )
        dr, keep, send, small = got[n:]
        arrived = tensor_scatter(got[:n])
        if layer == last:
            ffn_grads, arrived = tie(ffn_grads, arrived)
        arrived, swapped = tie(arrived, (swap(send, "dp", 1, 2), swap(small, "dp", 1, 2)))
        cut = kernel_call(
            functools.partial(grad_cut_body, chips),
            [place, Far(keep), swapped[0]],
            [((half // chips, model_width), BF16)] * chips,
            [pltpu.VMEM((half, model_width), F32)], scalars=1, name="grad_cut",
        )
        cuts[layer] = cut, small + swapped[1]
        if layer > 0:
            da1 = tensor_gather(add_up(got[0], arrived), n)
        else:
            moved = group_scatter(0)
            da1, moved = tie(tensor_gather(add_up(got[0], arrived), n), moved)
            joined[0] = group_gather(0, moved)
        ins = [me, Far(stream), *da1, Far(dr), Near(norm_gain, layer)]
        if layer > 0:
            below = layer - 1
            upstream, sent_grad = kernel_call(
                functools.partial(norm_one_back_body, n, True),
                ins + [Far(saved[below][3]), Near(ids_col, below), Near(slot_row, below)],
                [((rows, model_width), F32, 1), ((slots, model_width), BF16)],
                [stage], scalars=1, name="norm_back_send",
            )
        else:
            (grad_tokens,) = kernel_call(
                functools.partial(norm_one_back_body, n, False),
                ins, [((real, model_width), F32)], [stage], scalars=1, name="norm_back",
            )
    g1, gb1, g2, gb2 = ffn_grads

    pieces = []
    for layer in range(layers):
        own_half = joined[layer][0]
        pieces += own_half + [swap(rows_of, "dp", 1, 2) for rows_of in own_half]
    qkv_grad, out_grad = kernel_call(
        functools.partial(grad_join_body, layers, chips),
        [place, *pieces],
        [((layers, 3 * local_cols, model_width), F32), ((layers, local_cols, model_width), F32)],
        [pltpu.VMEM((2 * half, model_width), F32)], scalars=1, name="grad_join",
    )
    qkv_grad = qkv_grad.reshape(layers, 3, local_cols, model_width).transpose(0, 3, 1, 2)
    small = jnp.stack([joined[layer][1] for layer in range(layers)])
    gain_grad = jnp.stack([small[:, 0], small[:, 2]], 1)
    shift_grad = jnp.stack([small[:, 1], small[:, 3]], 1)
    qv_grad = lax.dynamic_slice_in_dim(small[:, 5:7], place[2] * local_cols, local_cols, 2)
    return (
        output.reshape(images, seq_len, model_width),
        grad_tokens.reshape(images, seq_len, model_width),
        gain_grad,
        shift_grad,
        qkv_grad,
        qv_grad,
        out_grad,
        small[:, 4],
        small[:, 8 : 8 + experts].transpose(0, 2, 1),
        g1[:, None],
        gb1,
        g2[:, None],
        gb2,
    )


def solution(mesh):
    n = mesh.shape["tensor"]
    groups = mesh.shape["dp"] * mesh.shape["expert"]
    return jax.shard_map(
        functools.partial(on_device, n, groups),
        mesh=mesh,
        in_specs=(
            P(("dp", "expert"), None, None),
            P(("dp", "expert"), None, None),
            P(None, ("dp", "expert"), None, None),
            P(),
            P(),
            P(None, None, None, "tensor"),
            P(None, None, "tensor"),
            P(None, "tensor", None),
            P(),
            P(),
            P(None, ("dp", "expert"), None, "tensor"),
            P(None, ("dp", "expert"), "tensor"),
            P(None, ("dp", "expert"), "tensor", None),
            P(None, ("dp", "expert"), None),
        ),
        out_specs=(
            P(("dp", "expert"), None, None),
            P(("dp", "expert"), None, None),
            P(),
            P(),
            P(None, None, None, "tensor"),
            P(None, None, "tensor"),
            P(None, "tensor", None),
            P(),
            P(),
            P(None, ("dp", "expert"), None, "tensor"),
            P(None, ("dp", "expert"), "tensor"),
            P(None, ("dp", "expert"), "tensor", None),
            P(None, ("dp", "expert"), None),
        ),
        check_vma=False,
    )
```

```python
import functools

import jax
import jax.numpy as jnp
from jax import lax
from jax.experimental import pallas as pl
from jax.experimental.pallas import tpu as pltpu
from jax.sharding import PartitionSpec as P

HEAD_DIM = 64
SCALE = HEAD_DIM ** (-0.5)
LANES = 128
GROUP_AXES = ("dp", "expert")
ALL_AXES = ("dp", "expert", "tensor")

epsilon = 1e-06
root_half = 0.7071067811865476
inv_root_tau = 0.3989422804014327

F32 = jnp.float32
BF16 = jnp.bfloat16
I32 = jnp.int32


def ceil_to(value, step):
    return -(-value // step) * step


def dot(a, b):
    return lax.dot_general(a, b, (((1,), (0,)), ((), ())), preferred_element_type=F32)


def dot_nt(a, b):
    return lax.dot_general(a, b, (((1,), (1,)), ((), ())), preferred_element_type=F32)


def dot_tn(a, b):
    return lax.dot_general(a, b, (((0,), (0,)), ((), ())), preferred_element_type=F32)


def split_two(v):
    high = v.astype(BF16)
    return high, (v - high.astype(F32)).astype(BF16)


class Far:
    def __init__(self, array, index=None):
        self.array, self.index = array, index
        self.shape = array.shape if index is None else array.shape[1:]


class Near:
    def __init__(self, array, index):
        self.array, self.index = array, index


class Fetched:
    def __init__(self, copy, ref):
        self.copy, self.ref, self.shape = copy, ref, ref.shape

    def __getitem__(self, at):
        if self.copy is not None:
            self.copy.wait()
            self.copy = None
        return self.ref[at]


class Kept:
    def __init__(self, ref, far_ref, sems):
        self.ref, self.far_ref, self.sems, self.shape = ref, far_ref, sems, ref.shape
        self.copies = []

    def __setitem__(self, at, value):
        self.ref[at] = value
        pair = self.ref, self.far_ref
        if at is not Ellipsis:
            rows = pl.ds(at[0].start, at[0].stop - at[0].start)
            pair = self.ref.at[rows], self.far_ref.at[rows]
        copy = pltpu.make_async_copy(*pair, self.sems.at[len(self.copies)])
        copy.start()
        self.copies.append(copy)


def kernel_call(body, ins, outs, scratch=(), scalars=0, vmem=16, name=None):
    fars = [i for i, v in enumerate(ins) if isinstance(v, Far)]
    keeps = [i for i, v in enumerate(outs) if len(v) > 2]
    arrays = [
        pltpu.with_memory_space_constraint(v.array, pltpu.HBM)
        if isinstance(v, Far)
        else v.array
        if isinstance(v, Near)
        else v
        for v in ins
    ]
    extra = [pltpu.VMEM(ins[i].shape, ins[i].array.dtype) for i in fars]
    extra += [pltpu.VMEM(outs[i][0], outs[i][1]) for i in keeps]
    extra += [pltpu.SemaphoreType.DMA((1,)) for _ in fars]
    extra += [pltpu.SemaphoreType.DMA((outs[i][2],)) for i in keeps]

    def whole(*refs):
        refs = list(refs)
        own = refs[len(ins) + len(outs) :]
        buffers, sems = own[: len(fars) + len(keeps)], own[len(fars) + len(keeps) :]
        sems, rest = sems[: len(buffers)], sems[len(buffers) :]
        for i, v in enumerate(ins):
            if isinstance(v, Near):
                refs[i] = refs[i].at[v.index]
        for at, i in enumerate(fars):
            source = refs[i] if ins[i].index is None else refs[i].at[ins[i].index]
            copy = pltpu.make_async_copy(source, buffers[at], sems[at].at[0])
            copy.start()
            refs[i] = Fetched(copy, buffers[at])
        for at, i in enumerate(keeps, len(fars)):
            refs[len(ins) + i] = Kept(buffers[at], refs[len(ins) + i], sems[at])
        body(*refs[: len(ins) + len(outs)], *rest)
        for i in fars:
            refs[i][...]
        for i in keeps:
            for copy in refs[len(ins) + i].copies:
                copy.wait()

    def space(i):
        if i < scalars:
            return pltpu.SMEM
        return pltpu.HBM if i in fars else pltpu.VMEM

    return pl.pallas_call(
        whole,
        out_shape=[
            pltpu.HBM(*v[:2]) if len(v) > 2 else jax.ShapeDtypeStruct(*v) for v in outs
        ],
        in_specs=[pl.BlockSpec(memory_space=space(i)) for i in range(len(ins))],
        out_specs=[
            pl.BlockSpec(memory_space=pltpu.HBM if i in keeps else pltpu.VMEM)
            for i in range(len(outs))
        ],
        scratch_shapes=extra + list(scratch),
        compiler_params=pltpu.CompilerParams(vmem_limit_bytes=vmem * 1024 * 1024),
        name=name,
    )(*arrays)


def pinned(array):
    return pltpu.with_memory_space_constraint(array, pltpu.HBM)


def block_call(body, ins, outs, grid, in_specs, out_specs, scratch=(), vmem=16, aliases=None,
               name=None):
    return pl.pallas_call(
        body,
        out_shape=[pltpu.HBM(shape, dtype) for shape, dtype in outs],
        grid=grid,
        in_specs=in_specs,
        out_specs=out_specs,
        scratch_shapes=list(scratch),
        input_output_aliases=aliases or {},
        compiler_params=pltpu.CompilerParams(vmem_limit_bytes=vmem * 1024 * 1024),
        name=name,
    )(*ins)


def load_rows(ref, scratch):
    if ref.shape[0] == scratch.shape[0]:
        return ref[...].astype(F32)
    scratch[...] = jnp.zeros_like(scratch)
    scratch[: ref.shape[0], :] = ref[...].astype(F32)
    return scratch[...]


def norm_parts(stream):
    row_mean = jnp.mean(stream, -1, keepdims=True)
    centered = stream - row_mean
    inv_std = lax.rsqrt(jnp.mean(centered * centered, -1, keepdims=True) + epsilon)
    return centered * inv_std, inv_std


def norm_back(upstream, normed, inv_std, gain_row):
    scaled = upstream * gain_row
    return inv_std * (
        scaled
        - jnp.mean(scaled, -1, keepdims=True)
        - normed * jnp.mean(scaled * normed, -1, keepdims=True)
    )


def head_mask(head, width):
    lane = lax.broadcasted_iota(I32, (1, width), 1)
    return (lane >= head * HEAD_DIM) & (lane < (head + 1) * HEAD_DIM)


def only_head(rows, head):
    return jnp.where(head_mask(head, rows.shape[1]), rows, jnp.zeros_like(rows))


def put_pieces(me_ref, value, scratch, out_refs):
    count = len(out_refs)
    chunk = out_refs[0].shape[0]
    scratch[...] = value
    for step, ref in enumerate(out_refs):
        owner = lax.rem(me_ref[0] + step, count)
        ref[...] = scratch[pl.ds(pl.multiple_of(owner * chunk, 8), chunk), :].astype(BF16)


def take_pieces(me_ref, in_refs, scratch):
    count = len(in_refs)
    chunk = in_refs[0].shape[0]
    for step, ref in enumerate(in_refs):
        owner = lax.rem(me_ref[0] + count - step, count)
        scratch[pl.ds(pl.multiple_of(owner * chunk, 8), chunk), :] = ref[...].astype(F32)
    return scratch[...]


def picked_probs(gate, ids):
    lane = lax.broadcasted_iota(I32, gate.shape, 1)
    return [
        jnp.sum(jnp.where(lane == ids[:, k : k + 1], gate, 0.0), -1, keepdims=True) for k in range(2)
    ]


def slot_pick_rows(slot_row, slots):
    tokens = slot_row.shape[1]
    at = lax.broadcasted_iota(I32, (slots, tokens), 0)
    return [jnp.where(at == slot_row[k : k + 1, :], 1.0, 0.0).astype(BF16) for k in range(2)]


def slot_pick_cols(slot_col, slots):
    tokens = slot_col.shape[0]
    at = lax.broadcasted_iota(I32, (tokens, slots), 1)
    return [jnp.where(at == slot_col[:, k : k + 1], 1.0, 0.0).astype(BF16) for k in range(2)]


def gelu_parts(pre_act):
    half = 0.5 * (1.0 + lax.erf(pre_act * root_half))
    return pre_act * half, half


def gelu_slope(pre_act, half):
    return half + pre_act * jnp.exp(-0.5 * pre_act * pre_act) * inv_root_tau


def slots_body(experts, cap, col_ref, row_ref, cot_ref, slot_col_ref, slot_row_ref, gx_ref, scratch):
    layers, tokens, _ = col_ref.shape
    down = lax.broadcasted_iota(I32, (tokens, tokens), 0)
    across = lax.broadcasted_iota(I32, (tokens, tokens), 1)
    before_col = jnp.where(across < down, 1.0, 0.0).astype(BF16)
    before_row = jnp.where(down < across, 1.0, 0.0).astype(BF16)
    lane = lax.broadcasted_iota(I32, (tokens, experts), 1)
    sub = lax.broadcasted_iota(I32, (experts, tokens), 0)
    for layer in range(layers):
        ids = col_ref[layer]
        one = [jnp.where(lane == ids[:, k : k + 1], 1.0, 0.0) for k in range(2)]
        earlier = dot(before_col, (one[0] + one[1]).astype(BF16))
        for k in range(2):
            at = jnp.sum(earlier * one[k], -1, keepdims=True).astype(I32)
            own = ids[:, k : k + 1]
            slot_col_ref[layer, :, k : k + 1] = jnp.where(own < 0, -1, own * cap + at)
        ids = row_ref[layer]
        one = [jnp.where(sub == ids[k : k + 1, :], 1.0, 0.0) for k in range(2)]
        earlier = dot((one[0] + one[1]).astype(BF16), before_row)
        for k in range(2):
            at = jnp.sum(earlier * one[k], 0, keepdims=True).astype(I32)
            own = ids[k : k + 1, :]
            slot_row_ref[layer, k : k + 1, :] = jnp.where(own < 0, -1, own * cap + at)
    picks = slot_pick_rows(slot_row_ref[layers - 1], gx_ref.shape[0])
    gx_ref[...] = dot(picks[0] + picks[1], load_rows(cot_ref, scratch).astype(BF16)).astype(BF16)


def attend(stream, heads, real, gain_row, shift_row, wqkv_ref, bqv_ref):
    normed, inv_std = norm_parts(stream)
    attn_input = (normed * gain_row + shift_row).astype(BF16)
    width = wqkv_ref.shape[0] // 3
    three = []
    for part in range(3):
        rows = dot_nt(attn_input, wqkv_ref[part * width : (part + 1) * width, :])
        if part != 1:
            rows = rows + bqv_ref[part // 2 : part // 2 + 1, :]
        three.append(rows.astype(BF16))
    query, key, value = three
    tokens = query.shape[0]
    keep = lax.broadcasted_iota(I32, (1, tokens), 1) < real
    mixed = jnp.zeros((tokens, width), F32)
    weights = []
    for head in range(heads):
        scores = dot_nt(only_head(query, head), key) * SCALE
        scores = jnp.where(keep, scores, -1e30)
        row_max = jnp.max(scores, -1, keepdims=True)
        raised = jnp.exp(scores - row_max)
        probs = raised / jnp.sum(raised, -1, keepdims=True)
        weights.append(probs)
        mixed = mixed + dot(probs.astype(BF16), only_head(value, head))
    return normed, attn_input, three, weights, mixed.astype(BF16)


def pack_heads(mixed):
    rows, width = mixed.shape
    full = width - width % LANES
    if full == width:
        return mixed
    left, half = mixed[:, full:].astype(F32), rows // 2
    beside = jnp.concatenate([left[:half], left[half:]], 1).astype(BF16)
    parts = [mixed[:, at : at + LANES] for at in range(0, full, LANES)]
    return jnp.concatenate(parts + [beside], 0)


def unpack_heads(packed, rows, width):
    full = width - width % LANES
    if full == width:
        return packed
    parts = [packed[at * rows : (at + 1) * rows] for at in range(full // LANES)]
    beside = packed[full // LANES * rows :].astype(F32)
    left = jnp.concatenate([beside[:, : LANES // 2], beside[:, LANES // 2 :]], 0)
    return jnp.concatenate(parts + [left.astype(BF16)], 1)


def attn_fwd_body(n, heads, real, from_mix, packed, me_ref, *refs):
    base_ref, *refs = refs
    if from_mix:
        mix_refs, refs = refs[:n], refs[n:]
    gain_ref, shift_ref, wqkv_ref, bqv_ref, *refs = refs
    piece_refs = ()
    if not packed:
        wout_ref, *refs = refs
        piece_refs, refs = refs[:n], refs[n:]
    scratch = refs[-1]
    if from_mix:
        stream = take_pieces(me_ref, mix_refs, scratch) + base_ref[...]
        refs[0][...] = stream
    else:
        stream = load_rows(base_ref, scratch)
    mixed = attend(
        stream, heads, real, gain_ref[0:1, :], shift_ref[0:1, :], wqkv_ref, bqv_ref
    )[-1]
    if not piece_refs:
        packed_ref, scratch = refs[-2:]
        packed_ref[...] = pack_heads(mixed)
    else:
        put_pieces(me_ref, dot(mixed, wout_ref[...]), scratch, piece_refs)


def moe_pre_body(n, layer, packed, place_ref, base_ref, *refs):
    me_ref = place_ref.at[pl.ds(2, 1)]
    proj_refs, refs = refs[:n], refs[n:]
    if packed:
        wout_ref, *side_refs = refs[: 2 * n - 1]
        refs = refs[2 * n - 1 :]
    outb_ref, gain_ref, shift_ref, router_ref, ids_ref, slot_row_ref, *refs = refs
    resid_ref, a2_ref, gate_ref, sent_ref, scratch, *refs = refs
    if packed:
        (sides,) = refs
    residual = load_rows(base_ref, scratch)
    if packed:
        width = wout_ref.shape[0]
        for step, mixed_ref in enumerate(proj_refs):
            mixed = unpack_heads(mixed_ref[...], residual.shape[0], width)
            if step > 0:
                wout_ref = sides.at[step - 1]
                for side in range(2):
                    low = lax.bitwise_xor(place_ref[0], side) * (width // 2)
                    at = pl.ds(pl.multiple_of(low, 16), width // 2)
                    wout_ref[at, :] = side_refs[2 * step - 2 + side][...]
            residual = residual + dot(mixed, wout_ref[...])
    else:
        residual = residual + take_pieces(me_ref, proj_refs, scratch)
    residual = residual + outb_ref[layer : layer + 1, :]
    resid_ref[...] = residual
    normed, _ = norm_parts(residual)
    moe_input = (normed * gain_ref[1:2, :] + shift_ref[1:2, :]).astype(BF16)
    a2_ref[...] = moe_input
    gate = gate_of(moe_input, router_ref[...])
    gate_ref[...] = gate
    picks = slot_pick_rows(slot_row_ref[...], sent_ref.shape[0])
    picks = picks[0] + picks[1]
    for at in row_parts(sent_ref.shape[0]):
        sent_ref[at, :] = dot(picks[at], moe_input).astype(BF16)


def gate_of(rows, router_parts):
    parts = dot(rows, router_parts)
    experts = parts.shape[1] // 3
    logits = parts[:, :experts] + (
        parts[:, experts : 2 * experts] + parts[:, 2 * experts :]
    )
    raised = jnp.exp(logits - jnp.max(logits, -1, keepdims=True))
    return raised / jnp.sum(raised, -1, keepdims=True)


PARTS = 4


def row_parts(rows):
    step = rows // PARTS
    return [slice(at, at + step) for at in range(0, rows, step)]


def ffn_fwd_body(layer, share, x_ref, w1_ref, b1_ref, w2_ref, b2_ref, pre_ref, out_ref):
    bias = b2_ref[layer] * share
    for at in row_parts(out_ref.shape[0]):
        pre_act = dot(x_ref[at, :], w1_ref[...]) + b1_ref[layer]
        pre_ref[at, :] = pre_act.astype(BF16)
        hidden, _ = gelu_parts(pre_act)
        out_ref[at, :] = (dot(hidden.astype(BF16), w2_ref[...]) + bias).astype(BF16)


def ffn_back_body(w2_ref, pre_ref, w1_ref, dy_ref, dx_ref, hid_ref, dpre_ref):
    for at in row_parts(dx_ref.shape[0]):
        dhidden = dot_nt(dy_ref[at, :], w2_ref[...])
        pre_act = pre_ref[at, :].astype(F32)
        hidden, half = gelu_parts(pre_act)
        hid_ref[at, :] = hidden.astype(BF16)
        dpre = (dhidden * gelu_slope(pre_act, half)).astype(BF16)
        dpre_ref[at, :] = dpre
        dx_ref[at, :] = dot_nt(dpre, w1_ref[...]).astype(BF16)


def ffn_both_body(
    layer, share, cap, place_ref, router_ref, x_ref, gx_ref, w1_ref, b1_ref, w2_ref, b2_ref,
    out_ref, dx_ref, hid_ref, dpre_ref, dy_ref,
):
    bias = b2_ref[layer] * share
    width = x_ref.shape[1]
    below = lax.broadcasted_iota(I32, (cap, LANES), 0) == lax.broadcasted_iota(I32, (cap, LANES), 1)
    at_row = lax.broadcasted_iota(I32, (cap, 1), 0)
    for at in row_parts(x_ref.shape[0]):
        x = x_ref[at, :]
        pre_act = dot(x, w1_ref[...]) + b1_ref[layer]
        gate = gate_of(x, router_ref[...])
        lane = lax.broadcasted_iota(I32, gate.shape, 1)
        chosen = jnp.sum(jnp.where(lane == place_ref[3], gate, 0.0), -1, keepdims=True)
        upstream = gx_ref[at, :].astype(F32)
        dy = (chosen * upstream).astype(BF16)
        dy_ref[at, :] = dy
        hidden, half = gelu_parts(pre_act)
        hidden = hidden.astype(BF16)
        hid_ref[at, :] = hidden
        result = (dot(hidden, w2_ref[...]) + bias).astype(BF16)
        out_ref[at, :] = result
        choice = jnp.sum(upstream * result.astype(F32), -1, keepdims=True)
        dpre = (dot_nt(dy, w2_ref[...]) * gelu_slope(pre_act, half)).astype(BF16)
        dpre_ref[at, :] = dpre
        dx = dot_nt(dpre, w1_ref[...])
        blocks = []
        for low in range(0, at.stop - at.start, cap):
            row = jnp.sum(jnp.where(below, choice[low : low + cap], 0.0), 0, keepdims=True)
            row = jnp.concatenate([row, jnp.zeros((1, width - LANES), F32)], 1)
            high = row.astype(BF16).astype(F32)
            block = jnp.where(at_row == cap - 2, high, dx[low : low + cap])
            blocks.append(jnp.where(at_row == cap - 1, row - high, block))
        dx_ref[at, :] = jnp.concatenate(blocks, 0).astype(BF16)


def ffn_grads_body(x_ref, dpre_ref, hid_ref, dy_ref, *refs):
    g1_ref, gb1_ref, g2_ref, gb2_ref = refs[-4:]
    g1_ref[0] = dot_tn(x_ref[...], dpre_ref[...])
    gb1_ref[0] = jnp.sum(dpre_ref[...].astype(F32), 0, keepdims=True)
    g2_ref[0] = dot_tn(hid_ref[...], dy_ref[...])
    gb2_ref[0] = jnp.sum(dy_ref[...].astype(F32), 0, keepdims=True)


def combine_body(n, me_ref, ret_ref, gate_ref, ids_ref, slot_col_ref, *refs):
    piece_refs, refs = refs[:n], refs[n:]
    scratch = refs[-1]
    picks = slot_pick_cols(slot_col_ref[...], ret_ref.shape[0])
    chosen = picked_probs(gate_ref[...], ids_ref[...])
    y0 = dot(picks[0], ret_ref[...])
    y1 = dot(picks[1], ret_ref[...])
    for ref, rows in zip(refs[:-1], (y0, y1)):
        ref[...] = rows.astype(BF16)
    put_pieces(me_ref, chosen[0] * y0 + chosen[1] * y1, scratch, piece_refs)


def router_back(choices, gate, ids, moe_input, router, grad_ref):
    lane = lax.broadcasted_iota(I32, gate.shape, 1)
    prob_grad = jnp.zeros_like(gate)
    for k in range(2):
        prob_grad = prob_grad + jnp.where(lane == ids[:, k : k + 1], choices[k], 0.0)
    logit_grad = gate * (prob_grad - jnp.sum(prob_grad * gate, -1, keepdims=True))
    high, low = split_two(logit_grad)
    grad_ref[...] = dot_tn(high, moe_input) + dot_tn(low, moe_input)
    w_high, w_low = split_two(router)
    return dot_nt(high, w_high) + (dot_nt(high, w_low) + dot_nt(low, w_high))


def moe_back_body(
    n, cap, fresh, me_ref, dx_ref, gate_ref, ids_ref, slot_col_ref, a2_ref, router_ref, *refs
):
    scratch = refs[-1]
    dx = dx_ref[...]
    slot_col = slot_col_ref[...]
    picks = slot_pick_cols(slot_col, dx.shape[0])
    grad = dot(picks[0] + picks[1], dx)
    gate, ids = gate_ref[...], ids_ref[...]
    if fresh:
        lane = lax.broadcasted_iota(I32, gate.shape, 1)
        spot = lax.broadcasted_iota(I32, (gate.shape[0], LANES), 1)
        ends = range(cap, dx.shape[0] + 1, cap)
        sides = [
            jnp.concatenate([dx[end - row : end - row + 1, :LANES] for end in ends], 0)
            for row in (2, 1)
        ]
        choices = []
        for k in range(2):
            own = jnp.where(lane == ids[:, k : k + 1], 1.0, 0.0).astype(BF16)
            values = dot(own, sides[0]) + dot(own, sides[1])
            here = spot == slot_col[:, k : k + 1] - ids[:, k : k + 1] * cap
            choices.append(jnp.sum(jnp.where(here, values, 0.0), -1, keepdims=True))
    else:
        up_ref, y0_ref, y1_ref, *refs = refs
        upstream = load_rows(up_ref, scratch)
        choices = [
            jnp.sum(upstream * ref[...].astype(F32), -1, keepdims=True) for ref in (y0_ref, y1_ref)
        ]
    piece_refs, (grad_ref, scratch) = refs[:n], refs[n:]
    grad = grad + router_back(choices, gate, ids, a2_ref[...], router_ref[...], grad_ref)
    put_pieces(me_ref, grad, scratch, piece_refs)


def attn_back_body(n, heads, real, place_ref, resid_ref, *refs):
    da2_refs, refs = refs[:n], refs[n:]
    up_ref, gain_ref, shift_ref, wqkv_ref, bqv_ref, wout_ref, stream_ref, router_ref, *refs = refs
    piece_refs, refs = refs[:n], refs[n:]
    dr_ref, keep_ref, send_ref, all_ref, scratch, grad_scratch = refs
    me_ref = place_ref.at[pl.ds(2, 1)]
    normed, attn_input, (query, key, value), weights, mixed = attend(
        load_rows(stream_ref, scratch), heads, real, gain_ref[0:1, :], shift_ref[0:1, :],
        wqkv_ref, bqv_ref,
    )
    upstream = load_rows(up_ref, scratch)
    moe_grad = take_pieces(me_ref, da2_refs, scratch)
    normed_two, inv_std = norm_parts(resid_ref[...])
    share = 1.0 / n
    all_ref[2:3, :] = jnp.sum(moe_grad * normed_two, 0, keepdims=True) * share
    all_ref[3:4, :] = jnp.sum(moe_grad, 0, keepdims=True) * share
    resid_grad = upstream + norm_back(moe_grad, normed_two, inv_std, gain_ref[1:2, :])
    dr_ref[...] = resid_grad
    all_ref[4:5, :] = jnp.sum(resid_grad, 0, keepdims=True) * share
    proj_grad = resid_grad.astype(BF16)
    mixed_grad = dot_nt(proj_grad, wout_ref[...]).astype(BF16)
    width = wout_ref.shape[0]
    dquery = jnp.zeros(query.shape, F32)
    dkey = jnp.zeros(query.shape, F32)
    dvalue = jnp.zeros(query.shape, F32)
    for head in range(heads):
        probs = weights[head]
        own = only_head(mixed_grad, head)
        dvalue = dvalue + dot_tn(probs.astype(BF16), own)
        dot_grad = dot_nt(own, value)
        score_grad = (
            probs * (dot_grad - jnp.sum(dot_grad * probs, -1, keepdims=True))
        ).astype(BF16)
        dquery = dquery + dot(score_grad, only_head(key, head))
        dkey = dkey + dot_tn(score_grad, only_head(query, head))
    attn_grad = None
    three = []
    for part, rows in enumerate((dquery * SCALE, dkey * SCALE, dvalue)):
        three.append(rows.astype(BF16))
        term = dot(three[part], wqkv_ref[part * width : (part + 1) * width, :])
        attn_grad = term if attn_grad is None else attn_grad + term
    put_pieces(me_ref, attn_grad, scratch, piece_refs)
    all_ref[0:1, :] = jnp.sum(attn_grad * normed, 0, keepdims=True)
    all_ref[1:2, :] = jnp.sum(attn_grad, 0, keepdims=True)
    all_ref[5:8, :] = jnp.zeros((3, all_ref.shape[1]), F32)
    for row, part in enumerate((0, 2)):
        sums = jnp.sum(three[part].astype(F32), 0, keepdims=True)
        for block in range(n):
            own = jnp.where(place_ref[2] == block, sums, 0.0)
            all_ref[5 + row : 6 + row, block * width : (block + 1) * width] = own
    all_ref[8:, :] = router_ref[...]
    for part in range(3):
        grad_scratch[part * width : (part + 1) * width, :] = dot_tn(three[part], attn_input)
    grad_scratch[3 * width :, :] = dot_tn(mixed, proj_grad)
    core, half = place_ref[0], keep_ref.shape[0]
    keep_ref[...] = grad_scratch[pl.ds(pl.multiple_of(core * half, 8), half), :].astype(BF16)
    send_ref[...] = grad_scratch[pl.ds(pl.multiple_of((1 - core) * half, 8), half), :].astype(BF16)


def grad_cut_body(count, place_ref, keep_ref, got_ref, *refs):
    small_refs, refs = refs[: -count - 1], refs[-count - 1 :]
    piece_refs, scratch = refs[:count], refs[count]
    rows, half = piece_refs[0].shape[0], keep_ref.shape[0]
    scratch[:half, :] = keep_ref[...].astype(F32) + got_ref[...].astype(F32)
    if small_refs:
        scratch[half:, :] = jnp.zeros((scratch.shape[0] - half, scratch.shape[1]), F32)
        total = small_refs[0][...].astype(F32)
        for ref in small_refs[1:]:
            total = total + ref[...].astype(F32)
        scratch[half : half + total.shape[0], :] = total
    for step, ref in enumerate(piece_refs):
        owner = lax.bitwise_xor(place_ref[1], step)
        ref[...] = scratch[pl.ds(pl.multiple_of(owner * rows, 8), rows), :].astype(BF16)


def grad_widen_body(count, place_ref, *refs):
    qkv_ref, out_ref, scratch = refs[-3:]
    rows, split = refs[0].shape[0], qkv_ref.shape[1]
    for side in range(2):
        core = lax.bitwise_xor(place_ref[0], side)
        for step in range(count):
            owner = core * count + lax.bitwise_xor(place_ref[1], step)
            ref = refs[side * count + step]
            scratch[pl.ds(pl.multiple_of(owner * rows, 8), rows), :] = ref[...].astype(F32)
    qkv_ref[0] = scratch[:split, :]
    out_ref[0] = scratch[split:, :]


def grad_join_body(layers, count, half, n, place_ref, *refs):
    piece_refs = refs[: 2 * count]
    qkv_ref, out_ref, gain_ref, shift_ref, bqv_ref, bout_ref, router_ref, scratch, below = refs[-9:]
    rows = piece_refs[0].shape[0]
    split, width = qkv_ref.shape[1], bqv_ref.shape[2]
    side_rows = count * rows
    for side in range(2):
        for step in range(count):
            owner = lax.bitwise_xor(place_ref[1], step)
            ref = piece_refs[side * count + step]
            below[side, pl.ds(pl.multiple_of(owner * rows, 8), rows), :] = ref[...].astype(F32)
        core = lax.bitwise_xor(place_ref[0], side)
        scratch[pl.ds(pl.multiple_of(core * half, 8), half), :] = below[side, :half, :]
    qkv_ref[0] = scratch[:split, :]
    out_ref[0] = scratch[split:, :]
    small = below[0, half:, :] + below[1, half:, :]
    one = 8 + router_ref.shape[1]
    for layer in range(layers):
        own = small[layer * one : (layer + 1) * one]
        gain_ref[layer, 0:1, :] = own[0:1]
        gain_ref[layer, 1:2, :] = own[2:3]
        shift_ref[layer, 0:1, :] = own[1:2]
        shift_ref[layer, 1:2, :] = own[3:4]
        bout_ref[layer : layer + 1, :] = own[4:5]
        picked = jnp.zeros((2, width), F32)
        for block in range(n):
            part = own[5:7, block * width : (block + 1) * width]
            picked = picked + jnp.where(place_ref[2] == block, part, 0.0)
        bqv_ref[layer] = picked
        router_ref[layer] = own[8:]


def norm_one_back_body(n, dispatch, me_ref, stream_ref, *refs):
    da1_refs, refs = refs[:n], refs[n:]
    dr_ref, gain_ref, *refs = refs
    if dispatch:
        gate_ref, ids_ref, slot_row_ref, *refs = refs
    gx_ref, *refs = refs
    if dispatch:
        sent_grad_ref, *refs = refs
    (scratch,) = refs
    attn_grad = take_pieces(me_ref, da1_refs, scratch)
    normed, inv_std = norm_parts(load_rows(stream_ref, scratch))
    upstream = dr_ref[...] + norm_back(attn_grad, normed, inv_std, gain_ref[0:1, :])
    if dispatch:
        gx_ref[...] = upstream
    else:
        gx_ref[:, 0, :] = upstream[: gx_ref.shape[0]]
    if dispatch:
        picks = slot_pick_rows(slot_row_ref[...], sent_grad_ref.shape[0])
        chosen = picked_probs(gate_ref[...], ids_ref[...])
        scaled = [(chosen[k] * upstream).astype(BF16) for k in range(2)]
        for at in row_parts(sent_grad_ref.shape[0]):
            rows = dot(picks[0][at], scaled[0]) + dot(picks[1][at], scaled[1])
            sent_grad_ref[at, :] = rows.astype(BF16)


def add_out_body(n, me_ref, base_ref, *refs):
    mix_refs, (out_ref, scratch) = refs[:n], refs[n:]
    total = base_ref[...] + take_pieces(me_ref, mix_refs, scratch)
    out_ref[:, 0, :] = total[: out_ref.shape[0]]


def step_on(rows, step, n):
    return lax.ppermute(rows, "tensor", [(i, (i + step) % n) for i in range(n)])


def add_up(own, arrived):
    total = own.astype(F32)
    for rows in arrived:
        total = total + rows.astype(F32)
    return total.astype(BF16)


def tensor_scatter(pieces):
    return [step_on(pieces[step], step, len(pieces)) for step in range(1, len(pieces))]


def tensor_gather(own, n):
    return [own] + [step_on(own, step, n) for step in range(1, n)]


def tie(first, other):
    flat, tree = jax.tree.flatten((first, other))
    return jax.tree.unflatten(tree, lax.optimization_barrier(tuple(flat)))


def tensor_total(pieces):
    return tensor_gather(add_up(pieces[0], tensor_scatter(pieces)), len(pieces))


def swap(rows, axis, step, size):
    return lax.ppermute(rows, axis, [(i, i ^ step) for i in range(size)])


def group_exchange(rows, groups):
    blocks = rows.reshape(groups, -1, rows.shape[-1])
    moved = lax.all_to_all(blocks, GROUP_AXES, split_axis=0, concat_axis=0, tiled=True)
    return moved.reshape(rows.shape)


def on_device(
    n,
    groups,
    tokens,
    cotangent,
    routes,
    norm_gain,
    norm_bias,
    w_qkv,
    b_qv,
    w_out,
    b_out,
    w_router,
    w_in,
    b_in,
    w_exp_out,
    b_exp_out,
):
    layers = w_qkv.shape[0]
    images, seq_len, model_width = tokens.shape
    real = images * seq_len
    experts = w_router.shape[2]
    capacity = 3 * real // experts
    cap = ceil_to(capacity + 2, 16)
    slots = experts * cap
    local_cols = w_qkv.shape[3]
    heads = local_cols // HEAD_DIM
    hidden = w_in.shape[3]
    chunk = ceil_to(-(-real // n), 8)
    rows = n * chunk
    me = lax.axis_index("tensor").astype(I32).reshape(1)
    place = jnp.stack(
        [lax.axis_index(name) for name in ALL_AXES] + [lax.axis_index(GROUP_AXES)]
    ).astype(I32)

    tokens_in = tokens.reshape(real, model_width)
    cot = cotangent.reshape(real, model_width)
    ids_col = jnp.pad(
        routes.reshape(layers, real, 2), ((0, 0), (0, rows - real), (0, 0)), constant_values=-1
    )
    ids_row = ids_col.transpose(0, 2, 1)
    qkv_weights = w_qkv.transpose(0, 2, 3, 1).reshape(layers, 3 * local_cols, model_width)

    last = layers - 1
    stage = pltpu.VMEM((rows, model_width), F32)
    piece = ((chunk, model_width), BF16)
    high = w_router.astype(BF16)
    rest = w_router - high.astype(F32)
    middle = rest.astype(BF16)
    low = (rest - middle.astype(F32)).astype(BF16)
    router_parts = jnp.concatenate([high, middle, low], 2)

    def norms(layer, near=True):
        wrap = Near if near else Far
        return [wrap(norm_gain, layer), wrap(norm_bias, layer)]

    def attn_weights(layer, near=True):
        wrap = Near if near else Far
        return [wrap(qkv_weights, layer), wrap(b_qv, layer), wrap(w_out, layer)]

    def attn_fwd(layer, base, mix):
        packed = layer == last
        outs = [] if packed else [piece] * n
        outs = outs + ([((rows, model_width), F32, 1)] if mix else [])
        if packed:
            outs.append(((rows * local_cols // LANES, LANES), BF16))
        weights = attn_weights(layer, mix)
        got = kernel_call(
            functools.partial(attn_fwd_body, n, heads, real, bool(mix), packed),
            [me, Far(base), *mix, *norms(layer, mix), *(weights[:2] if packed else weights)],
            outs, [stage], scalars=1, name="attn_fwd",
        )
        at = 0 if packed else n
        return got[-1:] if packed else got[:n], got[at] if mix else base

    def moe_pre(layer, base, proj):
        buffers = [stage]
        if layer == last:
            proj = proj + [Far(w_out, layer)] + [Far(v) for pair in heads_out for v in pair]
            buffers.append(pltpu.VMEM((n - 1, local_cols, model_width), BF16))
        return kernel_call(
            functools.partial(moe_pre_body, n, layer, layer == last),
            [place, Far(base), *proj, b_out, *norms(layer), Near(router_parts, layer),
             Near(ids_col, layer), Near(slot_row, layer)],
            [
                ((rows, model_width), F32, 1),
                ((rows, model_width), BF16, 1),
                ((rows, experts), F32, 1),
                ((slots, model_width), BF16, PARTS),
            ],
            buffers, scalars=1, name="moe_pre",
        )

    experts_in = w_in.reshape(layers, model_width, hidden)
    experts_out = w_exp_out.reshape(layers, hidden, model_width)

    def full_spec(shape):
        return pl.BlockSpec(shape, lambda i: (0,) * len(shape))

    def whole_spec(array):
        return pl.BlockSpec(array.shape, lambda i: (0,) * array.ndim)

    b_first = b_in.reshape(layers, 1, hidden)
    b_second = b_exp_out.reshape(layers, 1, model_width)

    side = local_cols // 2
    own_side = lax.dynamic_slice_in_dim(w_out[last], place[0] * side, side, 0)

    def far_heads(step):
        mine = step_on(own_side, step, n)
        return [mine, swap(mine, "dp", 1, 2)]

    saved, heads_out = [], [None] * (n - 1)
    stream, mix = tokens_in, ()
    for layer in range(layers):
        pieces, stream = attn_fwd(layer, stream, mix)
        if layer == 0:
            first_arrived = tensor_scatter(pieces)
            own_piece, late_cot = tie(pieces[0], cot)
        slot_col, slot_row, sent_cot = kernel_call(
            functools.partial(slots_body, experts, cap),
            [ids_col, ids_row, Far(late_cot)],
            [((layers, rows, 2), I32), ((layers, 2, rows), I32), ((slots, model_width), BF16)],
            [stage], name="slots",
        )
        if layer == last:
            proj = tensor_gather(pieces[0], n)
        elif layer > 0:
            proj = tensor_total(pieces)
        else:
            first_arrived, sent_cot = tie(first_arrived, sent_cot)
            proj = tensor_gather(add_up(own_piece, first_arrived), n)
            cot_arrived = group_exchange(sent_cot, groups)
        got = moe_pre(layer, stream, proj)
        residual, a2, gate, sent = got[:4]
        if layer == 0:
            sent, cot_arrived = tie(sent, cot_arrived)
        if layer < last:
            arrived = group_exchange(sent, groups)
            if layer == last - 1:
                for step in range(1, n, 2):
                    arrived, heads_out[step - 1] = tie(arrived, far_heads(step))
            pre_act, result = kernel_call(
                functools.partial(ffn_fwd_body, layer, 1.0 / n),
                [arrived, Far(experts_in, layer), b_first, Far(experts_out, layer), b_second],
                [((slots, hidden), BF16, PARTS), ((slots, model_width), BF16, PARTS)],
                name="ffn_fwd",
            )
            returned = group_exchange(result, groups)
            if layer == last - 1:
                for step in range(2, n, 2):
                    returned, heads_out[step - 1] = tie(returned, far_heads(step))
            got = kernel_call(
                functools.partial(combine_body, n),
                [me, returned, Far(gate), Near(ids_col, layer), Near(slot_col, layer)],
                [piece] * n + [((rows, model_width), BF16, 1)] * 2,
                [stage], scalars=1, name="combine",
            )
            mix = tensor_total(got[:n])
            saved.append((stream, residual, a2, gate, arrived, pre_act, got[n:]))
            stream = residual
        else:
            saved.append((stream, residual, a2, gate))

    half = (4 * local_cols) // 2
    chips = groups // 2
    small_rows = ceil_to(layers * (8 + experts), 8 * chips)
    cut_rows = (half + small_rows) // chips
    qkv_shape = (layers, 3 * local_cols, model_width)
    out_shape = (layers, local_cols, model_width)

    def expert_grads(layer, ffn_ins, before):
        return block_call(
            ffn_grads_body,
            [pinned(v) for v in ffn_ins] + list(before or ()),
            ffn_outs,
            grid=(1,),
            in_specs=[whole_spec(v) for v in ffn_ins]
            + [pl.BlockSpec(memory_space=pl.ANY)] * (4 if before else 0),
            out_specs=[
                pl.BlockSpec((1,) + shape[1:], lambda i: (layer, 0, 0)) for shape, _ in ffn_outs
            ],
            vmem=28,
            aliases={len(ffn_ins) + i: i for i in range(4)} if before else None,
            name="ffn_grads",
        )

    def widen(given):
        return block_call(
            functools.partial(grad_widen_body, chips),
            [place, *given],
            [(qkv_shape, F32), (out_shape, F32)],
            grid=(1,),
            in_specs=[pl.BlockSpec(memory_space=pltpu.SMEM)]
            + [full_spec((half // chips, model_width))] * (2 * chips),
            out_specs=[
                pl.BlockSpec((1,) + shape[1:], lambda i: (1, 0, 0))
                for shape in (qkv_shape, out_shape)
            ],
            scratch=[pltpu.VMEM((2 * half, model_width), F32)],
            name="grad_widen",
        )

    def add_out():
        (total,) = kernel_call(
            functools.partial(add_out_body, n),
            [me, Far(saved[last][1]), *out_chunks],
            [((real, 1, model_width), F32)], [stage], scalars=1, name="add_out",
        )
        return total

    ffn_outs = [
        ((layers, model_width, hidden), F32),
        ((layers, 1, hidden), F32),
        ((layers, hidden, model_width), F32),
        ((layers, 1, model_width), F32),
    ]
    ffn_grads, wide, small, cuts = None, None, {}, {}
    upstream = cot
    for layer in reversed(range(layers)):
        stream, residual, a2, gate = saved[layer][:4]
        back_ins = [Far(gate), Near(ids_col, layer), Near(slot_col, layer), Far(a2),
                    Near(w_router, layer)]
        if layer == last:
            arrived = group_exchange(sent, groups)
            result, dx, hid, dpre, grad_arrived = kernel_call(
                functools.partial(ffn_both_body, layer, 1.0 / n, cap),
                [place, Near(router_parts, layer), arrived, cot_arrived, Far(experts_in, layer),
                 b_first, Far(experts_out, layer), b_second],
                [((slots, model_width), BF16, PARTS)] * 2 + [((slots, hidden), BF16, PARTS)] * 2
                + [((slots, model_width), BF16, PARTS)],
                scalars=1, name="ffn_both",
            )
            dx = group_exchange(dx, groups)
            got = kernel_call(
                functools.partial(moe_back_body, n, cap, True),
                [me, dx, *back_ins],
                [piece] * n + [((experts, model_width), F32)],
                [stage], scalars=1, name="moe_back",
            )
            router_grad = got[n]
            ffn_grads = expert_grads(layer, [arrived, dpre, hid, grad_arrived], None)
        else:
            arrived, pre_act, (y0, y1) = saved[layer][4:]
            grad_arrived, cuts[layer + 1] = tie(
                group_exchange(sent_grad, groups), cuts[layer + 1]
            )
            if layer == last - 1:
                grad_arrived, out_arrived = tie(grad_arrived, tensor_scatter(out_mix))
                out_own = add_up(out_mix[0], out_arrived)
            dx, hid, dpre = kernel_call(
                ffn_back_body,
                [Far(experts_out, layer), Far(pre_act), Far(experts_in, layer), grad_arrived],
                [((slots, model_width), BF16, PARTS)] + [((slots, hidden), BF16, PARTS)] * 2,
                name="ffn_back",
            )
            ffn_grads = expert_grads(layer, [arrived, dpre, hid, grad_arrived], ffn_grads)
            dx, ffn_grads = tie(group_exchange(dx, groups), ffn_grads)
            if layer == last - 1:
                dx, out_chunks = tie(dx, tensor_gather(out_own, n))
            got = kernel_call(
                functools.partial(moe_back_body, n, cap, False),
                [me, dx, *back_ins, Far(upstream), Far(y0), Far(y1)],
                [piece] * n + [((experts, model_width), F32)],
                [stage], scalars=1, name="moe_back",
            )
            router_grad = got[n]
        arrived = tensor_scatter(got[:n])
        if layer < last:
            above = cuts[layer + 1]
            arrived, moved = tie(
                arrived, [swap(above[step], "expert", step, chips) for step in range(1, chips)]
            )
            grad_own = add_up(above[0], moved)
        da2 = tensor_gather(add_up(got[0], arrived), n)
        if layer == last:
            da2, returned = tie(da2, group_exchange(result, groups))
            out_mix = kernel_call(
                functools.partial(combine_body, n),
                [me, returned, Far(gate), Near(ids_col, layer), Near(slot_col, layer)],
                [piece] * n, [stage], scalars=1, name="combine",
            )
        if layer < last:
            da2, moved = tie(
                da2, [swap(grad_own, "expert", step, chips) for step in range(1, chips)]
            )
            halves = [grad_own] + moved
        if layer == last - 1:
            da2, output = tie(da2, add_out())
        got = kernel_call(
            functools.partial(attn_back_body, n, heads, real),
            [place, Far(residual), *da2, Far(upstream), *norms(layer), *attn_weights(layer),
             Far(stream), router_grad],
            [piece] * n + [
                ((rows, model_width), F32, 1),
                ((half, model_width), BF16, 1),
                ((half, model_width), BF16),
                ((8 + experts, model_width), F32),
            ],
            [stage, pltpu.VMEM((2 * half, model_width), F32)], scalars=1, name="attn_back",
        )
        dr, small[layer] = got[n], got[-1]
        keep, send = got[n + 1 : n + 3]
        if layer < last:
            halves += [swap(rows_of, "dp", 1, 2) for rows_of in halves]
        if layer > 0:
            arrived = tensor_scatter(got[:n])
            if layer == last:
                ffn_grads, arrived = tie(ffn_grads, arrived)
            da1 = tensor_gather(add_up(got[0], arrived), n)
            da1, got_half = tie(da1, swap(send, "dp", 1, 2))
            cuts[layer] = kernel_call(
                functools.partial(grad_cut_body, chips),
                [place, Far(keep), got_half],
                [((half // chips, model_width), BF16)] * chips,
                [pltpu.VMEM((half, model_width), F32)], scalars=1, name="grad_cut",
            )
        else:
            smalls = jnp.concatenate([small[at] for at in range(layers)], 0).astype(BF16)
            got_half = swap(send, "dp", 1, 2)
            others = [step_on(smalls, step, n) for step in range(1, n)]
            cut = kernel_call(
                functools.partial(grad_cut_body, chips),
                [place, Far(keep), got_half, smalls, *others],
                [((cut_rows, model_width), BF16)] * chips,
                [pltpu.VMEM((half + small_rows, model_width), F32)], scalars=1, name="grad_cut",
            )
            moved = [swap(cut[step], "expert", step, chips) for step in range(1, chips)]
            moved, (da1_arrived, wide) = tie(moved, (tensor_scatter(got[:n]), widen(halves)))
            arrived = moved
            da1 = tensor_gather(add_up(got[0], da1_arrived), n)
            own = add_up(cut[0], arrived)
            own_half = [own] + [swap(own, "expert", step, chips) for step in range(1, chips)]
            own_half, da1 = tie(own_half, da1)
            pieces = own_half + [swap(rows_of, "dp", 1, 2) for rows_of in own_half]
        ins = [me, Far(stream), *da1, Far(dr), Near(norm_gain, layer)]
        if layer > 0:
            below = layer - 1
            upstream, sent_grad = kernel_call(
                functools.partial(norm_one_back_body, n, True),
                ins + [Far(saved[below][3]), Near(ids_col, below), Near(slot_row, below)],
                [((rows, model_width), F32, 1), ((slots, model_width), BF16, PARTS)],
                [stage], scalars=1, name="norm_back_send",
            )
        else:
            (grad_tokens,) = kernel_call(
                functools.partial(norm_one_back_body, n, False),
                ins, [((real, 1, model_width), F32)], [stage], scalars=1, name="norm_back",
            )
    g1, gb1, g2, gb2 = ffn_grads

    small_shapes = [
        (layers, 2, model_width),
        (layers, 2, model_width),
        (layers, 2, local_cols),
        (layers, model_width),
        (layers, experts, model_width),
    ]
    given = list(wide or ())
    qkv_grad, out_grad, gain_grad, shift_grad, qv_grad, outb_grad, router_out = block_call(
        functools.partial(grad_join_body, layers, chips, half, n),
        [place, *pieces, *given],
        [(shape, F32) for shape in (qkv_shape, out_shape, *small_shapes)],
        grid=(1,),
        in_specs=[pl.BlockSpec(memory_space=pltpu.SMEM)]
        + [full_spec((cut_rows, model_width))] * (2 * chips)
        + [pl.BlockSpec(memory_space=pl.ANY)] * len(given),
        out_specs=[
            pl.BlockSpec((1,) + shape[1:], lambda i: (0, 0, 0)) for shape in (qkv_shape, out_shape)
        ]
        + [full_spec(shape) for shape in small_shapes],
        scratch=[
            pltpu.VMEM((2 * half, model_width), F32),
            pltpu.VMEM((2, half + small_rows, model_width), F32),
        ],
        vmem=24,
        aliases={1 + 2 * chips + i: i for i in range(len(given))},
        name="grad_join",
    )
    qkv_grad = qkv_grad.reshape(layers, 3, local_cols, model_width).transpose(0, 3, 1, 2)
    return (
        output.reshape(images, seq_len, model_width),
        grad_tokens.reshape(images, seq_len, model_width),
        gain_grad,
        shift_grad,
        qkv_grad,
        qv_grad,
        out_grad,
        outb_grad,
        router_out.transpose(0, 2, 1),
        g1[:, None],
        gb1,
        g2[:, None],
        gb2,
    )


def solution(mesh):
    n = mesh.shape["tensor"]
    groups = mesh.shape["dp"] * mesh.shape["expert"]
    return jax.shard_map(
        functools.partial(on_device, n, groups),
        mesh=mesh,
        in_specs=(
            P(("dp", "expert"), None, None),
            P(("dp", "expert"), None, None),
            P(None, ("dp", "expert"), None, None),
            P(),
            P(),
            P(None, None, None, "tensor"),
            P(None, None, "tensor"),
            P(None, "tensor", None),
            P(),
            P(),
            P(None, ("dp", "expert"), None, "tensor"),
            P(None, ("dp", "expert"), "tensor"),
            P(None, ("dp", "expert"), "tensor", None),
            P(None, ("dp", "expert"), None),
        ),
        out_specs=(
            P(("dp", "expert"), None, None),
            P(("dp", "expert"), None, None),
            P(),
            P(),
            P(None, None, None, "tensor"),
            P(None, None, "tensor"),
            P(None, "tensor", None),
            P(),
            P(),
            P(None, ("dp", "expert"), None, "tensor"),
            P(None, ("dp", "expert"), "tensor"),
            P(None, ("dp", "expert"), "tensor", None),
            P(None, ("dp", "expert"), None),
        ),
        check_vma=False,
    )
```

```python
import functools

import jax
import jax.numpy as jnp
from jax import lax
from jax.experimental import pallas as pl
from jax.experimental.pallas import tpu as pltpu
from jax.sharding import PartitionSpec as P

HEAD_DIM = 64
SCALE = HEAD_DIM ** (-0.5)
LANES = 128
GROUP_AXES = ("dp", "expert")
ALL_AXES = ("dp", "expert", "tensor")

epsilon = 1e-06
root_half = 0.7071067811865476
inv_root_tau = 0.3989422804014327

F32 = jnp.float32
BF16 = jnp.bfloat16
I32 = jnp.int32


def ceil_to(value, step):
    return -(-value // step) * step


def dot(a, b):
    return lax.dot_general(a, b, (((1,), (0,)), ((), ())), preferred_element_type=F32)


def dot_nt(a, b):
    return lax.dot_general(a, b, (((1,), (1,)), ((), ())), preferred_element_type=F32)


def dot_tn(a, b):
    return lax.dot_general(a, b, (((0,), (0,)), ((), ())), preferred_element_type=F32)


def split_two(v):
    high = v.astype(BF16)
    return high, (v - high.astype(F32)).astype(BF16)


class Far:
    def __init__(self, array, index=None):
        self.array, self.index = array, index
        self.shape = array.shape if index is None else array.shape[1:]


class Near:
    def __init__(self, array, index):
        self.array, self.index = array, index


class Fetched:
    def __init__(self, copy, ref):
        self.copy, self.ref, self.shape = copy, ref, ref.shape

    def __getitem__(self, at):
        if self.copy is not None:
            self.copy.wait()
            self.copy = None
        return self.ref[at]


class Kept:
    def __init__(self, ref, far_ref, sems):
        self.ref, self.far_ref, self.sems, self.shape = ref, far_ref, sems, ref.shape
        self.copies = []

    def __setitem__(self, at, value):
        self.ref[at] = value
        pair = self.ref, self.far_ref
        if at is not Ellipsis:
            rows = pl.ds(at[0].start, at[0].stop - at[0].start)
            pair = self.ref.at[rows], self.far_ref.at[rows]
        copy = pltpu.make_async_copy(*pair, self.sems.at[len(self.copies)])
        copy.start()
        self.copies.append(copy)


def kernel_call(body, ins, outs, scratch=(), scalars=0, vmem=16, name=None):
    fars = [i for i, v in enumerate(ins) if isinstance(v, Far)]
    keeps = [i for i, v in enumerate(outs) if len(v) > 2]
    arrays = [
        pltpu.with_memory_space_constraint(v.array, pltpu.HBM)
        if isinstance(v, Far)
        else v.array
        if isinstance(v, Near)
        else v
        for v in ins
    ]
    extra = [pltpu.VMEM(ins[i].shape, ins[i].array.dtype) for i in fars]
    extra += [pltpu.VMEM(outs[i][0], outs[i][1]) for i in keeps]
    extra += [pltpu.SemaphoreType.DMA((1,)) for _ in fars]
    extra += [pltpu.SemaphoreType.DMA((outs[i][2],)) for i in keeps]

    def whole(*refs):
        refs = list(refs)
        own = refs[len(ins) + len(outs) :]
        buffers, sems = own[: len(fars) + len(keeps)], own[len(fars) + len(keeps) :]
        sems, rest = sems[: len(buffers)], sems[len(buffers) :]
        for i, v in enumerate(ins):
            if isinstance(v, Near):
                refs[i] = refs[i].at[v.index]
        for at, i in enumerate(fars):
            source = refs[i] if ins[i].index is None else refs[i].at[ins[i].index]
            copy = pltpu.make_async_copy(source, buffers[at], sems[at].at[0])
            copy.start()
            refs[i] = Fetched(copy, buffers[at])
        for at, i in enumerate(keeps, len(fars)):
            refs[len(ins) + i] = Kept(buffers[at], refs[len(ins) + i], sems[at])
        body(*refs[: len(ins) + len(outs)], *rest)
        for i in fars:
            refs[i][...]
        for i in keeps:
            for copy in refs[len(ins) + i].copies:
                copy.wait()

    def space(i):
        if i < scalars:
            return pltpu.SMEM
        return pltpu.HBM if i in fars else pltpu.VMEM

    return pl.pallas_call(
        whole,
        out_shape=[
            pltpu.HBM(*v[:2]) if len(v) > 2 else jax.ShapeDtypeStruct(*v) for v in outs
        ],
        in_specs=[pl.BlockSpec(memory_space=space(i)) for i in range(len(ins))],
        out_specs=[
            pl.BlockSpec(memory_space=pltpu.HBM if i in keeps else pltpu.VMEM)
            for i in range(len(outs))
        ],
        scratch_shapes=extra + list(scratch),
        compiler_params=pltpu.CompilerParams(vmem_limit_bytes=vmem * 1024 * 1024),
        name=name,
    )(*arrays)


def pinned(array):
    return pltpu.with_memory_space_constraint(array, pltpu.HBM)


def block_call(body, ins, outs, grid, in_specs, out_specs, scratch=(), vmem=16, aliases=None,
               name=None):
    return pl.pallas_call(
        body,
        out_shape=[pltpu.HBM(shape, dtype) for shape, dtype in outs],
        grid=grid,
        in_specs=in_specs,
        out_specs=out_specs,
        scratch_shapes=list(scratch),
        input_output_aliases=aliases or {},
        compiler_params=pltpu.CompilerParams(vmem_limit_bytes=vmem * 1024 * 1024),
        name=name,
    )(*ins)


def load_rows(ref, scratch):
    if ref.shape[0] == scratch.shape[0]:
        return ref[...].astype(F32)
    scratch[...] = jnp.zeros_like(scratch)
    scratch[: ref.shape[0], :] = ref[...].astype(F32)
    return scratch[...]


def norm_parts(stream):
    row_mean = jnp.mean(stream, -1, keepdims=True)
    centered = stream - row_mean
    inv_std = lax.rsqrt(jnp.mean(centered * centered, -1, keepdims=True) + epsilon)
    return centered * inv_std, inv_std


def norm_back(upstream, normed, inv_std, gain_row):
    scaled = upstream * gain_row
    return inv_std * (
        scaled
        - jnp.mean(scaled, -1, keepdims=True)
        - normed * jnp.mean(scaled * normed, -1, keepdims=True)
    )


def head_mask(head, width):
    lane = lax.broadcasted_iota(I32, (1, width), 1)
    return (lane >= head * HEAD_DIM) & (lane < (head + 1) * HEAD_DIM)


def only_head(rows, head):
    return jnp.where(head_mask(head, rows.shape[1]), rows, jnp.zeros_like(rows))


def put_pieces(me_ref, value, scratch, out_refs):
    count = len(out_refs)
    chunk = out_refs[0].shape[0]
    scratch[...] = value
    for step, ref in enumerate(out_refs):
        owner = lax.rem(me_ref[0] + step, count)
        ref[...] = scratch[pl.ds(pl.multiple_of(owner * chunk, 8), chunk), :].astype(BF16)


def take_pieces(me_ref, in_refs, scratch):
    count = len(in_refs)
    chunk = in_refs[0].shape[0]
    for step, ref in enumerate(in_refs):
        owner = lax.rem(me_ref[0] + count - step, count)
        scratch[pl.ds(pl.multiple_of(owner * chunk, 8), chunk), :] = ref[...].astype(F32)
    return scratch[...]


def picked_probs(gate, ids):
    lane = lax.broadcasted_iota(I32, gate.shape, 1)
    return [
        jnp.sum(jnp.where(lane == ids[:, k : k + 1], gate, 0.0), -1, keepdims=True) for k in range(2)
    ]


def slot_pick_rows(slot_row, slots):
    tokens = slot_row.shape[1]
    at = lax.broadcasted_iota(I32, (slots, tokens), 0)
    return [jnp.where(at == slot_row[k : k + 1, :], 1.0, 0.0).astype(BF16) for k in range(2)]


def slot_pick_cols(slot_col, slots):
    tokens = slot_col.shape[0]
    at = lax.broadcasted_iota(I32, (tokens, slots), 1)
    return [jnp.where(at == slot_col[:, k : k + 1], 1.0, 0.0).astype(BF16) for k in range(2)]


def gelu_parts(pre_act):
    half = 0.5 * (1.0 + lax.erf(pre_act * root_half))
    return pre_act * half, half


def gelu_slope(pre_act, half):
    return half + pre_act * jnp.exp(-0.5 * pre_act * pre_act) * inv_root_tau


def slots_body(experts, cap, col_ref, row_ref, cot_ref, slot_col_ref, slot_row_ref, gx_ref, scratch):
    layers, tokens, _ = col_ref.shape
    down = lax.broadcasted_iota(I32, (tokens, tokens), 0)
    across = lax.broadcasted_iota(I32, (tokens, tokens), 1)
    before_col = jnp.where(across < down, 1.0, 0.0).astype(BF16)
    before_row = jnp.where(down < across, 1.0, 0.0).astype(BF16)
    lane = lax.broadcasted_iota(I32, (tokens, experts), 1)
    sub = lax.broadcasted_iota(I32, (experts, tokens), 0)
    for layer in range(layers):
        ids = col_ref[layer]
        one = [jnp.where(lane == ids[:, k : k + 1], 1.0, 0.0) for k in range(2)]
        earlier = dot(before_col, (one[0] + one[1]).astype(BF16))
        for k in range(2):
            at = jnp.sum(earlier * one[k], -1, keepdims=True).astype(I32)
            own = ids[:, k : k + 1]
            slot_col_ref[layer, :, k : k + 1] = jnp.where(own < 0, -1, own * cap + at)
        ids = row_ref[layer]
        one = [jnp.where(sub == ids[k : k + 1, :], 1.0, 0.0) for k in range(2)]
        earlier = dot((one[0] + one[1]).astype(BF16), before_row)
        for k in range(2):
            at = jnp.sum(earlier * one[k], 0, keepdims=True).astype(I32)
            own = ids[k : k + 1, :]
            slot_row_ref[layer, k : k + 1, :] = jnp.where(own < 0, -1, own * cap + at)
    picks = slot_pick_rows(slot_row_ref[layers - 1], gx_ref.shape[0])
    gx_ref[...] = dot(picks[0] + picks[1], load_rows(cot_ref, scratch).astype(BF16)).astype(BF16)


def attend(stream, heads, real, gain_row, shift_row, wqkv_ref, bqv_ref):
    normed, inv_std = norm_parts(stream)
    attn_input = (normed * gain_row + shift_row).astype(BF16)
    width = wqkv_ref.shape[0] // 3
    three = []
    for part in range(3):
        rows = dot_nt(attn_input, wqkv_ref[part * width : (part + 1) * width, :])
        if part != 1:
            rows = rows + bqv_ref[part // 2 : part // 2 + 1, :]
        three.append(rows.astype(BF16))
    query, key, value = three
    tokens = query.shape[0]
    keep = lax.broadcasted_iota(I32, (1, tokens), 1) < real
    mixed = jnp.zeros((tokens, width), F32)
    weights = []
    for head in range(heads):
        scores = dot_nt(only_head(query, head), key) * SCALE
        scores = jnp.where(keep, scores, -1e30)
        row_max = jnp.max(scores, -1, keepdims=True)
        raised = jnp.exp(scores - row_max)
        probs = raised / jnp.sum(raised, -1, keepdims=True)
        weights.append(probs)
        mixed = mixed + dot(probs.astype(BF16), only_head(value, head))
    return normed, attn_input, three, weights, mixed.astype(BF16)


def pack_heads(mixed):
    rows, width = mixed.shape
    full = width - width % LANES
    if full == width:
        return mixed
    left, half = mixed[:, full:].astype(F32), rows // 2
    beside = jnp.concatenate([left[:half], left[half:]], 1).astype(BF16)
    parts = [mixed[:, at : at + LANES] for at in range(0, full, LANES)]
    return jnp.concatenate(parts + [beside], 0)


def unpack_heads(packed, rows, width):
    full = width - width % LANES
    if full == width:
        return packed
    parts = [packed[at * rows : (at + 1) * rows] for at in range(full // LANES)]
    beside = packed[full // LANES * rows :].astype(F32)
    left = jnp.concatenate([beside[:, : LANES // 2], beside[:, LANES // 2 :]], 0)
    return jnp.concatenate(parts + [left.astype(BF16)], 1)


def attn_fwd_body(n, heads, real, from_mix, packed, me_ref, *refs):
    base_ref, *refs = refs
    if from_mix:
        mix_refs, refs = refs[:n], refs[n:]
    gain_ref, shift_ref, wqkv_ref, bqv_ref, *refs = refs
    piece_refs = ()
    if not packed:
        wout_ref, *refs = refs
        piece_refs, refs = refs[:n], refs[n:]
    scratch = refs[-1]
    if from_mix:
        stream = take_pieces(me_ref, mix_refs, scratch) + base_ref[...]
        refs[0][...] = stream
    else:
        stream = load_rows(base_ref, scratch)
    mixed = attend(
        stream, heads, real, gain_ref[0:1, :], shift_ref[0:1, :], wqkv_ref, bqv_ref
    )[-1]
    if not piece_refs:
        packed_ref, scratch = refs[-2:]
        packed_ref[...] = pack_heads(mixed)
    else:
        put_pieces(me_ref, dot(mixed, wout_ref[...]), scratch, piece_refs)


def moe_pre_body(n, layer, packed, place_ref, base_ref, *refs):
    me_ref = place_ref.at[pl.ds(2, 1)]
    proj_refs, refs = refs[:n], refs[n:]
    if packed:
        wout_ref, *side_refs = refs[: 2 * n - 1]
        refs = refs[2 * n - 1 :]
    outb_ref, gain_ref, shift_ref, router_ref, slot_row_ref, *refs = refs
    resid_ref, a2_ref, gate_ref, sent_ref, scratch, *refs = refs
    if packed:
        (sides,) = refs
    residual = load_rows(base_ref, scratch)
    if packed:
        width = wout_ref.shape[0]
        for step, mixed_ref in enumerate(proj_refs):
            mixed = unpack_heads(mixed_ref[...], residual.shape[0], width)
            if step > 0:
                wout_ref = sides.at[step - 1]
                for side in range(2):
                    low = lax.bitwise_xor(place_ref[0], side) * (width // 2)
                    at = pl.ds(pl.multiple_of(low, 16), width // 2)
                    wout_ref[at, :] = side_refs[2 * step - 2 + side][...]
            residual = residual + dot(mixed, wout_ref[...])
    else:
        residual = residual + take_pieces(me_ref, proj_refs, scratch)
    residual = residual + outb_ref[layer : layer + 1, :]
    resid_ref[...] = residual
    normed, _ = norm_parts(residual)
    moe_input = (normed * gain_ref[1:2, :] + shift_ref[1:2, :]).astype(BF16)
    a2_ref[...] = moe_input
    gate = gate_of(moe_input, router_ref[...])
    gate_ref[...] = gate
    picks = slot_pick_rows(slot_row_ref[...], sent_ref.shape[0])
    picks = picks[0] + picks[1]
    for at in row_parts(sent_ref.shape[0]):
        sent_ref[at, :] = dot(picks[at], moe_input).astype(BF16)


def gate_of(rows, router_parts):
    parts = dot(rows, router_parts)
    experts = parts.shape[1] // 3
    logits = parts[:, :experts] + (
        parts[:, experts : 2 * experts] + parts[:, 2 * experts :]
    )
    raised = jnp.exp(logits - jnp.max(logits, -1, keepdims=True))
    return raised / jnp.sum(raised, -1, keepdims=True)


PARTS = 4


def row_parts(rows):
    step = rows // PARTS
    return [slice(at, at + step) for at in range(0, rows, step)]


def ffn_fwd_body(share, x_ref, w1_ref, b1_ref, w2_ref, b2_ref, pre_ref, out_ref):
    bias = b2_ref[...] * share
    for at in row_parts(out_ref.shape[0]):
        pre_act = dot(x_ref[at, :], w1_ref[...]) + b1_ref[...]
        pre_ref[at, :] = pre_act.astype(BF16)
        hidden, _ = gelu_parts(pre_act)
        out_ref[at, :] = (dot(hidden.astype(BF16), w2_ref[...]) + bias).astype(BF16)


def ffn_back_body(w2_ref, pre_ref, w1_ref, dy_ref, dx_ref, hid_ref, dpre_ref):
    for at in row_parts(dx_ref.shape[0]):
        dhidden = dot_nt(dy_ref[at, :], w2_ref[...])
        pre_act = pre_ref[at, :].astype(F32)
        hidden, half = gelu_parts(pre_act)
        hid_ref[at, :] = hidden.astype(BF16)
        dpre = (dhidden * gelu_slope(pre_act, half)).astype(BF16)
        dpre_ref[at, :] = dpre
        dx_ref[at, :] = dot_nt(dpre, w1_ref[...]).astype(BF16)


def ffn_both_body(
    share, cap, place_ref, router_ref, x_ref, gx_ref, w1_ref, b1_ref, w2_ref, b2_ref,
    out_ref, dx_ref, hid_ref, dpre_ref, dy_ref,
):
    bias = b2_ref[...] * share
    width = x_ref.shape[1]
    below = lax.broadcasted_iota(I32, (cap, LANES), 0) == lax.broadcasted_iota(I32, (cap, LANES), 1)
    at_row = lax.broadcasted_iota(I32, (cap, 1), 0)
    for at in row_parts(x_ref.shape[0]):
        x = x_ref[at, :]
        pre_act = dot(x, w1_ref[...]) + b1_ref[...]
        gate = gate_of(x, router_ref[...])
        lane = lax.broadcasted_iota(I32, gate.shape, 1)
        chosen = jnp.sum(jnp.where(lane == place_ref[3], gate, 0.0), -1, keepdims=True)
        upstream = gx_ref[at, :].astype(F32)
        dy = (chosen * upstream).astype(BF16)
        dy_ref[at, :] = dy
        hidden, half = gelu_parts(pre_act)
        hidden = hidden.astype(BF16)
        hid_ref[at, :] = hidden
        result = (dot(hidden, w2_ref[...]) + bias).astype(BF16)
        out_ref[at, :] = result
        choice = jnp.sum(upstream * result.astype(F32), -1, keepdims=True)
        dpre = (dot_nt(dy, w2_ref[...]) * gelu_slope(pre_act, half)).astype(BF16)
        dpre_ref[at, :] = dpre
        dx = dot_nt(dpre, w1_ref[...])
        blocks = []
        for low in range(0, at.stop - at.start, cap):
            row = jnp.sum(jnp.where(below, choice[low : low + cap], 0.0), 0, keepdims=True)
            row = jnp.concatenate([row, jnp.zeros((1, width - LANES), F32)], 1)
            high = row.astype(BF16).astype(F32)
            block = jnp.where(at_row == cap - 2, high, dx[low : low + cap])
            blocks.append(jnp.where(at_row == cap - 1, row - high, block))
        dx_ref[at, :] = jnp.concatenate(blocks, 0).astype(BF16)


def ffn_grads_body(x_ref, dpre_ref, hid_ref, dy_ref, *refs):
    g1_ref, gb1_ref, g2_ref, gb2_ref = refs[-4:]
    g1_ref[0] = dot_tn(x_ref[...], dpre_ref[...])
    gb1_ref[0] = jnp.sum(dpre_ref[...].astype(F32), 0, keepdims=True)
    g2_ref[0] = dot_tn(hid_ref[...], dy_ref[...])
    gb2_ref[0] = jnp.sum(dy_ref[...].astype(F32), 0, keepdims=True)


def combine_body(n, me_ref, ret_ref, gate_ref, ids_ref, slot_col_ref, *refs):
    piece_refs, refs = refs[:n], refs[n:]
    scratch = refs[-1]
    picks = slot_pick_cols(slot_col_ref[...], ret_ref.shape[0])
    chosen = picked_probs(gate_ref[...], ids_ref[...])
    y0 = dot(picks[0], ret_ref[...])
    y1 = dot(picks[1], ret_ref[...])
    for ref, rows in zip(refs[:-1], (y0, y1)):
        ref[...] = rows.astype(BF16)
    put_pieces(me_ref, chosen[0] * y0 + chosen[1] * y1, scratch, piece_refs)


def router_back(choices, gate, ids, moe_input, router, grad_ref):
    lane = lax.broadcasted_iota(I32, gate.shape, 1)
    prob_grad = jnp.zeros_like(gate)
    for k in range(2):
        prob_grad = prob_grad + jnp.where(lane == ids[:, k : k + 1], choices[k], 0.0)
    logit_grad = gate * (prob_grad - jnp.sum(prob_grad * gate, -1, keepdims=True))
    high, low = split_two(logit_grad)
    grad_ref[...] = dot_tn(high, moe_input) + dot_tn(low, moe_input)
    experts = gate.shape[1]
    w_high, w_low = router[:, :experts], router[:, experts : 2 * experts]
    return dot_nt(high, w_high) + (dot_nt(high, w_low) + dot_nt(low, w_high))


def moe_back_body(
    n, cap, fresh, me_ref, dx_ref, gate_ref, ids_ref, slot_col_ref, a2_ref, router_ref, *refs
):
    scratch = refs[-1]
    dx = dx_ref[...]
    slot_col = slot_col_ref[...]
    picks = slot_pick_cols(slot_col, dx.shape[0])
    grad = dot(picks[0] + picks[1], dx)
    gate, ids = gate_ref[...], ids_ref[...]
    if fresh:
        lane = lax.broadcasted_iota(I32, gate.shape, 1)
        spot = lax.broadcasted_iota(I32, (gate.shape[0], LANES), 1)
        ends = range(cap, dx.shape[0] + 1, cap)
        sides = [
            jnp.concatenate([dx[end - row : end - row + 1, :LANES] for end in ends], 0)
            for row in (2, 1)
        ]
        choices = []
        for k in range(2):
            own = jnp.where(lane == ids[:, k : k + 1], 1.0, 0.0).astype(BF16)
            values = dot(own, sides[0]) + dot(own, sides[1])
            here = spot == slot_col[:, k : k + 1] - ids[:, k : k + 1] * cap
            choices.append(jnp.sum(jnp.where(here, values, 0.0), -1, keepdims=True))
    else:
        up_ref, y0_ref, y1_ref, *refs = refs
        upstream = load_rows(up_ref, scratch)
        choices = [
            jnp.sum(upstream * ref[...].astype(F32), -1, keepdims=True) for ref in (y0_ref, y1_ref)
        ]
    piece_refs, (grad_ref, scratch) = refs[:n], refs[n:]
    grad = grad + router_back(choices, gate, ids, a2_ref[...], router_ref[...], grad_ref)
    put_pieces(me_ref, grad, scratch, piece_refs)


def attn_back_body(n, heads, real, place_ref, resid_ref, *refs):
    da2_refs, refs = refs[:n], refs[n:]
    up_ref, gain_ref, shift_ref, wqkv_ref, bqv_ref, wout_ref, stream_ref, router_ref, *refs = refs
    piece_refs, refs = refs[:n], refs[n:]
    dr_ref, keep_ref, send_ref, all_ref, scratch, grad_scratch = refs
    me_ref = place_ref.at[pl.ds(2, 1)]
    normed, attn_input, (query, key, value), weights, mixed = attend(
        load_rows(stream_ref, scratch), heads, real, gain_ref[0:1, :], shift_ref[0:1, :],
        wqkv_ref, bqv_ref,
    )
    upstream = load_rows(up_ref, scratch)
    moe_grad = take_pieces(me_ref, da2_refs, scratch)
    normed_two, inv_std = norm_parts(resid_ref[...])
    share = 1.0 / n
    all_ref[2:3, :] = jnp.sum(moe_grad * normed_two, 0, keepdims=True) * share
    all_ref[3:4, :] = jnp.sum(moe_grad, 0, keepdims=True) * share
    resid_grad = upstream + norm_back(moe_grad, normed_two, inv_std, gain_ref[1:2, :])
    dr_ref[...] = resid_grad
    all_ref[4:5, :] = jnp.sum(resid_grad, 0, keepdims=True) * share
    proj_grad = resid_grad.astype(BF16)
    mixed_grad = dot_nt(proj_grad, wout_ref[...]).astype(BF16)
    width = wout_ref.shape[0]
    dquery = jnp.zeros(query.shape, F32)
    dkey = jnp.zeros(query.shape, F32)
    dvalue = jnp.zeros(query.shape, F32)
    for head in range(heads):
        probs = weights[head]
        own = only_head(mixed_grad, head)
        dvalue = dvalue + dot_tn(probs.astype(BF16), own)
        dot_grad = dot_nt(own, value)
        score_grad = (
            probs * (dot_grad - jnp.sum(dot_grad * probs, -1, keepdims=True))
        ).astype(BF16)
        dquery = dquery + dot(score_grad, only_head(key, head))
        dkey = dkey + dot_tn(score_grad, only_head(query, head))
    attn_grad = None
    three = []
    for part, rows in enumerate((dquery * SCALE, dkey * SCALE, dvalue)):
        three.append(rows.astype(BF16))
        term = dot(three[part], wqkv_ref[part * width : (part + 1) * width, :])
        attn_grad = term if attn_grad is None else attn_grad + term
    put_pieces(me_ref, attn_grad, scratch, piece_refs)
    all_ref[0:1, :] = jnp.sum(attn_grad * normed, 0, keepdims=True)
    all_ref[1:2, :] = jnp.sum(attn_grad, 0, keepdims=True)
    all_ref[5:8, :] = jnp.zeros((3, all_ref.shape[1]), F32)
    for row, part in enumerate((0, 2)):
        sums = jnp.sum(three[part].astype(F32), 0, keepdims=True)
        for block in range(n):
            own = jnp.where(place_ref[2] == block, sums, 0.0)
            all_ref[5 + row : 6 + row, block * width : (block + 1) * width] = own
    all_ref[8:, :] = router_ref[...]
    for part in range(3):
        grad_scratch[part * width : (part + 1) * width, :] = dot_tn(three[part], attn_input)
    grad_scratch[3 * width :, :] = dot_tn(mixed, proj_grad)
    core, half = place_ref[0], keep_ref.shape[0]
    keep_ref[...] = grad_scratch[pl.ds(pl.multiple_of(core * half, 8), half), :].astype(BF16)
    send_ref[...] = grad_scratch[pl.ds(pl.multiple_of((1 - core) * half, 8), half), :].astype(BF16)


def grad_cut_body(count, place_ref, keep_ref, got_ref, *refs):
    piece_refs, scratch = refs[:count], refs[count]
    rows = piece_refs[0].shape[0]
    scratch[...] = keep_ref[...].astype(F32) + got_ref[...].astype(F32)
    for step, ref in enumerate(piece_refs):
        owner = lax.bitwise_xor(place_ref[1], step)
        ref[...] = scratch[pl.ds(pl.multiple_of(owner * rows, 8), rows), :].astype(BF16)


def add_beside_body(own_count, *refs):
    refs, out_ref = refs[:-1], refs[-1]
    sums = []
    for part in (refs[:own_count], refs[own_count:]):
        total = part[0][...].astype(F32)
        for ref in part[1:]:
            total = total + ref[...].astype(F32)
        sums.append(total)
    out_ref[...] = jnp.concatenate(sums, 0).astype(BF16)


def grad_widen_body(count, place_ref, *refs):
    qkv_ref, out_ref, scratch = refs[-3:]
    rows, split = refs[0].shape[0], qkv_ref.shape[1]
    for side in range(2):
        core = lax.bitwise_xor(place_ref[0], side)
        for step in range(count):
            owner = core * count + lax.bitwise_xor(place_ref[1], step)
            ref = refs[side * count + step]
            scratch[pl.ds(pl.multiple_of(owner * rows, 8), rows), :] = ref[...].astype(F32)
    qkv_ref[0] = scratch[:split, :]
    out_ref[0] = scratch[split:, :]


def grad_join_body(layers, count, n, place_ref, *refs):
    piece_refs = refs[: 2 * count]
    qkv_ref, out_ref, gain_ref, shift_ref, bqv_ref, bout_ref, router_ref, scratch = refs[-8:]
    split, width = qkv_ref.shape[1], bqv_ref.shape[2]
    rows = scratch.shape[0] // (2 * count)
    small = None
    for side in range(2):
        core = lax.bitwise_xor(place_ref[0], side)
        for step in range(count):
            owner = core * count + lax.bitwise_xor(place_ref[1], step)
            both = piece_refs[side * count + step][...].astype(F32)
            scratch[pl.ds(pl.multiple_of(owner * rows, 8), rows), :] = both[:rows]
            small = both[rows:] if small is None else small + both[rows:]
    qkv_ref[0] = scratch[:split, :]
    out_ref[0] = scratch[split:, :]
    one = 8 + router_ref.shape[1]
    for layer in range(layers):
        own = small[layer * one : (layer + 1) * one]
        gain_ref[layer, 0:1, :] = own[0:1]
        gain_ref[layer, 1:2, :] = own[2:3]
        shift_ref[layer, 0:1, :] = own[1:2]
        shift_ref[layer, 1:2, :] = own[3:4]
        bout_ref[layer : layer + 1, :] = own[4:5]
        picked = jnp.zeros((2, width), F32)
        for block in range(n):
            part = own[5:7, block * width : (block + 1) * width]
            picked = picked + jnp.where(place_ref[2] == block, part, 0.0)
        bqv_ref[layer] = picked
        router_ref[layer] = own[8:]


def norm_one_back_body(n, dispatch, me_ref, stream_ref, *refs):
    da1_refs, refs = refs[:n], refs[n:]
    dr_ref, gain_ref, *refs = refs
    if dispatch:
        gate_ref, ids_ref, slot_row_ref, *refs = refs
    gx_ref, *refs = refs
    if dispatch:
        sent_grad_ref, *refs = refs
    (scratch,) = refs
    attn_grad = take_pieces(me_ref, da1_refs, scratch)
    normed, inv_std = norm_parts(load_rows(stream_ref, scratch))
    upstream = dr_ref[...] + norm_back(attn_grad, normed, inv_std, gain_ref[0:1, :])
    if dispatch:
        gx_ref[...] = upstream
    else:
        gx_ref[:, 0, :] = upstream[: gx_ref.shape[0]]
    if dispatch:
        picks = slot_pick_rows(slot_row_ref[...], sent_grad_ref.shape[0])
        chosen = picked_probs(gate_ref[...], ids_ref[...])
        scaled = [(chosen[k] * upstream).astype(BF16) for k in range(2)]
        for at in row_parts(sent_grad_ref.shape[0]):
            rows = dot(picks[0][at], scaled[0]) + dot(picks[1][at], scaled[1])
            sent_grad_ref[at, :] = rows.astype(BF16)


def add_out_body(n, me_ref, base_ref, *refs):
    mix_refs, (out_ref, scratch) = refs[:n], refs[n:]
    total = base_ref[...] + take_pieces(me_ref, mix_refs, scratch)
    out_ref[:, 0, :] = total[: out_ref.shape[0]]


def step_on(rows, step, n):
    return lax.ppermute(rows, "tensor", [(i, (i + step) % n) for i in range(n)])


def add_up(own, arrived):
    total = own.astype(F32)
    for rows in arrived:
        total = total + rows.astype(F32)
    return total.astype(BF16)


def tensor_scatter(pieces):
    return [step_on(pieces[step], step, len(pieces)) for step in range(1, len(pieces))]


def tensor_gather(own, n):
    return [own] + [step_on(own, step, n) for step in range(1, n)]


def tie(first, other):
    flat, tree = jax.tree.flatten((first, other))
    return jax.tree.unflatten(tree, lax.optimization_barrier(tuple(flat)))


def tensor_total(pieces):
    return tensor_gather(add_up(pieces[0], tensor_scatter(pieces)), len(pieces))


def swap(rows, axis, step, size):
    return lax.ppermute(rows, axis, [(i, i ^ step) for i in range(size)])


def group_exchange(rows, groups):
    blocks = rows.reshape(groups, -1, rows.shape[-1])
    moved = lax.all_to_all(blocks, GROUP_AXES, split_axis=0, concat_axis=0, tiled=True)
    return moved.reshape(rows.shape)


def on_device(
    n,
    groups,
    tokens,
    cotangent,
    routes,
    norm_gain,
    norm_bias,
    w_qkv,
    b_qv,
    w_out,
    b_out,
    w_router,
    w_in,
    b_in,
    w_exp_out,
    b_exp_out,
):
    layers = w_qkv.shape[0]
    images, seq_len, model_width = tokens.shape
    real = images * seq_len
    experts = w_router.shape[2]
    capacity = 3 * real // experts
    cap = ceil_to(capacity + 2, 16)
    slots = experts * cap
    local_cols = w_qkv.shape[3]
    heads = local_cols // HEAD_DIM
    hidden = w_in.shape[3]
    chunk = ceil_to(-(-real // n), 8)
    rows = n * chunk
    me = lax.axis_index("tensor").astype(I32).reshape(1)
    place = jnp.stack(
        [lax.axis_index(name) for name in ALL_AXES] + [lax.axis_index(GROUP_AXES)]
    ).astype(I32)

    tokens_in = tokens.reshape(real, model_width)
    cot = cotangent.reshape(real, model_width)
    ids_col = jnp.pad(
        routes.reshape(layers, real, 2), ((0, 0), (0, rows - real), (0, 0)), constant_values=-1
    )
    ids_row = ids_col.transpose(0, 2, 1)
    qkv_weights = w_qkv.transpose(0, 2, 3, 1).reshape(layers, 3 * local_cols, model_width)

    last = layers - 1
    stage = pltpu.VMEM((rows, model_width), F32)
    piece = ((chunk, model_width), BF16)
    high = w_router.astype(BF16)
    rest = w_router - high.astype(F32)
    middle = rest.astype(BF16)
    low = (rest - middle.astype(F32)).astype(BF16)
    router_parts = jnp.concatenate([high, middle, low], 2)

    def norms(layer, near=True):
        wrap = Near if near else Far
        return [wrap(norm_gain, layer), wrap(norm_bias, layer)]

    def attn_weights(layer, near=True):
        wrap = Near if near else Far
        return [wrap(qkv_weights, layer), wrap(b_qv, layer), wrap(w_out, layer)]

    def attn_fwd(layer, base, mix):
        packed = layer == last
        outs = [] if packed else [piece] * n
        outs = outs + ([((rows, model_width), F32, 1)] if mix else [])
        if packed:
            outs.append(((rows * local_cols // LANES, LANES), BF16))
        weights = attn_weights(layer, mix)
        got = kernel_call(
            functools.partial(attn_fwd_body, n, heads, real, bool(mix), packed),
            [me, Far(base), *mix, *norms(layer, mix), *(weights[:2] if packed else weights)],
            outs, [stage], scalars=1, name="attn_fwd",
        )
        at = 0 if packed else n
        return got[-1:] if packed else got[:n], got[at] if mix else base

    def moe_pre(layer, base, proj):
        buffers = [stage]
        if layer == last:
            proj = proj + [Far(w_out, layer)] + [Far(v) for pair in heads_out for v in pair]
            buffers.append(pltpu.VMEM((n - 1, local_cols, model_width), BF16))
        return kernel_call(
            functools.partial(moe_pre_body, n, layer, layer == last),
            [place, Far(base), *proj, b_out, *norms(layer), Far(router_parts, layer),
             Far(slot_row, layer)],
            [
                ((rows, model_width), F32, 1),
                ((rows, model_width), BF16, 1),
                ((rows, experts), F32, 1),
                ((slots, model_width), BF16, PARTS),
            ],
            buffers, scalars=1, name="moe_pre",
        )

    experts_in = w_in.reshape(layers, model_width, hidden)
    experts_out = w_exp_out.reshape(layers, hidden, model_width)

    def full_spec(shape):
        return pl.BlockSpec(shape, lambda i: (0,) * len(shape))

    def whole_spec(array):
        return pl.BlockSpec(array.shape, lambda i: (0,) * array.ndim)

    b_first = b_in.reshape(layers, 1, hidden)
    b_second = b_exp_out.reshape(layers, 1, model_width)

    side = local_cols // 2
    own_side = lax.dynamic_slice_in_dim(w_out[last], place[0] * side, side, 0)

    def far_heads(step):
        mine = step_on(own_side, step, n)
        return [mine, swap(mine, "dp", 1, 2)]

    saved, heads_out = [], [None] * (n - 1)
    stream, mix = tokens_in, ()
    for layer in range(layers):
        pieces, stream = attn_fwd(layer, stream, mix)
        if layer == 0:
            first_arrived = tensor_scatter(pieces)
            own_piece, late_cot = tie(pieces[0], cot)
        slot_col, slot_row, sent_cot = kernel_call(
            functools.partial(slots_body, experts, cap),
            [ids_col, ids_row, Far(late_cot)],
            [((layers, rows, 2), I32), ((layers, 2, rows), I32), ((slots, model_width), BF16, PARTS)],
            [stage], name="slots",
        )
        if layer == last:
            proj = tensor_gather(pieces[0], n)
        elif layer > 0:
            proj = tensor_total(pieces)
        else:
            first_arrived, sent_cot = tie(first_arrived, sent_cot)
            proj = tensor_gather(add_up(own_piece, first_arrived), n)
            cot_arrived = group_exchange(sent_cot, groups)
        got = moe_pre(layer, stream, proj)
        residual, a2, gate, sent = got[:4]
        if layer == 0:
            sent, cot_arrived = tie(sent, cot_arrived)
        if layer < last:
            arrived = group_exchange(sent, groups)
            if layer == last - 1:
                for step in range(1, n, 2):
                    arrived, heads_out[step - 1] = tie(arrived, far_heads(step))
            pre_act, result = kernel_call(
                functools.partial(ffn_fwd_body, 1.0 / n),
                [arrived, Far(experts_in, layer), Far(b_first, layer), Far(experts_out, layer),
                 Far(b_second, layer)],
                [((slots, hidden), BF16, PARTS), ((slots, model_width), BF16, PARTS)],
                name="ffn_fwd",
            )
            returned = group_exchange(result, groups)
            if layer == last - 1:
                for step in range(2, n, 2):
                    returned, heads_out[step - 1] = tie(returned, far_heads(step))
            got = kernel_call(
                functools.partial(combine_body, n),
                [me, returned, Far(gate), Far(ids_col, layer), Far(slot_col, layer)],
                [piece] * n + [((rows, model_width), BF16, 1)] * 2,
                [stage], scalars=1, name="combine",
            )
            mix = tensor_total(got[:n])
            saved.append((stream, residual, a2, gate, arrived, pre_act, got[n:]))
            stream = residual
        else:
            saved.append((stream, residual, a2, gate))

    half = (4 * local_cols) // 2
    chips = groups // 2
    qkv_shape = (layers, 3 * local_cols, model_width)
    out_shape = (layers, local_cols, model_width)

    def expert_grads(layer, ffn_ins, before):
        return block_call(
            ffn_grads_body,
            [pinned(v) for v in ffn_ins] + list(before or ()),
            ffn_outs,
            grid=(1,),
            in_specs=[whole_spec(v) for v in ffn_ins]
            + [pl.BlockSpec(memory_space=pl.ANY)] * (4 if before else 0),
            out_specs=[
                pl.BlockSpec((1,) + shape[1:], lambda i: (layer, 0, 0)) for shape, _ in ffn_outs
            ],
            vmem=28,
            aliases={len(ffn_ins) + i: i for i in range(4)} if before else None,
            name="ffn_grads",
        )

    def widen(given):
        return block_call(
            functools.partial(grad_widen_body, chips),
            [place, *given],
            [(qkv_shape, F32), (out_shape, F32)],
            grid=(1,),
            in_specs=[pl.BlockSpec(memory_space=pltpu.SMEM)]
            + [full_spec((half // chips, model_width))] * (2 * chips),
            out_specs=[
                pl.BlockSpec((1,) + shape[1:], lambda i: (1, 0, 0))
                for shape in (qkv_shape, out_shape)
            ],
            scratch=[pltpu.VMEM((2 * half, model_width), F32)],
            name="grad_widen",
        )

    def add_out():
        (total,) = kernel_call(
            functools.partial(add_out_body, n),
            [me, Far(saved[last][1]), *out_chunks],
            [((real, 1, model_width), F32)], [stage], scalars=1, name="add_out",
        )
        return total

    ffn_outs = [
        ((layers, model_width, hidden), F32),
        ((layers, 1, hidden), F32),
        ((layers, hidden, model_width), F32),
        ((layers, 1, model_width), F32),
    ]
    ffn_grads, wide, small, cuts = None, None, {}, {}
    upstream = cot
    for layer in reversed(range(layers)):
        stream, residual, a2, gate = saved[layer][:4]
        back_ins = [Far(gate), Far(ids_col, layer), Far(slot_col, layer), Far(a2),
                    Far(router_parts, layer)]
        if layer == last:
            arrived = group_exchange(sent, groups)
            result, dx, hid, dpre, grad_arrived = kernel_call(
                functools.partial(ffn_both_body, 1.0 / n, cap),
                [place, Far(router_parts, layer), arrived, cot_arrived, Far(experts_in, layer),
                 Far(b_first, layer), Far(experts_out, layer), Far(b_second, layer)],
                [((slots, model_width), BF16, PARTS)] * 2 + [((slots, hidden), BF16, PARTS)] * 2
                + [((slots, model_width), BF16, PARTS)],
                scalars=1, name="ffn_both",
            )
            dx = group_exchange(dx, groups)
            got = kernel_call(
                functools.partial(moe_back_body, n, cap, True),
                [me, dx, *back_ins],
                [piece] * n + [((experts, model_width), F32)],
                [stage], scalars=1, name="moe_back",
            )
            router_grad = got[n]
            ffn_grads = expert_grads(layer, [arrived, dpre, hid, grad_arrived], None)
        else:
            arrived, pre_act, (y0, y1) = saved[layer][4:]
            grad_arrived, cuts[layer + 1] = tie(
                group_exchange(sent_grad, groups), cuts[layer + 1]
            )
            if layer == last - 1:
                grad_arrived, out_arrived = tie(grad_arrived, tensor_scatter(out_mix))
                out_own = add_up(out_mix[0], out_arrived)
            dx, hid, dpre = kernel_call(
                ffn_back_body,
                [Far(experts_out, layer), Far(pre_act), Far(experts_in, layer), grad_arrived],
                [((slots, model_width), BF16, PARTS)] + [((slots, hidden), BF16, PARTS)] * 2,
                name="ffn_back",
            )
            ffn_grads = expert_grads(layer, [arrived, dpre, hid, grad_arrived], ffn_grads)
            dx, ffn_grads = tie(group_exchange(dx, groups), ffn_grads)
            if layer == last - 1:
                dx, out_chunks = tie(dx, tensor_gather(out_own, n))
            got = kernel_call(
                functools.partial(moe_back_body, n, cap, False),
                [me, dx, *back_ins, Far(upstream), Far(y0), Far(y1)],
                [piece] * n + [((experts, model_width), F32)],
                [stage], scalars=1, name="moe_back",
            )
            router_grad = got[n]
        arrived = tensor_scatter(got[:n])
        if layer < last:
            above = cuts[layer + 1]
            arrived, moved = tie(
                arrived, [swap(above[step], "expert", step, chips) for step in range(1, chips)]
            )
            grad_own = add_up(above[0], moved)
        da2 = tensor_gather(add_up(got[0], arrived), n)
        if layer < last:
            da2, moved = tie(
                da2, [swap(grad_own, "expert", step, chips) for step in range(1, chips)]
            )
            halves = [grad_own] + moved
        if layer == last - 1:
            da2, output = tie(da2, add_out())
        got = kernel_call(
            functools.partial(attn_back_body, n, heads, real),
            [place, Far(residual), *da2, Far(upstream), *norms(layer), *attn_weights(layer),
             Far(stream), router_grad],
            [piece] * n + [
                ((rows, model_width), F32, 1),
                ((half, model_width), BF16, 1),
                ((half, model_width), BF16),
                ((8 + experts, model_width), F32),
            ],
            [stage, pltpu.VMEM((2 * half, model_width), F32)], scalars=1, name="attn_back",
        )
        dr, small[layer] = got[n], got[-1]
        keep, send = got[n + 1 : n + 3]
        if layer < last:
            halves += [swap(rows_of, "dp", 1, 2) for rows_of in halves]
        if layer > 0:
            arrived = tensor_scatter(got[:n])
            if layer == last:
                ffn_grads, arrived = tie(ffn_grads, arrived)
            da1 = tensor_gather(add_up(got[0], arrived), n)
            if layer == last:
                da1, returned = tie(da1, group_exchange(result, groups))
                out_mix = kernel_call(
                    functools.partial(combine_body, n),
                    [me, returned, Far(gate), Far(ids_col, layer), Far(slot_col, layer)],
                    [piece] * n, [stage], scalars=1, name="combine",
                )
            da1, got_half = tie(da1, swap(send, "dp", 1, 2))
            cuts[layer] = kernel_call(
                functools.partial(grad_cut_body, chips),
                [place, Far(keep), got_half],
                [((half // chips, model_width), BF16)] * chips,
                [pltpu.VMEM((half, model_width), F32)], scalars=1, name="grad_cut",
            )
        else:
            smalls = jnp.concatenate([small[at] for at in range(layers)], 0).astype(BF16)
            spare = ceil_to(smalls.shape[0], 16) - smalls.shape[0]
            smalls = jnp.pad(smalls, ((0, spare), (0, 0)))
            cut = kernel_call(
                functools.partial(grad_cut_body, chips),
                [place, Far(keep), swap(send, "dp", 1, 2)],
                [((half // chips, model_width), BF16)] * chips,
                [pltpu.VMEM((half, model_width), F32)], scalars=1, name="grad_cut",
            )
            cut, (smalls, late) = tie(cut, (smalls, list(got[:n])))
            moved = [swap(cut[step], "expert", step, chips) for step in range(1, chips)]
            others = [step_on(smalls, step, n) for step in range(1, n)]
            moved, (others, da1_arrived, wide) = tie(
                moved, (others, tensor_scatter(late), widen(halves))
            )
            (own,) = kernel_call(
                functools.partial(add_beside_body, chips),
                [cut[0], *moved, smalls, *others],
                [((half // chips + smalls.shape[0], model_width), BF16)],
                name="add_beside",
            )
            da1 = tensor_gather(add_up(late[0], da1_arrived), n)
            own_half = [own] + [swap(own, "expert", step, chips) for step in range(1, chips)]
            own_half, da1 = tie(own_half, da1)
            pieces = own_half + [swap(rows_of, "dp", 1, 2) for rows_of in own_half]
        ins = [me, Far(stream), *da1, Far(dr), Near(norm_gain, layer)]
        if layer > 0:
            below = layer - 1
            upstream, sent_grad = kernel_call(
                functools.partial(norm_one_back_body, n, True),
                ins + [Far(saved[below][3]), Far(ids_col, below), Far(slot_row, below)],
                [((rows, model_width), F32, 1), ((slots, model_width), BF16, PARTS)],
                [stage], scalars=1, name="norm_back_send",
            )
        else:
            (grad_tokens,) = kernel_call(
                functools.partial(norm_one_back_body, n, False),
                ins, [((real, 1, model_width), F32)], [stage], scalars=1, name="norm_back",
            )
    g1, gb1, g2, gb2 = ffn_grads

    small_shapes = [
        (layers, 2, model_width),
        (layers, 2, model_width),
        (layers, 2, local_cols),
        (layers, model_width),
        (layers, experts, model_width),
    ]
    given = list(wide or ())
    qkv_grad, out_grad, gain_grad, shift_grad, qv_grad, outb_grad, router_out = block_call(
        functools.partial(grad_join_body, layers, chips, n),
        [place, *pieces, *given],
        [(shape, F32) for shape in (qkv_shape, out_shape, *small_shapes)],
        grid=(1,),
        in_specs=[pl.BlockSpec(memory_space=pltpu.SMEM)]
        + [full_spec(pieces[0].shape)] * (2 * chips)
        + [pl.BlockSpec(memory_space=pl.ANY)] * len(given),
        out_specs=[
            pl.BlockSpec((1,) + shape[1:], lambda i: (0, 0, 0)) for shape in (qkv_shape, out_shape)
        ]
        + [full_spec(shape) for shape in small_shapes],
        scratch=[pltpu.VMEM((2 * half, model_width), F32)],
        vmem=24,
        aliases={1 + 2 * chips + i: i for i in range(len(given))},
        name="grad_join",
    )
    qkv_grad = qkv_grad.reshape(layers, 3, local_cols, model_width).transpose(0, 3, 1, 2)
    return (
        output.reshape(images, seq_len, model_width),
        grad_tokens.reshape(images, seq_len, model_width),
        gain_grad,
        shift_grad,
        qkv_grad,
        qv_grad,
        out_grad,
        outb_grad,
        router_out.transpose(0, 2, 1),
        g1[:, None],
        gb1,
        g2[:, None],
        gb2,
    )


def solution(mesh):
    n = mesh.shape["tensor"]
    groups = mesh.shape["dp"] * mesh.shape["expert"]
    return jax.shard_map(
        functools.partial(on_device, n, groups),
        mesh=mesh,
        in_specs=(
            P(("dp", "expert"), None, None),
            P(("dp", "expert"), None, None),
            P(None, ("dp", "expert"), None, None),
            P(),
            P(),
            P(None, None, None, "tensor"),
            P(None, None, "tensor"),
            P(None, "tensor", None),
            P(),
            P(),
            P(None, ("dp", "expert"), None, "tensor"),
            P(None, ("dp", "expert"), "tensor"),
            P(None, ("dp", "expert"), "tensor", None),
            P(None, ("dp", "expert"), None),
        ),
        out_specs=(
            P(("dp", "expert"), None, None),
            P(("dp", "expert"), None, None),
            P(),
            P(),
            P(None, None, None, "tensor"),
            P(None, None, "tensor"),
            P(None, "tensor", None),
            P(),
            P(),
            P(None, ("dp", "expert"), None, "tensor"),
            P(None, ("dp", "expert"), "tensor"),
            P(None, ("dp", "expert"), "tensor", None),
            P(None, ("dp", "expert"), None),
        ),
        check_vma=False,
    )
```

```python
import functools

import jax
import jax.numpy as jnp
from jax import lax
from jax.experimental import pallas as pl
from jax.experimental.pallas import tpu as pltpu
from jax.sharding import PartitionSpec as P

HEAD_DIM = 64
SCALE = HEAD_DIM ** (-0.5)
LANES = 128
GROUP_AXES = ("dp", "expert")
ALL_AXES = ("dp", "expert", "tensor")

epsilon = 1e-06
root_half = 0.7071067811865476
inv_root_tau = 0.3989422804014327

F32 = jnp.float32
BF16 = jnp.bfloat16
I32 = jnp.int32


def ceil_to(value, step):
    return -(-value // step) * step


def dot(a, b):
    return lax.dot_general(a, b, (((1,), (0,)), ((), ())), preferred_element_type=F32)


def dot_nt(a, b):
    return lax.dot_general(a, b, (((1,), (1,)), ((), ())), preferred_element_type=F32)


def dot_tn(a, b):
    return lax.dot_general(a, b, (((0,), (0,)), ((), ())), preferred_element_type=F32)


def split_two(v):
    high = v.astype(BF16)
    return high, (v - high.astype(F32)).astype(BF16)


class Far:
    def __init__(self, array, index=None):
        self.array, self.index = array, index
        self.shape = array.shape if index is None else array.shape[1:]


class Near:
    def __init__(self, array, index):
        self.array, self.index = array, index


class Fetched:
    def __init__(self, copy, ref):
        self.copy, self.ref, self.shape = copy, ref, ref.shape

    def __getitem__(self, at):
        if self.copy is not None:
            self.copy.wait()
            self.copy = None
        return self.ref[at]


class Kept:
    def __init__(self, ref, far_ref, sems):
        self.ref, self.far_ref, self.sems, self.shape = ref, far_ref, sems, ref.shape
        self.copies = []

    def __setitem__(self, at, value):
        self.ref[at] = value
        pair = self.ref, self.far_ref
        if at is not Ellipsis:
            rows = pl.ds(at[0].start, at[0].stop - at[0].start)
            pair = self.ref.at[rows], self.far_ref.at[rows]
        copy = pltpu.make_async_copy(*pair, self.sems.at[len(self.copies)])
        copy.start()
        self.copies.append(copy)


def kernel_call(body, ins, outs, scratch=(), scalars=0, vmem=16, name=None):
    fars = [i for i, v in enumerate(ins) if isinstance(v, Far)]
    keeps = [i for i, v in enumerate(outs) if len(v) > 2]
    arrays = [
        pltpu.with_memory_space_constraint(v.array, pltpu.HBM)
        if isinstance(v, Far)
        else v.array
        if isinstance(v, Near)
        else v
        for v in ins
    ]
    extra = [pltpu.VMEM(ins[i].shape, ins[i].array.dtype) for i in fars]
    extra += [pltpu.VMEM(outs[i][0], outs[i][1]) for i in keeps]
    extra += [pltpu.SemaphoreType.DMA((1,)) for _ in fars]
    extra += [pltpu.SemaphoreType.DMA((outs[i][2],)) for i in keeps]

    def whole(*refs):
        refs = list(refs)
        own = refs[len(ins) + len(outs) :]
        buffers, sems = own[: len(fars) + len(keeps)], own[len(fars) + len(keeps) :]
        sems, rest = sems[: len(buffers)], sems[len(buffers) :]
        for i, v in enumerate(ins):
            if isinstance(v, Near):
                refs[i] = refs[i].at[v.index]
        for at, i in enumerate(fars):
            source = refs[i] if ins[i].index is None else refs[i].at[ins[i].index]
            copy = pltpu.make_async_copy(source, buffers[at], sems[at].at[0])
            copy.start()
            refs[i] = Fetched(copy, buffers[at])
        for at, i in enumerate(keeps, len(fars)):
            refs[len(ins) + i] = Kept(buffers[at], refs[len(ins) + i], sems[at])
        body(*refs[: len(ins) + len(outs)], *rest)
        for i in fars:
            refs[i][...]
        for i in keeps:
            for copy in refs[len(ins) + i].copies:
                copy.wait()

    def space(i):
        if i < scalars:
            return pltpu.SMEM
        return pltpu.HBM if i in fars else pltpu.VMEM

    return pl.pallas_call(
        whole,
        out_shape=[
            pltpu.HBM(*v[:2]) if len(v) > 2 else jax.ShapeDtypeStruct(*v) for v in outs
        ],
        in_specs=[pl.BlockSpec(memory_space=space(i)) for i in range(len(ins))],
        out_specs=[
            pl.BlockSpec(memory_space=pltpu.HBM if i in keeps else pltpu.VMEM)
            for i in range(len(outs))
        ],
        scratch_shapes=extra + list(scratch),
        compiler_params=pltpu.CompilerParams(vmem_limit_bytes=vmem * 1024 * 1024),
        name=name,
    )(*arrays)


def pinned(array):
    return pltpu.with_memory_space_constraint(array, pltpu.HBM)


def block_call(body, ins, outs, grid, in_specs, out_specs, scratch=(), vmem=16, aliases=None,
               name=None):
    return pl.pallas_call(
        body,
        out_shape=[pltpu.HBM(shape, dtype) for shape, dtype in outs],
        grid=grid,
        in_specs=in_specs,
        out_specs=out_specs,
        scratch_shapes=list(scratch),
        input_output_aliases=aliases or {},
        compiler_params=pltpu.CompilerParams(vmem_limit_bytes=vmem * 1024 * 1024),
        name=name,
    )(*ins)


def load_rows(ref, scratch):
    if ref.shape[0] == scratch.shape[0]:
        return ref[...].astype(F32)
    scratch[...] = jnp.zeros_like(scratch)
    scratch[: ref.shape[0], :] = ref[...].astype(F32)
    return scratch[...]


def norm_parts(stream):
    row_mean = jnp.mean(stream, -1, keepdims=True)
    centered = stream - row_mean
    inv_std = lax.rsqrt(jnp.mean(centered * centered, -1, keepdims=True) + epsilon)
    return centered * inv_std, inv_std


def norm_back(upstream, normed, inv_std, gain_row):
    scaled = upstream * gain_row
    return inv_std * (
        scaled
        - jnp.mean(scaled, -1, keepdims=True)
        - normed * jnp.mean(scaled * normed, -1, keepdims=True)
    )


def head_mask(head, width):
    lane = lax.broadcasted_iota(I32, (1, width), 1)
    return (lane >= head * HEAD_DIM) & (lane < (head + 1) * HEAD_DIM)


def only_head(rows, head):
    return jnp.where(head_mask(head, rows.shape[1]), rows, jnp.zeros_like(rows))


def put_pieces(me_ref, value, scratch, out_refs):
    count = len(out_refs)
    chunk = out_refs[0].shape[0]
    scratch[...] = value
    for step, ref in enumerate(out_refs):
        owner = lax.rem(me_ref[0] + step, count)
        ref[...] = scratch[pl.ds(pl.multiple_of(owner * chunk, 8), chunk), :].astype(BF16)


def take_pieces(me_ref, in_refs, scratch):
    count = len(in_refs)
    chunk = in_refs[0].shape[0]
    for step, ref in enumerate(in_refs):
        owner = lax.rem(me_ref[0] + count - step, count)
        scratch[pl.ds(pl.multiple_of(owner * chunk, 8), chunk), :] = ref[...].astype(F32)
    return scratch[...]


def picked_probs(gate, ids):
    lane = lax.broadcasted_iota(I32, gate.shape, 1)
    return [
        jnp.sum(jnp.where(lane == ids[:, k : k + 1], gate, 0.0), -1, keepdims=True) for k in range(2)
    ]


def slot_pick_rows(slot_row, slots):
    tokens = slot_row.shape[1]
    at = lax.broadcasted_iota(I32, (slots, tokens), 0)
    return [jnp.where(at == slot_row[k : k + 1, :], 1.0, 0.0).astype(BF16) for k in range(2)]


def slot_pick_cols(slot_col, slots):
    tokens = slot_col.shape[0]
    at = lax.broadcasted_iota(I32, (tokens, slots), 1)
    return [jnp.where(at == slot_col[:, k : k + 1], 1.0, 0.0).astype(BF16) for k in range(2)]


def gelu_parts(pre_act):
    half = 0.5 * (1.0 + lax.erf(pre_act * root_half))
    return pre_act * half, half


def gelu_slope(pre_act, half):
    return half + pre_act * jnp.exp(-0.5 * pre_act * pre_act) * inv_root_tau


def slots_body(experts, cap, col_ref, row_ref, cot_ref, slot_col_ref, slot_row_ref, gx_ref, scratch):
    layers, tokens, _ = col_ref.shape
    down = lax.broadcasted_iota(I32, (tokens, tokens), 0)
    across = lax.broadcasted_iota(I32, (tokens, tokens), 1)
    before_col = jnp.where(across < down, 1.0, 0.0).astype(BF16)
    before_row = jnp.where(down < across, 1.0, 0.0).astype(BF16)
    lane = lax.broadcasted_iota(I32, (tokens, experts), 1)
    sub = lax.broadcasted_iota(I32, (experts, tokens), 0)
    for layer in range(layers):
        ids = col_ref[layer]
        one = [jnp.where(lane == ids[:, k : k + 1], 1.0, 0.0) for k in range(2)]
        earlier = dot(before_col, (one[0] + one[1]).astype(BF16))
        for k in range(2):
            at = jnp.sum(earlier * one[k], -1, keepdims=True).astype(I32)
            own = ids[:, k : k + 1]
            slot_col_ref[layer, :, k : k + 1] = jnp.where(own < 0, -1, own * cap + at)
        ids = row_ref[layer]
        one = [jnp.where(sub == ids[k : k + 1, :], 1.0, 0.0) for k in range(2)]
        earlier = dot((one[0] + one[1]).astype(BF16), before_row)
        for k in range(2):
            at = jnp.sum(earlier * one[k], 0, keepdims=True).astype(I32)
            own = ids[k : k + 1, :]
            slot_row_ref[layer, k : k + 1, :] = jnp.where(own < 0, -1, own * cap + at)
    picks = slot_pick_rows(slot_row_ref[layers - 1], gx_ref.shape[0])
    gx_ref[...] = dot(picks[0] + picks[1], load_rows(cot_ref, scratch).astype(BF16)).astype(BF16)


def attend(stream, heads, real, gain_row, shift_row, wqkv_ref, bqv_ref):
    normed, inv_std = norm_parts(stream)
    attn_input = (normed * gain_row + shift_row).astype(BF16)
    width = wqkv_ref.shape[0] // 3
    three = []
    for part in range(3):
        rows = dot_nt(attn_input, wqkv_ref[part * width : (part + 1) * width, :])
        if part != 1:
            rows = rows + bqv_ref[part // 2 : part // 2 + 1, :]
        three.append(rows.astype(BF16))
    query, key, value = three
    tokens = query.shape[0]
    keep = lax.broadcasted_iota(I32, (1, tokens), 1) < real
    mixed = jnp.zeros((tokens, width), F32)
    weights = []
    for head in range(heads):
        scores = dot_nt(only_head(query, head), key) * SCALE
        scores = jnp.where(keep, scores, -1e30)
        row_max = jnp.max(scores, -1, keepdims=True)
        raised = jnp.exp(scores - row_max)
        probs = raised / jnp.sum(raised, -1, keepdims=True)
        weights.append(probs)
        mixed = mixed + dot(probs.astype(BF16), only_head(value, head))
    return normed, attn_input, three, weights, mixed.astype(BF16)


def pack_heads(mixed):
    rows, width = mixed.shape
    full = width - width % LANES
    if full == width:
        return mixed
    left, half = mixed[:, full:].astype(F32), rows // 2
    beside = jnp.concatenate([left[:half], left[half:]], 1).astype(BF16)
    parts = [mixed[:, at : at + LANES] for at in range(0, full, LANES)]
    return jnp.concatenate(parts + [beside], 0)


def unpack_heads(packed, rows, width):
    full = width - width % LANES
    if full == width:
        return packed
    parts = [packed[at * rows : (at + 1) * rows] for at in range(full // LANES)]
    beside = packed[full // LANES * rows :].astype(F32)
    left = jnp.concatenate([beside[:, : LANES // 2], beside[:, LANES // 2 :]], 0)
    return jnp.concatenate(parts + [left.astype(BF16)], 1)


def attn_fwd_body(n, heads, real, from_mix, packed, me_ref, *refs):
    base_ref, *refs = refs
    if from_mix:
        mix_refs, refs = refs[:n], refs[n:]
    gain_ref, shift_ref, wqkv_ref, bqv_ref, *refs = refs
    piece_refs = ()
    if not packed:
        wout_ref, *refs = refs
        piece_refs, refs = refs[:n], refs[n:]
    scratch = refs[-1]
    if from_mix:
        stream = take_pieces(me_ref, mix_refs, scratch) + base_ref[...]
        refs[0][...] = stream
    else:
        stream = load_rows(base_ref, scratch)
    mixed = attend(
        stream, heads, real, gain_ref[0:1, :], shift_ref[0:1, :], wqkv_ref, bqv_ref
    )[-1]
    if not piece_refs:
        packed_ref, scratch = refs[-2:]
        packed_ref[...] = pack_heads(mixed)
    else:
        put_pieces(me_ref, dot(mixed, wout_ref[...]), scratch, piece_refs)


def moe_pre_body(n, layer, packed, place_ref, base_ref, *refs):
    me_ref = place_ref.at[pl.ds(2, 1)]
    proj_refs, refs = refs[:n], refs[n:]
    if packed:
        wout_ref, *side_refs = refs[: 2 * n - 1]
        refs = refs[2 * n - 1 :]
    outb_ref, gain_ref, shift_ref, router_ref, slot_row_ref, *refs = refs
    resid_ref, a2_ref, gate_ref, sent_ref, scratch, *refs = refs
    if packed:
        (sides,) = refs
    residual = load_rows(base_ref, scratch)
    if packed:
        width = wout_ref.shape[0]
        for step, mixed_ref in enumerate(proj_refs):
            mixed = unpack_heads(mixed_ref[...], residual.shape[0], width)
            if step > 0:
                wout_ref = sides.at[step - 1]
                for side in range(2):
                    low = lax.bitwise_xor(place_ref[0], side) * (width // 2)
                    at = pl.ds(pl.multiple_of(low, 16), width // 2)
                    wout_ref[at, :] = side_refs[2 * step - 2 + side][...]
            residual = residual + dot(mixed, wout_ref[...])
    else:
        residual = residual + take_pieces(me_ref, proj_refs, scratch)
    residual = residual + outb_ref[layer : layer + 1, :]
    resid_ref[...] = residual
    normed, _ = norm_parts(residual)
    moe_input = (normed * gain_ref[1:2, :] + shift_ref[1:2, :]).astype(BF16)
    a2_ref[...] = moe_input
    gate = gate_of(moe_input, router_ref[...])
    gate_ref[...] = gate
    picks = slot_pick_rows(slot_row_ref[...], sent_ref.shape[0])
    picks = picks[0] + picks[1]
    for at in row_parts(sent_ref.shape[0]):
        sent_ref[at, :] = dot(picks[at], moe_input).astype(BF16)


def gate_of(rows, router_parts):
    parts = dot(rows, router_parts)
    experts = parts.shape[1] // 3
    logits = parts[:, :experts] + (
        parts[:, experts : 2 * experts] + parts[:, 2 * experts :]
    )
    raised = jnp.exp(logits - jnp.max(logits, -1, keepdims=True))
    return raised / jnp.sum(raised, -1, keepdims=True)


PARTS = 2


def row_parts(rows):
    step = rows // PARTS
    return [slice(at, at + step) for at in range(0, rows, step)]


def ffn_fwd_body(share, x_ref, w1_ref, b1_ref, w2_ref, b2_ref, pre_ref, out_ref):
    bias = b2_ref[...] * share
    for at in row_parts(out_ref.shape[0]):
        pre_act = dot(x_ref[at, :], w1_ref[...]) + b1_ref[...]
        pre_ref[at, :] = pre_act.astype(BF16)
        hidden, _ = gelu_parts(pre_act)
        out_ref[at, :] = (dot(hidden.astype(BF16), w2_ref[...]) + bias).astype(BF16)


def ffn_back_body(w2_ref, pre_ref, w1_ref, dy_ref, dx_ref, hid_ref, dpre_ref):
    for at in row_parts(dx_ref.shape[0]):
        dhidden = dot_nt(dy_ref[at, :], w2_ref[...])
        pre_act = pre_ref[at, :].astype(F32)
        hidden, half = gelu_parts(pre_act)
        hid_ref[at, :] = hidden.astype(BF16)
        dpre = (dhidden * gelu_slope(pre_act, half)).astype(BF16)
        dpre_ref[at, :] = dpre
        dx_ref[at, :] = dot_nt(dpre, w1_ref[...]).astype(BF16)


def ffn_both_body(
    share, cap, place_ref, router_ref, x_ref, gx_ref, w1_ref, b1_ref, w2_ref, b2_ref,
    out_ref, dx_ref, hid_ref, dpre_ref, dy_ref,
):
    bias = b2_ref[...] * share
    width = x_ref.shape[1]
    below = lax.broadcasted_iota(I32, (cap, LANES), 0) == lax.broadcasted_iota(I32, (cap, LANES), 1)
    at_row = lax.broadcasted_iota(I32, (cap, 1), 0)
    for at in row_parts(x_ref.shape[0]):
        x = x_ref[at, :]
        pre_act = dot(x, w1_ref[...]) + b1_ref[...]
        gate = gate_of(x, router_ref[...])
        lane = lax.broadcasted_iota(I32, gate.shape, 1)
        chosen = jnp.sum(jnp.where(lane == place_ref[3], gate, 0.0), -1, keepdims=True)
        upstream = gx_ref[at, :].astype(F32)
        dy = (chosen * upstream).astype(BF16)
        dy_ref[at, :] = dy
        hidden, half = gelu_parts(pre_act)
        hidden = hidden.astype(BF16)
        hid_ref[at, :] = hidden
        result = (dot(hidden, w2_ref[...]) + bias).astype(BF16)
        out_ref[at, :] = result
        choice = jnp.sum(upstream * result.astype(F32), -1, keepdims=True)
        dpre = (dot_nt(dy, w2_ref[...]) * gelu_slope(pre_act, half)).astype(BF16)
        dpre_ref[at, :] = dpre
        dx = dot_nt(dpre, w1_ref[...])
        blocks = []
        for low in range(0, at.stop - at.start, cap):
            row = jnp.sum(jnp.where(below, choice[low : low + cap], 0.0), 0, keepdims=True)
            row = jnp.concatenate([row, jnp.zeros((1, width - LANES), F32)], 1)
            high = row.astype(BF16).astype(F32)
            block = jnp.where(at_row == cap - 2, high, dx[low : low + cap])
            blocks.append(jnp.where(at_row == cap - 1, row - high, block))
        dx_ref[at, :] = jnp.concatenate(blocks, 0).astype(BF16)


def ffn_grads_body(x_ref, dpre_ref, hid_ref, dy_ref, *refs):
    g1_ref, gb1_ref, g2_ref, gb2_ref = refs[-4:]
    g1_ref[0] = dot_tn(x_ref[...], dpre_ref[...])
    gb1_ref[0] = jnp.sum(dpre_ref[...].astype(F32), 0, keepdims=True)
    g2_ref[0] = dot_tn(hid_ref[...], dy_ref[...])
    gb2_ref[0] = jnp.sum(dy_ref[...].astype(F32), 0, keepdims=True)


def combine_body(n, me_ref, ret_ref, slot_col_ref, gate_ref, ids_ref, *refs):
    piece_refs, refs = refs[:n], refs[n:]
    scratch = refs[-1]
    picks = slot_pick_cols(slot_col_ref[...], ret_ref.shape[0])
    chosen = picked_probs(gate_ref[...], ids_ref[...])
    y0 = dot(picks[0], ret_ref[...])
    y1 = dot(picks[1], ret_ref[...])
    for ref, rows in zip(refs[:-1], (y0, y1)):
        ref[...] = rows.astype(BF16)
    put_pieces(me_ref, chosen[0] * y0 + chosen[1] * y1, scratch, piece_refs)


def router_back(choices, gate, ids, moe_input, router, grad_ref):
    lane = lax.broadcasted_iota(I32, gate.shape, 1)
    prob_grad = jnp.zeros_like(gate)
    for k in range(2):
        prob_grad = prob_grad + jnp.where(lane == ids[:, k : k + 1], choices[k], 0.0)
    logit_grad = gate * (prob_grad - jnp.sum(prob_grad * gate, -1, keepdims=True))
    high, low = split_two(logit_grad)
    grad_ref[...] = dot_tn(high, moe_input) + dot_tn(low, moe_input)
    experts = gate.shape[1]
    w_high, w_low = router[:, :experts], router[:, experts : 2 * experts]
    return dot_nt(high, w_high) + (dot_nt(high, w_low) + dot_nt(low, w_high))


def moe_back_body(
    n, cap, fresh, me_ref, dx_ref, slot_col_ref, gate_ref, ids_ref, a2_ref, router_ref, *refs
):
    scratch = refs[-1]
    dx = dx_ref[...]
    slot_col = slot_col_ref[...]
    picks = slot_pick_cols(slot_col, dx.shape[0])
    grad = dot(picks[0] + picks[1], dx)
    gate, ids = gate_ref[...], ids_ref[...]
    if fresh:
        lane = lax.broadcasted_iota(I32, gate.shape, 1)
        spot = lax.broadcasted_iota(I32, (gate.shape[0], LANES), 1)
        ends = range(cap, dx.shape[0] + 1, cap)
        sides = [
            jnp.concatenate([dx[end - row : end - row + 1, :LANES] for end in ends], 0)
            for row in (2, 1)
        ]
        choices = []
        for k in range(2):
            own = jnp.where(lane == ids[:, k : k + 1], 1.0, 0.0).astype(BF16)
            values = dot(own, sides[0]) + dot(own, sides[1])
            here = spot == slot_col[:, k : k + 1] - ids[:, k : k + 1] * cap
            choices.append(jnp.sum(jnp.where(here, values, 0.0), -1, keepdims=True))
    else:
        up_ref, y0_ref, y1_ref, *refs = refs
        upstream = load_rows(up_ref, scratch)
        choices = [
            jnp.sum(upstream * ref[...].astype(F32), -1, keepdims=True) for ref in (y0_ref, y1_ref)
        ]
    piece_refs, (grad_ref, scratch) = refs[:n], refs[n:]
    grad = grad + router_back(choices, gate, ids, a2_ref[...], router_ref[...], grad_ref)
    put_pieces(me_ref, grad, scratch, piece_refs)


def attn_back_body(n, heads, real, place_ref, stream_ref, resid_ref, *refs):
    da2_refs, refs = refs[:n], refs[n:]
    up_ref, gain_ref, shift_ref, wqkv_ref, bqv_ref, wout_ref, router_ref, *refs = refs
    piece_refs, refs = refs[:n], refs[n:]
    dr_ref, keep_ref, send_ref, all_ref, scratch, grad_scratch = refs
    me_ref = place_ref.at[pl.ds(2, 1)]
    normed, attn_input, (query, key, value), weights, mixed = attend(
        load_rows(stream_ref, scratch), heads, real, gain_ref[0:1, :], shift_ref[0:1, :],
        wqkv_ref, bqv_ref,
    )
    upstream = load_rows(up_ref, scratch)
    moe_grad = take_pieces(me_ref, da2_refs, scratch)
    normed_two, inv_std = norm_parts(resid_ref[...])
    share = 1.0 / n
    all_ref[2:3, :] = jnp.sum(moe_grad * normed_two, 0, keepdims=True) * share
    all_ref[3:4, :] = jnp.sum(moe_grad, 0, keepdims=True) * share
    resid_grad = upstream + norm_back(moe_grad, normed_two, inv_std, gain_ref[1:2, :])
    dr_ref[...] = resid_grad
    all_ref[4:5, :] = jnp.sum(resid_grad, 0, keepdims=True) * share
    proj_grad = resid_grad.astype(BF16)
    mixed_grad = dot_nt(proj_grad, wout_ref[...]).astype(BF16)
    width = wout_ref.shape[0]
    dquery = jnp.zeros(query.shape, F32)
    dkey = jnp.zeros(query.shape, F32)
    dvalue = jnp.zeros(query.shape, F32)
    for head in range(heads):
        probs = weights[head]
        own = only_head(mixed_grad, head)
        dvalue = dvalue + dot_tn(probs.astype(BF16), own)
        dot_grad = dot_nt(own, value)
        score_grad = (
            probs * (dot_grad - jnp.sum(dot_grad * probs, -1, keepdims=True))
        ).astype(BF16)
        dquery = dquery + dot(score_grad, only_head(key, head))
        dkey = dkey + dot_tn(score_grad, only_head(query, head))
    attn_grad = None
    three = []
    for part, rows in enumerate((dquery * SCALE, dkey * SCALE, dvalue)):
        three.append(rows.astype(BF16))
        term = dot(three[part], wqkv_ref[part * width : (part + 1) * width, :])
        attn_grad = term if attn_grad is None else attn_grad + term
    put_pieces(me_ref, attn_grad, scratch, piece_refs)
    all_ref[0:1, :] = jnp.sum(attn_grad * normed, 0, keepdims=True)
    all_ref[1:2, :] = jnp.sum(attn_grad, 0, keepdims=True)
    all_ref[5:8, :] = jnp.zeros((3, all_ref.shape[1]), F32)
    for row, part in enumerate((0, 2)):
        sums = jnp.sum(three[part].astype(F32), 0, keepdims=True)
        for block in range(n):
            own = jnp.where(place_ref[2] == block, sums, 0.0)
            all_ref[5 + row : 6 + row, block * width : (block + 1) * width] = own
    all_ref[8:, :] = router_ref[...]
    core = place_ref[0]
    pairs = [(three[part], attn_input) for part in range(3)] + [(mixed, proj_grad)]
    for at, (left, right) in enumerate(pairs):
        low = at % 2 * width
        grad_scratch[at // 2, low : low + width, :] = dot_tn(left, right).astype(BF16)
    keep_ref[...] = grad_scratch[core]
    send_ref[...] = grad_scratch[1 - core]


def grad_cut_body(count, place_ref, keep_ref, got_ref, *refs):
    piece_refs, scratch = refs[:count], refs[count]
    rows = piece_refs[0].shape[0]
    scratch[...] = keep_ref[...].astype(F32) + got_ref[...].astype(F32)
    for step, ref in enumerate(piece_refs):
        owner = lax.bitwise_xor(place_ref[1], step)
        ref[...] = scratch[pl.ds(pl.multiple_of(owner * rows, 8), rows), :].astype(BF16)


def add_beside_body(own_count, *refs):
    refs, out_ref = refs[:-1], refs[-1]
    sums = []
    for part in (refs[:own_count], refs[own_count:]):
        total = part[0][...].astype(F32)
        for ref in part[1:]:
            total = total + ref[...].astype(F32)
        sums.append(total)
    out_ref[...] = jnp.concatenate(sums, 0).astype(BF16)


def grad_widen_body(count, place_ref, *refs):
    qkv_ref, out_ref, scratch = refs[-3:]
    rows, split = refs[0].shape[0], qkv_ref.shape[1]
    for side in range(2):
        core = lax.bitwise_xor(place_ref[0], side)
        for step in range(count):
            owner = core * count + lax.bitwise_xor(place_ref[1], step)
            ref = refs[side * count + step]
            scratch[pl.ds(pl.multiple_of(owner * rows, 8), rows), :] = ref[...].astype(F32)
    qkv_ref[0] = scratch[:split, :]
    out_ref[0] = scratch[split:, :]


def grad_join_body(layers, count, n, place_ref, *refs):
    piece_refs = refs[: 2 * count]
    qkv_ref, out_ref, gain_ref, shift_ref, bqv_ref, bout_ref, router_ref, scratch = refs[-8:]
    split, width = qkv_ref.shape[1], bqv_ref.shape[2]
    rows = scratch.shape[0] // (2 * count)
    small = None
    for side in range(2):
        core = lax.bitwise_xor(place_ref[0], side)
        for step in range(count):
            owner = core * count + lax.bitwise_xor(place_ref[1], step)
            both = piece_refs[side * count + step][...].astype(F32)
            scratch[pl.ds(pl.multiple_of(owner * rows, 8), rows), :] = both[:rows]
            small = both[rows:] if small is None else small + both[rows:]
    qkv_ref[0] = scratch[:split, :]
    out_ref[0] = scratch[split:, :]
    one = 8 + router_ref.shape[1]
    for layer in range(layers):
        own = small[layer * one : (layer + 1) * one]
        gain_ref[layer, 0:1, :] = own[0:1]
        gain_ref[layer, 1:2, :] = own[2:3]
        shift_ref[layer, 0:1, :] = own[1:2]
        shift_ref[layer, 1:2, :] = own[3:4]
        bout_ref[layer : layer + 1, :] = own[4:5]
        picked = jnp.zeros((2, width), F32)
        for block in range(n):
            part = own[5:7, block * width : (block + 1) * width]
            picked = picked + jnp.where(place_ref[2] == block, part, 0.0)
        bqv_ref[layer] = picked
        router_ref[layer] = own[8:]


def norm_one_back_body(n, dispatch, me_ref, stream_ref, *refs):
    da1_refs, refs = refs[:n], refs[n:]
    dr_ref, gain_ref, *refs = refs
    if dispatch:
        gate_ref, ids_ref, slot_row_ref, *refs = refs
    gx_ref, *refs = refs
    if dispatch:
        sent_grad_ref, *refs = refs
    (scratch,) = refs
    attn_grad = take_pieces(me_ref, da1_refs, scratch)
    normed, inv_std = norm_parts(load_rows(stream_ref, scratch))
    upstream = dr_ref[...] + norm_back(attn_grad, normed, inv_std, gain_ref[0:1, :])
    if dispatch:
        gx_ref[...] = upstream
    else:
        gx_ref[:, 0, :] = upstream[: gx_ref.shape[0]]
    if dispatch:
        picks = slot_pick_rows(slot_row_ref[...], sent_grad_ref.shape[0])
        chosen = picked_probs(gate_ref[...], ids_ref[...])
        scaled = [(chosen[k] * upstream).astype(BF16) for k in range(2)]
        for at in row_parts(sent_grad_ref.shape[0]):
            rows = dot(picks[0][at], scaled[0]) + dot(picks[1][at], scaled[1])
            sent_grad_ref[at, :] = rows.astype(BF16)


def add_out_body(n, me_ref, base_ref, *refs):
    mix_refs, (out_ref, scratch) = refs[:n], refs[n:]
    total = base_ref[...] + take_pieces(me_ref, mix_refs, scratch)
    out_ref[:, 0, :] = total[: out_ref.shape[0]]


def step_on(rows, step, n):
    return lax.ppermute(rows, "tensor", [(i, (i + step) % n) for i in range(n)])


def add_up(own, arrived):
    total = own.astype(F32)
    for rows in arrived:
        total = total + rows.astype(F32)
    return total.astype(BF16)


def tensor_scatter(pieces):
    return [step_on(pieces[step], step, len(pieces)) for step in range(1, len(pieces))]


def tensor_gather(own, n):
    return [own] + [step_on(own, step, n) for step in range(1, n)]


def tie(first, other):
    flat, tree = jax.tree.flatten((first, other))
    return jax.tree.unflatten(tree, lax.optimization_barrier(tuple(flat)))


def tensor_total(pieces):
    return tensor_gather(add_up(pieces[0], tensor_scatter(pieces)), len(pieces))


def swap(rows, axis, step, size):
    return lax.ppermute(rows, axis, [(i, i ^ step) for i in range(size)])


def group_exchange(rows, groups):
    blocks = rows.reshape(groups, -1, rows.shape[-1])
    moved = lax.all_to_all(blocks, GROUP_AXES, split_axis=0, concat_axis=0, tiled=True)
    return moved.reshape(rows.shape)


def on_device(
    n,
    groups,
    tokens,
    cotangent,
    routes,
    norm_gain,
    norm_bias,
    w_qkv,
    b_qv,
    w_out,
    b_out,
    w_router,
    w_in,
    b_in,
    w_exp_out,
    b_exp_out,
):
    layers = w_qkv.shape[0]
    images, seq_len, model_width = tokens.shape
    real = images * seq_len
    experts = w_router.shape[2]
    capacity = 3 * real // experts
    cap = ceil_to(capacity + 2, 16)
    slots = experts * cap
    local_cols = w_qkv.shape[3]
    heads = local_cols // HEAD_DIM
    hidden = w_in.shape[3]
    chunk = ceil_to(-(-real // n), 8)
    rows = n * chunk
    me = lax.axis_index("tensor").astype(I32).reshape(1)
    place = jnp.stack(
        [lax.axis_index(name) for name in ALL_AXES] + [lax.axis_index(GROUP_AXES)]
    ).astype(I32)

    tokens_in = tokens.reshape(real, model_width)
    cot = cotangent.reshape(real, model_width)
    ids_col = jnp.pad(
        routes.reshape(layers, real, 2), ((0, 0), (0, rows - real), (0, 0)), constant_values=-1
    )
    ids_row = ids_col.transpose(0, 2, 1)
    qkv_weights = w_qkv.transpose(0, 2, 3, 1).reshape(layers, 3 * local_cols, model_width)

    last = layers - 1
    stage = pltpu.VMEM((rows, model_width), F32)
    piece = ((chunk, model_width), BF16)
    high = w_router.astype(BF16)
    rest = w_router - high.astype(F32)
    middle = rest.astype(BF16)
    low = (rest - middle.astype(F32)).astype(BF16)
    router_parts = jnp.concatenate([high, middle, low], 2)

    def norms(layer, near=True):
        wrap = Near if near else Far
        return [wrap(norm_gain, layer), wrap(norm_bias, layer)]

    def attn_weights(layer, near=True):
        wrap = Near if near else Far
        return [wrap(qkv_weights, layer), wrap(b_qv, layer), wrap(w_out, layer)]

    def attn_fwd(layer, base, mix):
        packed = layer == last
        outs = [] if packed else [piece] * n
        outs = outs + ([((rows, model_width), F32, 1)] if mix else [])
        if packed:
            outs.append(((rows * local_cols // LANES, LANES), BF16))
        weights = attn_weights(layer, mix)
        got = kernel_call(
            functools.partial(attn_fwd_body, n, heads, real, bool(mix), packed),
            [me, Far(base), *mix, *norms(layer, mix), *(weights[:2] if packed else weights)],
            outs, [stage], scalars=1, name="attn_fwd",
        )
        at = 0 if packed else n
        return got[-1:] if packed else got[:n], got[at] if mix else base

    def moe_pre(layer, base, proj):
        buffers = [stage]
        if layer == last:
            proj = proj + [Far(w_out, layer)] + [v for pair in heads_out for v in pair]
            buffers.append(pltpu.VMEM((n - 1, local_cols, model_width), BF16))
        return kernel_call(
            functools.partial(moe_pre_body, n, layer, layer == last),
            [place, Far(base), *proj, b_out, *norms(layer), Far(router_parts, layer),
             Far(slot_row, layer)],
            [
                ((rows, model_width), F32, 1),
                ((rows, model_width), BF16, 1),
                ((rows, experts), F32, 1),
                ((slots, model_width), BF16, PARTS),
            ],
            buffers, scalars=1, name="moe_pre",
        )

    experts_in = w_in.reshape(layers, model_width, hidden)
    experts_out = w_exp_out.reshape(layers, hidden, model_width)

    def full_spec(shape):
        return pl.BlockSpec(shape, lambda i: (0,) * len(shape))

    def whole_spec(array):
        return pl.BlockSpec(array.shape, lambda i: (0,) * array.ndim)

    b_first = b_in.reshape(layers, 1, hidden)
    b_second = b_exp_out.reshape(layers, 1, model_width)

    side = local_cols // 2
    own_side = lax.dynamic_slice_in_dim(w_out[last], place[0] * side, side, 0)

    def far_heads(step):
        mine = step_on(own_side, step, n)
        return [mine, swap(mine, "dp", 1, 2)]

    saved, heads_out = [], [None] * (n - 1)
    stream, mix = tokens_in, ()
    for layer in range(layers):
        pieces, stream = attn_fwd(layer, stream, mix)
        if layer == 0:
            first_arrived = tensor_scatter(pieces)
            own_piece, late_cot = tie(pieces[0], cot)
        slot_col, slot_row, sent_cot = kernel_call(
            functools.partial(slots_body, experts, cap),
            [ids_col, ids_row, Far(late_cot)],
            [((layers, rows, 2), I32), ((layers, 2, rows), I32), ((slots, model_width), BF16, PARTS)],
            [stage], name="slots",
        )
        if layer == last:
            proj = tensor_gather(pieces[0], n)
        elif layer > 0:
            proj = tensor_total(pieces)
        else:
            first_arrived, sent_cot = tie(first_arrived, sent_cot)
            proj = tensor_gather(add_up(own_piece, first_arrived), n)
            cot_arrived = group_exchange(sent_cot, groups)
        got = moe_pre(layer, stream, proj)
        residual, a2, gate, sent = got[:4]
        if layer == 0:
            sent, cot_arrived = tie(sent, cot_arrived)
        if layer < last:
            arrived = group_exchange(sent, groups)
            if layer == last - 1:
                for step in range(1, n, 2):
                    arrived, heads_out[step - 1] = tie(arrived, far_heads(step))
            pre_act, result = kernel_call(
                functools.partial(ffn_fwd_body, 1.0 / n),
                [arrived, Far(experts_in, layer), Far(b_first, layer), Far(experts_out, layer),
                 Far(b_second, layer)],
                [((slots, hidden), BF16, PARTS), ((slots, model_width), BF16, PARTS)],
                name="ffn_fwd",
            )
            returned = group_exchange(result, groups)
            if layer == last - 1:
                for step in range(2, n, 2):
                    returned, heads_out[step - 1] = tie(returned, far_heads(step))
            got = kernel_call(
                functools.partial(combine_body, n),
                [me, returned, Far(slot_col, layer), Far(gate), Far(ids_col, layer)],
                [piece] * n + [((rows, model_width), BF16, 1)] * 2,
                [stage], scalars=1, name="combine",
            )
            mix = tensor_total(got[:n])
            saved.append((stream, residual, a2, gate, arrived, pre_act, got[n:]))
            stream = residual
        else:
            saved.append((stream, residual, a2, gate))

    half = (4 * local_cols) // 2
    chips = groups // 2
    qkv_shape = (layers, 3 * local_cols, model_width)
    out_shape = (layers, local_cols, model_width)

    def expert_grads(layer, ffn_ins, before):
        return block_call(
            ffn_grads_body,
            [pinned(v) for v in ffn_ins] + list(before or ()),
            ffn_outs,
            grid=(1,),
            in_specs=[whole_spec(v) for v in ffn_ins]
            + [pl.BlockSpec(memory_space=pl.ANY)] * (4 if before else 0),
            out_specs=[
                pl.BlockSpec((1,) + shape[1:], lambda i: (layer, 0, 0)) for shape, _ in ffn_outs
            ],
            vmem=28,
            aliases={len(ffn_ins) + i: i for i in range(4)} if before else None,
            name="ffn_grads",
        )

    def widen(given):
        return block_call(
            functools.partial(grad_widen_body, chips),
            [place, *given],
            [(qkv_shape, F32), (out_shape, F32)],
            grid=(1,),
            in_specs=[pl.BlockSpec(memory_space=pltpu.SMEM)]
            + [full_spec((half // chips, model_width))] * (2 * chips),
            out_specs=[
                pl.BlockSpec((1,) + shape[1:], lambda i: (1, 0, 0))
                for shape in (qkv_shape, out_shape)
            ],
            scratch=[pltpu.VMEM((2 * half, model_width), F32)],
            name="grad_widen",
        )

    def add_out():
        (total,) = kernel_call(
            functools.partial(add_out_body, n),
            [me, Far(saved[last][1]), *out_chunks],
            [((real, 1, model_width), F32)], [stage], scalars=1, name="add_out",
        )
        return total

    ffn_outs = [
        ((layers, model_width, hidden), F32),
        ((layers, 1, hidden), F32),
        ((layers, hidden, model_width), F32),
        ((layers, 1, model_width), F32),
    ]
    ffn_grads, wide, small, cuts = None, None, {}, {}
    upstream = cot
    for layer in reversed(range(layers)):
        stream, residual, a2, gate = saved[layer][:4]
        back_ins = [Far(slot_col, layer), Far(gate), Far(ids_col, layer), Far(a2),
                    Far(router_parts, layer)]
        if layer == last:
            arrived = group_exchange(sent, groups)
            result, dx, hid, dpre, grad_arrived = kernel_call(
                functools.partial(ffn_both_body, 1.0 / n, cap),
                [place, Far(router_parts, layer), arrived, cot_arrived, Far(experts_in, layer),
                 Far(b_first, layer), Far(experts_out, layer), Far(b_second, layer)],
                [((slots, model_width), BF16, PARTS)] * 2 + [((slots, hidden), BF16, PARTS)] * 2
                + [((slots, model_width), BF16, PARTS)],
                scalars=1, name="ffn_both",
            )
            dx = group_exchange(dx, groups)
            got = kernel_call(
                functools.partial(moe_back_body, n, cap, True),
                [me, dx, *back_ins],
                [piece] * n + [((experts, model_width), F32)],
                [stage], scalars=1, name="moe_back",
            )
            router_grad = got[n]
            ffn_grads = expert_grads(layer, [arrived, dpre, hid, grad_arrived], None)
        else:
            arrived, pre_act, (y0, y1) = saved[layer][4:]
            grad_arrived, cuts[layer + 1] = tie(
                group_exchange(sent_grad, groups), cuts[layer + 1]
            )
            if layer == last - 1:
                grad_arrived, out_arrived = tie(grad_arrived, tensor_scatter(out_mix))
                out_own = add_up(out_mix[0], out_arrived)
            dx, hid, dpre = kernel_call(
                ffn_back_body,
                [Far(experts_out, layer), Far(pre_act), Far(experts_in, layer), grad_arrived],
                [((slots, model_width), BF16, PARTS)] + [((slots, hidden), BF16, PARTS)] * 2,
                name="ffn_back",
            )
            ffn_grads = expert_grads(layer, [arrived, dpre, hid, grad_arrived], ffn_grads)
            dx = group_exchange(dx, groups)
            if layer == last - 1:
                dx, out_chunks = tie(dx, tensor_gather(out_own, n))
            got = kernel_call(
                functools.partial(moe_back_body, n, cap, False),
                [me, dx, *back_ins, Far(upstream), Far(y0), Far(y1)],
                [piece] * n + [((experts, model_width), F32)],
                [stage], scalars=1, name="moe_back",
            )
            router_grad = got[n]
        arrived = tensor_scatter(got[:n])
        if layer < last:
            above = cuts[layer + 1]
            ffn_grads, arrived = tie(ffn_grads, arrived)
            arrived, moved = tie(
                arrived, [swap(above[step], "expert", step, chips) for step in range(1, chips)]
            )
            grad_own = add_up(above[0], moved)
        da2 = tensor_gather(add_up(got[0], arrived), n)
        if layer < last:
            da2, moved = tie(
                da2, [swap(grad_own, "expert", step, chips) for step in range(1, chips)]
            )
            halves = [grad_own] + moved
        if layer == last - 1:
            da2, output = tie(da2, add_out())
        got = kernel_call(
            functools.partial(attn_back_body, n, heads, real),
            [place, Far(stream), Far(residual), *da2, Far(upstream), *norms(layer),
             *attn_weights(layer), router_grad],
            [piece] * n + [
                ((rows, model_width), F32, 1),
                ((half, model_width), BF16, 1),
                ((half, model_width), BF16),
                ((8 + experts, model_width), F32),
            ],
            [stage, pltpu.VMEM((2, half, model_width), BF16)], scalars=1, name="attn_back",
        )
        dr, small[layer] = got[n], got[-1]
        keep, send = got[n + 1 : n + 3]
        if layer < last:
            halves += [swap(rows_of, "dp", 1, 2) for rows_of in halves]
        if layer > 0:
            arrived = tensor_scatter(got[:n])
            if layer == last:
                ffn_grads, arrived = tie(ffn_grads, arrived)
            da1 = tensor_gather(add_up(got[0], arrived), n)
            if layer == last:
                da1, returned = tie(da1, group_exchange(result, groups))
                out_mix = kernel_call(
                    functools.partial(combine_body, n),
                    [me, returned, Far(slot_col, layer), Far(gate), Far(ids_col, layer)],
                    [piece] * n, [stage], scalars=1, name="combine",
                )
            da1, got_half = tie(da1, swap(send, "dp", 1, 2))
            cuts[layer] = kernel_call(
                functools.partial(grad_cut_body, chips),
                [place, Far(keep), got_half],
                [((half // chips, model_width), BF16)] * chips,
                [pltpu.VMEM((half, model_width), F32)], scalars=1, name="grad_cut",
            )
        else:
            smalls = jnp.concatenate([small[at] for at in range(layers)], 0).astype(BF16)
            spare = ceil_to(smalls.shape[0], 16) - smalls.shape[0]
            smalls = jnp.pad(smalls, ((0, spare), (0, 0)))
            cut = kernel_call(
                functools.partial(grad_cut_body, chips),
                [place, Far(keep), swap(send, "dp", 1, 2)],
                [((half // chips, model_width), BF16)] * chips,
                [pltpu.VMEM((half, model_width), F32)], scalars=1, name="grad_cut",
            )
            cut, (smalls, late) = tie(cut, (smalls, list(got[:n])))
            moved = [swap(cut[step], "expert", step, chips) for step in range(1, chips)]
            others = [step_on(smalls, step, n) for step in range(1, n)]
            moved, (others, da1_arrived, wide) = tie(
                moved, (others, tensor_scatter(late), widen(halves))
            )
            (own,) = kernel_call(
                functools.partial(add_beside_body, chips),
                [cut[0], *moved, smalls, *others],
                [((half // chips + smalls.shape[0], model_width), BF16)],
                name="add_beside",
            )
            da1 = tensor_gather(add_up(late[0], da1_arrived), n)
            own_half = [own] + [swap(own, "expert", step, chips) for step in range(1, chips)]
            own_half, da1 = tie(own_half, da1)
            pieces = own_half + [swap(rows_of, "dp", 1, 2) for rows_of in own_half]
        ins = [me, Far(stream), *da1, Far(dr), Near(norm_gain, layer)]
        if layer > 0:
            below = layer - 1
            upstream, sent_grad = kernel_call(
                functools.partial(norm_one_back_body, n, True),
                ins + [Far(saved[below][3]), Far(ids_col, below), Far(slot_row, below)],
                [((rows, model_width), F32, 1), ((slots, model_width), BF16, PARTS)],
                [stage], scalars=1, name="norm_back_send",
            )
        else:
            (grad_tokens,) = kernel_call(
                functools.partial(norm_one_back_body, n, False),
                ins, [((real, 1, model_width), F32)], [stage], scalars=1, name="norm_back",
            )
    g1, gb1, g2, gb2 = ffn_grads

    small_shapes = [
        (layers, 2, model_width),
        (layers, 2, model_width),
        (layers, 2, local_cols),
        (layers, model_width),
        (layers, experts, model_width),
    ]
    given = list(wide or ())
    qkv_grad, out_grad, gain_grad, shift_grad, qv_grad, outb_grad, router_out = block_call(
        functools.partial(grad_join_body, layers, chips, n),
        [place, *pieces, *given],
        [(shape, F32) for shape in (qkv_shape, out_shape, *small_shapes)],
        grid=(1,),
        in_specs=[pl.BlockSpec(memory_space=pltpu.SMEM)]
        + [full_spec(pieces[0].shape)] * (2 * chips)
        + [pl.BlockSpec(memory_space=pl.ANY)] * len(given),
        out_specs=[
            pl.BlockSpec((1,) + shape[1:], lambda i: (0, 0, 0)) for shape in (qkv_shape, out_shape)
        ]
        + [full_spec(shape) for shape in small_shapes],
        scratch=[pltpu.VMEM((2 * half, model_width), F32)],
        vmem=24,
        aliases={1 + 2 * chips + i: i for i in range(len(given))},
        name="grad_join",
    )
    qkv_grad = qkv_grad.reshape(layers, 3, local_cols, model_width).transpose(0, 3, 1, 2)
    return (
        output.reshape(images, seq_len, model_width),
        grad_tokens.reshape(images, seq_len, model_width),
        gain_grad,
        shift_grad,
        qkv_grad,
        qv_grad,
        out_grad,
        outb_grad,
        router_out.transpose(0, 2, 1),
        g1[:, None],
        gb1,
        g2[:, None],
        gb2,
    )


def solution(mesh):
    n = mesh.shape["tensor"]
    groups = mesh.shape["dp"] * mesh.shape["expert"]
    return jax.shard_map(
        functools.partial(on_device, n, groups),
        mesh=mesh,
        in_specs=(
            P(("dp", "expert"), None, None),
            P(("dp", "expert"), None, None),
            P(None, ("dp", "expert"), None, None),
            P(),
            P(),
            P(None, None, None, "tensor"),
            P(None, None, "tensor"),
            P(None, "tensor", None),
            P(),
            P(),
            P(None, ("dp", "expert"), None, "tensor"),
            P(None, ("dp", "expert"), "tensor"),
            P(None, ("dp", "expert"), "tensor", None),
            P(None, ("dp", "expert"), None),
        ),
        out_specs=(
            P(("dp", "expert"), None, None),
            P(("dp", "expert"), None, None),
            P(),
            P(),
            P(None, None, None, "tensor"),
            P(None, None, "tensor"),
            P(None, "tensor", None),
            P(),
            P(),
            P(None, ("dp", "expert"), None, "tensor"),
            P(None, ("dp", "expert"), "tensor"),
            P(None, ("dp", "expert"), "tensor", None),
            P(None, ("dp", "expert"), None),
        ),
        check_vma=False,
    )
```

```python
import functools

import jax
import jax.numpy as jnp
from jax import lax
from jax.experimental import pallas as pl
from jax.experimental.pallas import tpu as pltpu
from jax.sharding import PartitionSpec as P

HEAD_DIM = 64
SCALE = HEAD_DIM ** (-0.5)
LANES = 128
GROUP_AXES = ("dp", "expert")
ALL_AXES = ("dp", "expert", "tensor")

epsilon = 1e-06
root_half = 0.7071067811865476
inv_root_tau = 0.3989422804014327

F32 = jnp.float32
BF16 = jnp.bfloat16
I32 = jnp.int32


def ceil_to(value, step):
    return -(-value // step) * step


def dot(a, b):
    return lax.dot_general(a, b, (((1,), (0,)), ((), ())), preferred_element_type=F32)


def dot_nt(a, b):
    return lax.dot_general(a, b, (((1,), (1,)), ((), ())), preferred_element_type=F32)


def dot_tn(a, b):
    return lax.dot_general(a, b, (((0,), (0,)), ((), ())), preferred_element_type=F32)


def split_two(v):
    high = v.astype(BF16)
    return high, (v - high.astype(F32)).astype(BF16)


class Far:
    def __init__(self, array, index=None):
        self.array, self.index = array, index
        self.shape = array.shape if index is None else array.shape[1:]


class Near:
    def __init__(self, array, index):
        self.array, self.index = array, index


class Fetched:
    def __init__(self, copy, ref):
        self.copy, self.ref, self.shape = copy, ref, ref.shape

    def __getitem__(self, at):
        if self.copy is not None:
            self.copy.wait()
            self.copy = None
        return self.ref[at]


class Kept:
    def __init__(self, ref, far_ref, sems):
        self.ref, self.far_ref, self.sems, self.shape = ref, far_ref, sems, ref.shape
        self.copies = []

    def __setitem__(self, at, value):
        self.ref[at] = value
        pair = self.ref, self.far_ref
        if at is not Ellipsis:
            rows = pl.ds(at[0].start, at[0].stop - at[0].start)
            pair = self.ref.at[rows], self.far_ref.at[rows]
        copy = pltpu.make_async_copy(*pair, self.sems.at[len(self.copies)])
        copy.start()
        self.copies.append(copy)


def kernel_call(body, ins, outs, scratch=(), scalars=0, vmem=16, name=None):
    fars = [i for i, v in enumerate(ins) if isinstance(v, Far)]
    keeps = [i for i, v in enumerate(outs) if len(v) > 2]
    arrays = [
        pltpu.with_memory_space_constraint(v.array, pltpu.HBM)
        if isinstance(v, Far)
        else v.array
        if isinstance(v, Near)
        else v
        for v in ins
    ]
    extra = [pltpu.VMEM(ins[i].shape, ins[i].array.dtype) for i in fars]
    extra += [pltpu.VMEM(outs[i][0], outs[i][1]) for i in keeps]
    extra += [pltpu.SemaphoreType.DMA((1,)) for _ in fars]
    extra += [pltpu.SemaphoreType.DMA((outs[i][2],)) for i in keeps]

    def whole(*refs):
        refs = list(refs)
        own = refs[len(ins) + len(outs) :]
        buffers, sems = own[: len(fars) + len(keeps)], own[len(fars) + len(keeps) :]
        sems, rest = sems[: len(buffers)], sems[len(buffers) :]
        for i, v in enumerate(ins):
            if isinstance(v, Near):
                refs[i] = refs[i].at[v.index]
        for at, i in enumerate(fars):
            source = refs[i] if ins[i].index is None else refs[i].at[ins[i].index]
            copy = pltpu.make_async_copy(source, buffers[at], sems[at].at[0])
            copy.start()
            refs[i] = Fetched(copy, buffers[at])
        for at, i in enumerate(keeps, len(fars)):
            refs[len(ins) + i] = Kept(buffers[at], refs[len(ins) + i], sems[at])
        body(*refs[: len(ins) + len(outs)], *rest)
        for i in fars:
            refs[i][...]
        for i in keeps:
            for copy in refs[len(ins) + i].copies:
                copy.wait()

    def space(i):
        if i < scalars:
            return pltpu.SMEM
        return pltpu.HBM if i in fars else pltpu.VMEM

    return pl.pallas_call(
        whole,
        out_shape=[
            pltpu.HBM(*v[:2]) if len(v) > 2 else jax.ShapeDtypeStruct(*v) for v in outs
        ],
        in_specs=[pl.BlockSpec(memory_space=space(i)) for i in range(len(ins))],
        out_specs=[
            pl.BlockSpec(memory_space=pltpu.HBM if i in keeps else pltpu.VMEM)
            for i in range(len(outs))
        ],
        scratch_shapes=extra + list(scratch),
        compiler_params=pltpu.CompilerParams(vmem_limit_bytes=vmem * 1024 * 1024),
        name=name,
    )(*arrays)


def pinned(array):
    return pltpu.with_memory_space_constraint(array, pltpu.HBM)


def block_call(body, ins, outs, grid, in_specs, out_specs, scratch=(), vmem=16, aliases=None,
               name=None):
    return pl.pallas_call(
        body,
        out_shape=[pltpu.HBM(shape, dtype) for shape, dtype in outs],
        grid=grid,
        in_specs=in_specs,
        out_specs=out_specs,
        scratch_shapes=list(scratch),
        input_output_aliases=aliases or {},
        compiler_params=pltpu.CompilerParams(vmem_limit_bytes=vmem * 1024 * 1024),
        name=name,
    )(*ins)


def load_rows(ref, scratch):
    if ref.shape[0] == scratch.shape[0]:
        return ref[...].astype(F32)
    scratch[...] = jnp.zeros_like(scratch)
    scratch[: ref.shape[0], :] = ref[...].astype(F32)
    return scratch[...]


def norm_parts(stream):
    row_mean = jnp.mean(stream, -1, keepdims=True)
    centered = stream - row_mean
    inv_std = lax.rsqrt(jnp.mean(centered * centered, -1, keepdims=True) + epsilon)
    return centered * inv_std, inv_std


def norm_back(upstream, normed, inv_std, gain_row):
    scaled = upstream * gain_row
    return inv_std * (
        scaled
        - jnp.mean(scaled, -1, keepdims=True)
        - normed * jnp.mean(scaled * normed, -1, keepdims=True)
    )


def head_mask(head, width):
    lane = lax.broadcasted_iota(I32, (1, width), 1)
    return (lane >= head * HEAD_DIM) & (lane < (head + 1) * HEAD_DIM)


def only_head(rows, head):
    return jnp.where(head_mask(head, rows.shape[1]), rows, jnp.zeros_like(rows))


def put_pieces(me_ref, value, scratch, out_refs):
    count = len(out_refs)
    chunk = out_refs[0].shape[0]
    scratch[...] = value
    for step, ref in enumerate(out_refs):
        owner = lax.rem(me_ref[0] + step, count)
        ref[...] = scratch[pl.ds(pl.multiple_of(owner * chunk, 8), chunk), :].astype(BF16)


def take_pieces(me_ref, in_refs, scratch):
    count = len(in_refs)
    chunk = in_refs[0].shape[0]
    for step, ref in enumerate(in_refs):
        owner = lax.rem(me_ref[0] + count - step, count)
        scratch[pl.ds(pl.multiple_of(owner * chunk, 8), chunk), :] = ref[...].astype(F32)
    return scratch[...]


def picked_probs(gate, ids):
    lane = lax.broadcasted_iota(I32, gate.shape, 1)
    return [
        jnp.sum(jnp.where(lane == ids[:, k : k + 1], gate, 0.0), -1, keepdims=True) for k in range(2)
    ]


def slot_pick_rows(slot_row, slots):
    tokens = slot_row.shape[1]
    at = lax.broadcasted_iota(I32, (slots, tokens), 0)
    return [jnp.where(at == slot_row[k : k + 1, :], 1.0, 0.0).astype(BF16) for k in range(2)]


def slot_pick_cols(slot_col, slots):
    tokens = slot_col.shape[0]
    at = lax.broadcasted_iota(I32, (tokens, slots), 1)
    return [jnp.where(at == slot_col[:, k : k + 1], 1.0, 0.0).astype(BF16) for k in range(2)]


def gelu_parts(pre_act):
    half = 0.5 * (1.0 + lax.erf(pre_act * root_half))
    return pre_act * half, half


def gelu_slope(pre_act, half):
    return half + pre_act * jnp.exp(-0.5 * pre_act * pre_act) * inv_root_tau


def slots_body(experts, cap, col_ref, row_ref, cot_ref, slot_col_ref, slot_row_ref, gx_ref, scratch):
    layers, tokens, _ = col_ref.shape
    down = lax.broadcasted_iota(I32, (tokens, tokens), 0)
    across = lax.broadcasted_iota(I32, (tokens, tokens), 1)
    before_col = jnp.where(across < down, 1.0, 0.0).astype(BF16)
    before_row = jnp.where(down < across, 1.0, 0.0).astype(BF16)
    lane = lax.broadcasted_iota(I32, (tokens, experts), 1)
    sub = lax.broadcasted_iota(I32, (experts, tokens), 0)
    for layer in range(layers):
        ids = col_ref[layer]
        one = [jnp.where(lane == ids[:, k : k + 1], 1.0, 0.0) for k in range(2)]
        earlier = dot(before_col, (one[0] + one[1]).astype(BF16))
        for k in range(2):
            at = jnp.sum(earlier * one[k], -1, keepdims=True).astype(I32)
            own = ids[:, k : k + 1]
            slot_col_ref[layer, :, k : k + 1] = jnp.where(own < 0, -1, own * cap + at)
        ids = row_ref[layer]
        one = [jnp.where(sub == ids[k : k + 1, :], 1.0, 0.0) for k in range(2)]
        earlier = dot((one[0] + one[1]).astype(BF16), before_row)
        for k in range(2):
            at = jnp.sum(earlier * one[k], 0, keepdims=True).astype(I32)
            own = ids[k : k + 1, :]
            slot_row_ref[layer, k : k + 1, :] = jnp.where(own < 0, -1, own * cap + at)
    picks = slot_pick_rows(slot_row_ref[layers - 1], gx_ref.shape[0])
    gx_ref[...] = dot(picks[0] + picks[1], load_rows(cot_ref, scratch).astype(BF16)).astype(BF16)


def attend(stream, heads, real, gain_row, shift_row, wqkv_ref, bqv_ref):
    normed, inv_std = norm_parts(stream)
    attn_input = (normed * gain_row + shift_row).astype(BF16)
    width = wqkv_ref.shape[0] // 3
    three = []
    for part in range(3):
        rows = dot_nt(attn_input, wqkv_ref[part * width : (part + 1) * width, :])
        if part != 1:
            rows = rows + bqv_ref[part // 2 : part // 2 + 1, :]
        three.append(rows.astype(BF16))
    query, key, value = three
    tokens = query.shape[0]
    keep = lax.broadcasted_iota(I32, (1, tokens), 1) < real
    mixed = jnp.zeros((tokens, width), F32)
    weights = []
    for head in range(heads):
        scores = dot_nt(only_head(query, head), key) * SCALE
        scores = jnp.where(keep, scores, -1e30)
        row_max = jnp.max(scores, -1, keepdims=True)
        raised = jnp.exp(scores - row_max)
        probs = raised / jnp.sum(raised, -1, keepdims=True)
        weights.append(probs)
        mixed = mixed + dot(probs.astype(BF16), only_head(value, head))
    return normed, attn_input, three, weights, mixed.astype(BF16)


def pack_heads(mixed):
    rows, width = mixed.shape
    full = width - width % LANES
    if full == width:
        return mixed
    left, half = mixed[:, full:].astype(F32), rows // 2
    beside = jnp.concatenate([left[:half], left[half:]], 1).astype(BF16)
    parts = [mixed[:, at : at + LANES] for at in range(0, full, LANES)]
    return jnp.concatenate(parts + [beside], 0)


def unpack_heads(packed, rows, width):
    full = width - width % LANES
    if full == width:
        return packed
    parts = [packed[at * rows : (at + 1) * rows] for at in range(full // LANES)]
    beside = packed[full // LANES * rows :].astype(F32)
    left = jnp.concatenate([beside[:, : LANES // 2], beside[:, LANES // 2 :]], 0)
    return jnp.concatenate(parts + [left.astype(BF16)], 1)


def attn_fwd_body(n, heads, real, from_mix, packed, me_ref, *refs):
    base_ref, *refs = refs
    if from_mix:
        mix_refs, refs = refs[:n], refs[n:]
    gain_ref, shift_ref, wqkv_ref, bqv_ref, *refs = refs
    piece_refs = ()
    if not packed:
        wout_ref, *refs = refs
        piece_refs, refs = refs[:n], refs[n:]
    scratch = refs[-1]
    if from_mix:
        stream = take_pieces(me_ref, mix_refs, scratch) + base_ref[...]
        refs[0][...] = stream
    else:
        stream = load_rows(base_ref, scratch)
    mixed = attend(
        stream, heads, real, gain_ref[0:1, :], shift_ref[0:1, :], wqkv_ref, bqv_ref
    )[-1]
    if not piece_refs:
        packed_ref, scratch = refs[-2:]
        packed_ref[...] = pack_heads(mixed)
    else:
        put_pieces(me_ref, dot(mixed, wout_ref[...]), scratch, piece_refs)


def moe_pre_body(n, layer, packed, place_ref, base_ref, *refs):
    me_ref = place_ref.at[pl.ds(2, 1)]
    proj_refs, refs = refs[:n], refs[n:]
    if packed:
        wout_ref, *side_refs = refs[: 2 * n - 1]
        refs = refs[2 * n - 1 :]
    outb_ref, gain_ref, shift_ref, router_ref, slot_row_ref, *refs = refs
    resid_ref, a2_ref, gate_ref, sent_ref, scratch, *refs = refs
    if packed:
        (sides,) = refs
    residual = load_rows(base_ref, scratch)
    if packed:
        width = wout_ref.shape[0]
        for step, mixed_ref in enumerate(proj_refs):
            mixed = unpack_heads(mixed_ref[...], residual.shape[0], width)
            if step > 0:
                wout_ref = sides.at[step - 1]
                for side in range(2):
                    low = lax.bitwise_xor(place_ref[0], side) * (width // 2)
                    at = pl.ds(pl.multiple_of(low, 16), width // 2)
                    wout_ref[at, :] = side_refs[2 * step - 2 + side][...]
            residual = residual + dot(mixed, wout_ref[...])
    else:
        residual = residual + take_pieces(me_ref, proj_refs, scratch)
    residual = residual + outb_ref[layer : layer + 1, :]
    resid_ref[...] = residual
    normed, _ = norm_parts(residual)
    moe_input = (normed * gain_ref[1:2, :] + shift_ref[1:2, :]).astype(BF16)
    a2_ref[...] = moe_input
    gate = gate_of(moe_input, router_ref[...])
    gate_ref[...] = gate
    picks = slot_pick_rows(slot_row_ref[...], sent_ref.shape[0])
    picks = picks[0] + picks[1]
    for at in row_parts(sent_ref.shape[0]):
        sent_ref[at, :] = dot(picks[at], moe_input).astype(BF16)


def gate_of(rows, router_parts):
    parts = dot(rows, router_parts)
    experts = parts.shape[1] // 3
    logits = parts[:, :experts] + (
        parts[:, experts : 2 * experts] + parts[:, 2 * experts :]
    )
    raised = jnp.exp(logits - jnp.max(logits, -1, keepdims=True))
    return raised / jnp.sum(raised, -1, keepdims=True)


PARTS = 2


def row_parts(rows):
    step = rows // PARTS
    return [slice(at, at + step) for at in range(0, rows, step)]


def ffn_fwd_body(share, x_ref, w1_ref, b1_ref, w2_ref, b2_ref, pre_ref, out_ref):
    bias = b2_ref[...] * share
    for at in row_parts(out_ref.shape[0]):
        pre_act = dot(x_ref[at, :], w1_ref[...]) + b1_ref[...]
        pre_ref[at, :] = pre_act.astype(BF16)
        hidden, _ = gelu_parts(pre_act)
        out_ref[at, :] = (dot(hidden.astype(BF16), w2_ref[...]) + bias).astype(BF16)


def ffn_back_body(w2_ref, pre_ref, w1_ref, dy_ref, dx_ref, hid_ref, dpre_ref):
    for at in row_parts(dx_ref.shape[0]):
        dhidden = dot_nt(dy_ref[at, :], w2_ref[...])
        pre_act = pre_ref[at, :].astype(F32)
        hidden, half = gelu_parts(pre_act)
        hid_ref[at, :] = hidden.astype(BF16)
        dpre = (dhidden * gelu_slope(pre_act, half)).astype(BF16)
        dpre_ref[at, :] = dpre
        dx_ref[at, :] = dot_nt(dpre, w1_ref[...]).astype(BF16)


def ffn_both_body(
    share, cap, place_ref, router_ref, x_ref, gx_ref, w1_ref, b1_ref, w2_ref, b2_ref,
    out_ref, dx_ref, hid_ref, dpre_ref, dy_ref,
):
    bias = b2_ref[...] * share
    width = x_ref.shape[1]
    below = lax.broadcasted_iota(I32, (cap, LANES), 0) == lax.broadcasted_iota(I32, (cap, LANES), 1)
    at_row = lax.broadcasted_iota(I32, (cap, 1), 0)
    for at in row_parts(x_ref.shape[0]):
        x = x_ref[at, :]
        pre_act = dot(x, w1_ref[...]) + b1_ref[...]
        gate = gate_of(x, router_ref[...])
        lane = lax.broadcasted_iota(I32, gate.shape, 1)
        chosen = jnp.sum(jnp.where(lane == place_ref[3], gate, 0.0), -1, keepdims=True)
        upstream = gx_ref[at, :].astype(F32)
        dy = (chosen * upstream).astype(BF16)
        dy_ref[at, :] = dy
        hidden, half = gelu_parts(pre_act)
        hidden = hidden.astype(BF16)
        hid_ref[at, :] = hidden
        result = (dot(hidden, w2_ref[...]) + bias).astype(BF16)
        out_ref[at, :] = result
        choice = jnp.sum(upstream * result.astype(F32), -1, keepdims=True)
        dpre = (dot_nt(dy, w2_ref[...]) * gelu_slope(pre_act, half)).astype(BF16)
        dpre_ref[at, :] = dpre
        dx = dot_nt(dpre, w1_ref[...])
        blocks = []
        for low in range(0, at.stop - at.start, cap):
            row = jnp.sum(jnp.where(below, choice[low : low + cap], 0.0), 0, keepdims=True)
            row = jnp.concatenate([row, jnp.zeros((1, width - LANES), F32)], 1)
            high = row.astype(BF16).astype(F32)
            block = jnp.where(at_row == cap - 2, high, dx[low : low + cap])
            blocks.append(jnp.where(at_row == cap - 1, row - high, block))
        dx_ref[at, :] = jnp.concatenate(blocks, 0).astype(BF16)


def ffn_grads_body(x_ref, dpre_ref, hid_ref, dy_ref, *refs):
    g1_ref, gb1_ref, g2_ref, gb2_ref = refs[-4:]
    g1_ref[0] = dot_tn(x_ref[...], dpre_ref[...])
    gb1_ref[0] = jnp.sum(dpre_ref[...].astype(F32), 0, keepdims=True)
    g2_ref[0] = dot_tn(hid_ref[...], dy_ref[...])
    gb2_ref[0] = jnp.sum(dy_ref[...].astype(F32), 0, keepdims=True)


def combine_body(n, me_ref, ret_ref, slot_col_ref, gate_ref, ids_ref, *refs):
    piece_refs, refs = refs[:n], refs[n:]
    scratch = refs[-1]
    picks = slot_pick_cols(slot_col_ref[...], ret_ref.shape[0])
    chosen = picked_probs(gate_ref[...], ids_ref[...])
    y0 = dot(picks[0], ret_ref[...])
    y1 = dot(picks[1], ret_ref[...])
    for ref, rows in zip(refs[:-1], (y0, y1)):
        ref[...] = rows.astype(BF16)
    put_pieces(me_ref, chosen[0] * y0 + chosen[1] * y1, scratch, piece_refs)


def router_back(choices, gate, ids, moe_input, router, grad_ref):
    lane = lax.broadcasted_iota(I32, gate.shape, 1)
    prob_grad = jnp.zeros_like(gate)
    for k in range(2):
        prob_grad = prob_grad + jnp.where(lane == ids[:, k : k + 1], choices[k], 0.0)
    logit_grad = gate * (prob_grad - jnp.sum(prob_grad * gate, -1, keepdims=True))
    high, low = split_two(logit_grad)
    grad_ref[...] = dot_tn(high, moe_input) + dot_tn(low, moe_input)
    experts = gate.shape[1]
    w_high, w_low = router[:, :experts], router[:, experts : 2 * experts]
    return dot_nt(high, w_high) + (dot_nt(high, w_low) + dot_nt(low, w_high))


def moe_back_body(
    n, cap, fresh, me_ref, dx_ref, slot_col_ref, gate_ref, ids_ref, a2_ref, router_ref, *refs
):
    scratch = refs[-1]
    dx = dx_ref[...]
    slot_col = slot_col_ref[...]
    picks = slot_pick_cols(slot_col, dx.shape[0])
    grad = dot(picks[0] + picks[1], dx)
    gate, ids = gate_ref[...], ids_ref[...]
    if fresh:
        lane = lax.broadcasted_iota(I32, gate.shape, 1)
        spot = lax.broadcasted_iota(I32, (gate.shape[0], LANES), 1)
        ends = range(cap, dx.shape[0] + 1, cap)
        sides = [
            jnp.concatenate([dx[end - row : end - row + 1, :LANES] for end in ends], 0)
            for row in (2, 1)
        ]
        choices = []
        for k in range(2):
            own = jnp.where(lane == ids[:, k : k + 1], 1.0, 0.0).astype(BF16)
            values = dot(own, sides[0]) + dot(own, sides[1])
            here = spot == slot_col[:, k : k + 1] - ids[:, k : k + 1] * cap
            choices.append(jnp.sum(jnp.where(here, values, 0.0), -1, keepdims=True))
    else:
        up_ref, y0_ref, y1_ref, *refs = refs
        upstream = load_rows(up_ref, scratch)
        choices = [
            jnp.sum(upstream * ref[...].astype(F32), -1, keepdims=True) for ref in (y0_ref, y1_ref)
        ]
    piece_refs, (grad_ref, scratch) = refs[:n], refs[n:]
    grad = grad + router_back(choices, gate, ids, a2_ref[...], router_ref[...], grad_ref)
    put_pieces(me_ref, grad, scratch, piece_refs)


def attn_back_body(n, heads, real, place_ref, stream_ref, resid_ref, *refs):
    da2_refs, refs = refs[:n], refs[n:]
    up_ref, gain_ref, shift_ref, wqkv_ref, bqv_ref, wout_ref, router_ref, *refs = refs
    piece_refs, refs = refs[:n], refs[n:]
    dr_ref, keep_ref, send_ref, all_ref, scratch, grad_scratch = refs
    me_ref = place_ref.at[pl.ds(2, 1)]
    normed, attn_input, (query, key, value), weights, mixed = attend(
        load_rows(stream_ref, scratch), heads, real, gain_ref[0:1, :], shift_ref[0:1, :],
        wqkv_ref, bqv_ref,
    )
    upstream = load_rows(up_ref, scratch)
    moe_grad = take_pieces(me_ref, da2_refs, scratch)
    normed_two, inv_std = norm_parts(resid_ref[...])
    share = 1.0 / n
    all_ref[2:3, :] = jnp.sum(moe_grad * normed_two, 0, keepdims=True) * share
    all_ref[3:4, :] = jnp.sum(moe_grad, 0, keepdims=True) * share
    resid_grad = upstream + norm_back(moe_grad, normed_two, inv_std, gain_ref[1:2, :])
    dr_ref[...] = resid_grad
    all_ref[4:5, :] = jnp.sum(resid_grad, 0, keepdims=True) * share
    proj_grad = resid_grad.astype(BF16)
    mixed_grad = dot_nt(proj_grad, wout_ref[...]).astype(BF16)
    width = wout_ref.shape[0]
    dquery = jnp.zeros(query.shape, F32)
    dkey = jnp.zeros(query.shape, F32)
    dvalue = jnp.zeros(query.shape, F32)
    for head in range(heads):
        probs = weights[head]
        own = only_head(mixed_grad, head)
        dvalue = dvalue + dot_tn(probs.astype(BF16), own)
        dot_grad = dot_nt(own, value)
        score_grad = (
            probs * (dot_grad - jnp.sum(dot_grad * probs, -1, keepdims=True))
        ).astype(BF16)
        dquery = dquery + dot(score_grad, only_head(key, head))
        dkey = dkey + dot_tn(score_grad, only_head(query, head))
    attn_grad = None
    three = []
    for part, rows in enumerate((dquery * SCALE, dkey * SCALE, dvalue)):
        three.append(rows.astype(BF16))
        term = dot(three[part], wqkv_ref[part * width : (part + 1) * width, :])
        attn_grad = term if attn_grad is None else attn_grad + term
    put_pieces(me_ref, attn_grad, scratch, piece_refs)
    all_ref[0:1, :] = jnp.sum(attn_grad * normed, 0, keepdims=True)
    all_ref[1:2, :] = jnp.sum(attn_grad, 0, keepdims=True)
    all_ref[5:8, :] = jnp.zeros((3, all_ref.shape[1]), F32)
    for row, part in enumerate((0, 2)):
        sums = jnp.sum(three[part].astype(F32), 0, keepdims=True)
        for block in range(n):
            own = jnp.where(place_ref[2] == block, sums, 0.0)
            all_ref[5 + row : 6 + row, block * width : (block + 1) * width] = own
    all_ref[8:, :] = router_ref[...]
    core = place_ref[0]
    pairs = [(three[part], attn_input) for part in range(3)] + [(mixed, proj_grad)]
    for at, (left, right) in enumerate(pairs):
        low = at % 2 * width
        grad_scratch[at // 2, low : low + width, :] = dot_tn(left, right).astype(BF16)
    keep_ref[...] = grad_scratch[core]
    send_ref[...] = grad_scratch[1 - core]


def grad_cut_body(count, place_ref, keep_ref, got_ref, *refs):
    piece_refs, scratch = refs[:count], refs[count]
    rows = piece_refs[0].shape[0]
    scratch[...] = keep_ref[...].astype(F32) + got_ref[...].astype(F32)
    for step, ref in enumerate(piece_refs):
        owner = lax.bitwise_xor(place_ref[1], step)
        ref[...] = scratch[pl.ds(pl.multiple_of(owner * rows, 8), rows), :].astype(BF16)


def add_beside_body(own_count, *refs):
    refs, out_ref = refs[:-1], refs[-1]
    sums = []
    for part in (refs[:own_count], refs[own_count:]):
        total = part[0][...].astype(F32)
        for ref in part[1:]:
            total = total + ref[...].astype(F32)
        sums.append(total)
    out_ref[...] = jnp.concatenate(sums, 0).astype(BF16)


def grad_widen_body(count, place_ref, *refs):
    qkv_ref, out_ref, scratch = refs[-3:]
    rows, split = refs[0].shape[0], qkv_ref.shape[1]
    for side in range(2):
        core = lax.bitwise_xor(place_ref[0], side)
        for step in range(count):
            owner = core * count + lax.bitwise_xor(place_ref[1], step)
            ref = refs[side * count + step]
            scratch[pl.ds(pl.multiple_of(owner * rows, 8), rows), :] = ref[...].astype(F32)
    qkv_ref[0] = scratch[:split, :]
    out_ref[0] = scratch[split:, :]


def grad_join_body(layers, count, n, place_ref, *refs):
    piece_refs = refs[: 2 * count]
    qkv_ref, out_ref, gain_ref, shift_ref, bqv_ref, bout_ref, router_ref, scratch = refs[-8:]
    split, width = qkv_ref.shape[1], bqv_ref.shape[2]
    rows = scratch.shape[0] // (2 * count)
    small = None
    for side in range(2):
        core = lax.bitwise_xor(place_ref[0], side)
        for step in range(count):
            owner = core * count + lax.bitwise_xor(place_ref[1], step)
            both = piece_refs[side * count + step][...].astype(F32)
            scratch[pl.ds(pl.multiple_of(owner * rows, 8), rows), :] = both[:rows]
            small = both[rows:] if small is None else small + both[rows:]
    qkv_ref[0] = scratch[:split, :]
    out_ref[0] = scratch[split:, :]
    one = 8 + router_ref.shape[1]
    for layer in range(layers):
        own = small[layer * one : (layer + 1) * one]
        gain_ref[layer, 0:1, :] = own[0:1]
        gain_ref[layer, 1:2, :] = own[2:3]
        shift_ref[layer, 0:1, :] = own[1:2]
        shift_ref[layer, 1:2, :] = own[3:4]
        bout_ref[layer : layer + 1, :] = own[4:5]
        picked = jnp.zeros((2, width), F32)
        for block in range(n):
            part = own[5:7, block * width : (block + 1) * width]
            picked = picked + jnp.where(place_ref[2] == block, part, 0.0)
        bqv_ref[layer] = picked
        router_ref[layer] = own[8:]


def norm_one_back_body(n, dispatch, me_ref, stream_ref, *refs):
    da1_refs, refs = refs[:n], refs[n:]
    dr_ref, gain_ref, *refs = refs
    if dispatch:
        gate_ref, ids_ref, slot_row_ref, *refs = refs
    gx_ref, *refs = refs
    if dispatch:
        sent_grad_ref, *refs = refs
    (scratch,) = refs
    attn_grad = take_pieces(me_ref, da1_refs, scratch)
    normed, inv_std = norm_parts(load_rows(stream_ref, scratch))
    upstream = dr_ref[...] + norm_back(attn_grad, normed, inv_std, gain_ref[0:1, :])
    if dispatch:
        gx_ref[...] = upstream
    else:
        gx_ref[:, 0, :] = upstream[: gx_ref.shape[0]]
    if dispatch:
        picks = slot_pick_rows(slot_row_ref[...], sent_grad_ref.shape[0])
        chosen = picked_probs(gate_ref[...], ids_ref[...])
        scaled = [(chosen[k] * upstream).astype(BF16) for k in range(2)]
        for at in row_parts(sent_grad_ref.shape[0]):
            rows = dot(picks[0][at], scaled[0]) + dot(picks[1][at], scaled[1])
            sent_grad_ref[at, :] = rows.astype(BF16)


def add_out_body(n, me_ref, base_ref, *refs):
    mix_refs, (out_ref, scratch) = refs[:n], refs[n:]
    total = base_ref[...] + take_pieces(me_ref, mix_refs, scratch)
    out_ref[:, 0, :] = total[: out_ref.shape[0]]


def step_on(rows, step, n):
    return lax.ppermute(rows, "tensor", [(i, (i + step) % n) for i in range(n)])


def add_up(own, arrived):
    total = own.astype(F32)
    for rows in arrived:
        total = total + rows.astype(F32)
    return total.astype(BF16)


def tensor_scatter(pieces):
    return [step_on(pieces[step], step, len(pieces)) for step in range(1, len(pieces))]


def tensor_gather(own, n):
    return [own] + [step_on(own, step, n) for step in range(1, n)]


def tie(first, other):
    flat, tree = jax.tree.flatten((first, other))
    return jax.tree.unflatten(tree, lax.optimization_barrier(tuple(flat)))


def tensor_total(pieces):
    return tensor_gather(add_up(pieces[0], tensor_scatter(pieces)), len(pieces))


def swap(rows, axis, step, size):
    return lax.ppermute(rows, axis, [(i, i ^ step) for i in range(size)])


def group_exchange(rows, groups):
    blocks = rows.reshape(groups, -1, rows.shape[-1])
    moved = lax.all_to_all(blocks, GROUP_AXES, split_axis=0, concat_axis=0, tiled=True)
    return moved.reshape(rows.shape)


def on_device(
    n,
    groups,
    tokens,
    cotangent,
    routes,
    norm_gain,
    norm_bias,
    w_qkv,
    b_qv,
    w_out,
    b_out,
    w_router,
    w_in,
    b_in,
    w_exp_out,
    b_exp_out,
):
    layers = w_qkv.shape[0]
    images, seq_len, model_width = tokens.shape
    real = images * seq_len
    experts = w_router.shape[2]
    capacity = 3 * real // experts
    cap = ceil_to(capacity + 2, 16)
    slots = experts * cap
    local_cols = w_qkv.shape[3]
    heads = local_cols // HEAD_DIM
    hidden = w_in.shape[3]
    chunk = ceil_to(-(-real // n), 8)
    rows = n * chunk
    me = lax.axis_index("tensor").astype(I32).reshape(1)
    place = jnp.stack(
        [lax.axis_index(name) for name in ALL_AXES] + [lax.axis_index(GROUP_AXES)]
    ).astype(I32)

    tokens_in = tokens.reshape(real, model_width)
    cot = cotangent.reshape(real, model_width)
    ids_col = jnp.pad(
        routes.reshape(layers, real, 2), ((0, 0), (0, rows - real), (0, 0)), constant_values=-1
    )
    ids_row = ids_col.transpose(0, 2, 1)
    qkv_weights = w_qkv.transpose(0, 2, 3, 1).reshape(layers, 3 * local_cols, model_width)

    last = layers - 1
    stage = pltpu.VMEM((rows, model_width), F32)
    piece = ((chunk, model_width), BF16)
    high = w_router.astype(BF16)
    rest = w_router - high.astype(F32)
    middle = rest.astype(BF16)
    low = (rest - middle.astype(F32)).astype(BF16)
    router_parts = jnp.concatenate([high, middle, low], 2)

    def norms(layer, near=True):
        wrap = Near if near else Far
        return [wrap(norm_gain, layer), wrap(norm_bias, layer)]

    def attn_weights(layer, near=True):
        wrap = Near if near else Far
        return [wrap(qkv_weights, layer), wrap(b_qv, layer), wrap(w_out, layer)]

    def attn_fwd(layer, base, mix):
        packed = layer == last
        outs = [] if packed else [piece] * n
        outs = outs + ([((rows, model_width), F32, 1)] if mix else [])
        if packed:
            outs.append(((rows * local_cols // LANES, LANES), BF16))
        weights = attn_weights(layer, mix)
        got = kernel_call(
            functools.partial(attn_fwd_body, n, heads, real, bool(mix), packed),
            [me, Far(base), *mix, *norms(layer, mix), *(weights[:2] if packed else weights)],
            outs, [stage], scalars=1, name="attn_fwd",
        )
        at = 0 if packed else n
        return got[-1:] if packed else got[:n], got[at] if mix else base

    def moe_pre(layer, base, proj):
        buffers = [stage]
        if layer == last:
            proj = proj + [Far(w_out, layer)] + [v for pair in heads_out for v in pair]
            buffers.append(pltpu.VMEM((n - 1, local_cols, model_width), BF16))
        return kernel_call(
            functools.partial(moe_pre_body, n, layer, layer == last),
            [place, Far(base), *proj, b_out, *norms(layer), Far(router_parts, layer),
             Far(slot_row, layer)],
            [
                ((rows, model_width), F32, 1),
                ((rows, model_width), BF16, 1),
                ((rows, experts), F32, 1),
                ((slots, model_width), BF16, PARTS),
            ],
            buffers, scalars=1, name="moe_pre",
        )

    experts_in = w_in.reshape(layers, model_width, hidden)
    experts_out = w_exp_out.reshape(layers, hidden, model_width)

    def full_spec(shape):
        return pl.BlockSpec(shape, lambda i: (0,) * len(shape))

    def whole_spec(array):
        return pl.BlockSpec(array.shape, lambda i: (0,) * array.ndim)

    b_first = b_in.reshape(layers, 1, hidden)
    b_second = b_exp_out.reshape(layers, 1, model_width)

    side = local_cols // 2
    own_side = lax.dynamic_slice_in_dim(w_out[last], place[0] * side, side, 0)

    def far_heads(step):
        mine = step_on(own_side, step, n)
        return [mine, swap(mine, "dp", 1, 2)]

    saved, heads_out = [], [None] * (n - 1)
    stream, mix = tokens_in, ()
    for layer in range(layers):
        pieces, stream = attn_fwd(layer, stream, mix)
        if layer == 0:
            first_arrived = tensor_scatter(pieces)
            own_piece, late_cot = tie(pieces[0], cot)
        slot_col, slot_row, sent_cot = kernel_call(
            functools.partial(slots_body, experts, cap),
            [ids_col, ids_row, Far(late_cot)],
            [((layers, rows, 2), I32), ((layers, 2, rows), I32), ((slots, model_width), BF16, PARTS)],
            [stage], name="slots",
        )
        if layer == last:
            proj = tensor_gather(pieces[0], n)
        elif layer > 0:
            proj = tensor_total(pieces)
        else:
            first_arrived, sent_cot = tie(first_arrived, sent_cot)
            proj = tensor_gather(add_up(own_piece, first_arrived), n)
            cot_arrived = group_exchange(sent_cot, groups)
        got = moe_pre(layer, stream, proj)
        residual, a2, gate, sent = got[:4]
        if layer == 0:
            sent, cot_arrived = tie(sent, cot_arrived)
        if layer < last:
            arrived = group_exchange(sent, groups)
            if layer == last - 1:
                for step in range(1, n, 2):
                    arrived, heads_out[step - 1] = tie(arrived, far_heads(step))
            pre_act, result = kernel_call(
                functools.partial(ffn_fwd_body, 1.0 / n),
                [arrived, Far(experts_in, layer), Far(b_first, layer), Far(experts_out, layer),
                 Far(b_second, layer)],
                [((slots, hidden), BF16, PARTS), ((slots, model_width), BF16, PARTS)],
                name="ffn_fwd",
            )
            returned = group_exchange(result, groups)
            if layer == last - 1:
                for step in range(2, n, 2):
                    returned, heads_out[step - 1] = tie(returned, far_heads(step))
            got = kernel_call(
                functools.partial(combine_body, n),
                [me, returned, Far(slot_col, layer), Far(gate), Far(ids_col, layer)],
                [piece] * n + [((rows, model_width), BF16, 1)] * 2,
                [stage], scalars=1, name="combine",
            )
            mix = tensor_total(got[:n])
            saved.append((stream, residual, a2, gate, arrived, pre_act, got[n:]))
            stream = residual
        else:
            saved.append((stream, residual, a2, gate))

    half = (4 * local_cols) // 2
    chips = groups // 2
    qkv_shape = (layers, 3 * local_cols, model_width)
    out_shape = (layers, local_cols, model_width)

    def expert_grads(layer, ffn_ins, before):
        return block_call(
            ffn_grads_body,
            [pinned(v) for v in ffn_ins] + list(before or ()),
            ffn_outs,
            grid=(1,),
            in_specs=[whole_spec(v) for v in ffn_ins]
            + [pl.BlockSpec(memory_space=pl.ANY)] * (4 if before else 0),
            out_specs=[
                pl.BlockSpec((1,) + shape[1:], lambda i: (layer, 0, 0)) for shape, _ in ffn_outs
            ],
            vmem=28,
            aliases={len(ffn_ins) + i: i for i in range(4)} if before else None,
            name="ffn_grads",
        )

    def widen(given):
        return block_call(
            functools.partial(grad_widen_body, chips),
            [place, *given],
            [(qkv_shape, F32), (out_shape, F32)],
            grid=(1,),
            in_specs=[pl.BlockSpec(memory_space=pltpu.SMEM)]
            + [full_spec((half // chips, model_width))] * (2 * chips),
            out_specs=[
                pl.BlockSpec((1,) + shape[1:], lambda i: (1, 0, 0))
                for shape in (qkv_shape, out_shape)
            ],
            scratch=[pltpu.VMEM((2 * half, model_width), F32)],
            name="grad_widen",
        )

    def add_out():
        (total,) = kernel_call(
            functools.partial(add_out_body, n),
            [me, Far(saved[last][1]), *out_chunks],
            [((real, 1, model_width), F32)], [stage], scalars=1, name="add_out",
        )
        return total

    ffn_outs = [
        ((layers, model_width, hidden), F32),
        ((layers, 1, hidden), F32),
        ((layers, hidden, model_width), F32),
        ((layers, 1, model_width), F32),
    ]
    ffn_grads, wide, small, cuts = None, None, {}, {}
    upstream = cot
    for layer in reversed(range(layers)):
        stream, residual, a2, gate = saved[layer][:4]
        back_ins = [Far(slot_col, layer), Far(gate), Far(ids_col, layer), Far(a2),
                    Far(router_parts, layer)]
        if layer == last:
            arrived = group_exchange(sent, groups)
            result, dx, hid, dpre, grad_arrived = kernel_call(
                functools.partial(ffn_both_body, 1.0 / n, cap),
                [place, Far(router_parts, layer), arrived, cot_arrived, Far(experts_in, layer),
                 Far(b_first, layer), Far(experts_out, layer), Far(b_second, layer)],
                [((slots, model_width), BF16, PARTS)] * 2 + [((slots, hidden), BF16, PARTS)] * 2
                + [((slots, model_width), BF16, PARTS)],
                scalars=1, name="ffn_both",
            )
            dx = group_exchange(dx, groups)
            got = kernel_call(
                functools.partial(moe_back_body, n, cap, True),
                [me, dx, *back_ins],
                [piece] * n + [((experts, model_width), F32)],
                [stage], scalars=1, name="moe_back",
            )
            router_grad = got[n]
            ffn_grads = expert_grads(layer, [arrived, dpre, hid, grad_arrived], None)
        else:
            arrived, pre_act, (y0, y1) = saved[layer][4:]
            grad_arrived, cuts[layer + 1] = tie(
                group_exchange(sent_grad, groups), cuts[layer + 1]
            )
            if layer == last - 1:
                grad_arrived, out_arrived = tie(grad_arrived, tensor_scatter(out_mix))
                out_own = add_up(out_mix[0], out_arrived)
            dx, hid, dpre = kernel_call(
                ffn_back_body,
                [Far(experts_out, layer), Far(pre_act), Far(experts_in, layer), grad_arrived],
                [((slots, model_width), BF16, PARTS)] + [((slots, hidden), BF16, PARTS)] * 2,
                name="ffn_back",
            )
            ffn_grads = expert_grads(layer, [arrived, dpre, hid, grad_arrived], ffn_grads)
            dx = group_exchange(dx, groups)
            if layer == last - 1:
                dx, out_chunks = tie(dx, tensor_gather(out_own, n))
            got = kernel_call(
                functools.partial(moe_back_body, n, cap, False),
                [me, dx, *back_ins, Far(upstream), Far(y0), Far(y1)],
                [piece] * n + [((experts, model_width), F32)],
                [stage], scalars=1, name="moe_back",
            )
            router_grad = got[n]
        arrived = tensor_scatter(got[:n])
        if layer < last:
            above = cuts[layer + 1]
            ffn_grads, arrived = tie(ffn_grads, arrived)
            arrived, moved = tie(
                arrived, [swap(above[step], "expert", step, chips) for step in range(1, chips)]
            )
            grad_own = add_up(above[0], moved)
        da2 = tensor_gather(add_up(got[0], arrived), n)
        if layer < last:
            da2, moved = tie(
                da2, [swap(grad_own, "expert", step, chips) for step in range(1, chips)]
            )
            halves = [grad_own] + moved
        if layer == last - 1:
            da2, output = tie(da2, add_out())
        got = kernel_call(
            functools.partial(attn_back_body, n, heads, real),
            [place, Far(stream), Far(residual), *da2, Far(upstream), *norms(layer),
             *attn_weights(layer), router_grad],
            [piece] * n + [
                ((rows, model_width), F32, 1),
                ((half, model_width), BF16, 1),
                ((half, model_width), BF16),
                ((8 + experts, model_width), F32),
            ],
            [stage, pltpu.VMEM((2, half, model_width), BF16)], scalars=1, name="attn_back",
        )
        dr, small[layer] = got[n], got[-1]
        keep, send = got[n + 1 : n + 3]
        if layer < last:
            halves += [swap(rows_of, "dp", 1, 2) for rows_of in halves]
        if layer > 0:
            arrived = tensor_scatter(got[:n])
            if layer == last:
                ffn_grads, arrived = tie(ffn_grads, arrived)
            da1 = tensor_gather(add_up(got[0], arrived), n)
            if layer == last:
                da1, returned = tie(da1, group_exchange(result, groups))
                out_mix = kernel_call(
                    functools.partial(combine_body, n),
                    [me, returned, Far(slot_col, layer), Far(gate), Far(ids_col, layer)],
                    [piece] * n, [stage], scalars=1, name="combine",
                )
            da1, got_half = tie(da1, swap(send, "dp", 1, 2))
            cuts[layer] = kernel_call(
                functools.partial(grad_cut_body, chips),
                [place, Far(keep), got_half],
                [((half // chips, model_width), BF16)] * chips,
                [pltpu.VMEM((half, model_width), F32)], scalars=1, name="grad_cut",
            )
        else:
            smalls = jnp.concatenate([small[at] for at in range(layers)], 0).astype(BF16)
            spare = ceil_to(smalls.shape[0], 16) - smalls.shape[0]
            smalls = jnp.pad(smalls, ((0, spare), (0, 0)))
            cut = kernel_call(
                functools.partial(grad_cut_body, chips),
                [place, Far(keep), swap(send, "dp", 1, 2)],
                [((half // chips, model_width), BF16)] * chips,
                [pltpu.VMEM((half, model_width), F32)], scalars=1, name="grad_cut",
            )
            cut, smalls = tie(cut, smalls)
            moved = [swap(cut[step], "expert", step, chips) for step in range(1, chips)]
            others = [step_on(smalls, step, n) for step in range(1, n)]
            moved, (others, wide) = tie(moved, (others, widen(halves)))
            (own,) = kernel_call(
                functools.partial(add_beside_body, chips),
                [cut[0], *moved, smalls, *others],
                [((half // chips + smalls.shape[0], model_width), BF16)],
                name="add_beside",
            )
            da1 = tensor_total(got[:n])
            own_half = [own] + [swap(own, "expert", step, chips) for step in range(1, chips)]
            own_half, da1 = tie(own_half, da1)
            pieces = own_half + [swap(rows_of, "dp", 1, 2) for rows_of in own_half]
        ins = [me, Far(stream), *da1, Far(dr), Near(norm_gain, layer)]
        if layer > 0:
            below = layer - 1
            upstream, sent_grad = kernel_call(
                functools.partial(norm_one_back_body, n, True),
                ins + [Far(saved[below][3]), Far(ids_col, below), Far(slot_row, below)],
                [((rows, model_width), F32, 1), ((slots, model_width), BF16, PARTS)],
                [stage], scalars=1, name="norm_back_send",
            )
        else:
            (grad_tokens,) = kernel_call(
                functools.partial(norm_one_back_body, n, False),
                ins, [((real, 1, model_width), F32)], [stage], scalars=1, name="norm_back",
            )
    g1, gb1, g2, gb2 = ffn_grads

    small_shapes = [
        (layers, 2, model_width),
        (layers, 2, model_width),
        (layers, 2, local_cols),
        (layers, model_width),
        (layers, experts, model_width),
    ]
    given = list(wide or ())
    qkv_grad, out_grad, gain_grad, shift_grad, qv_grad, outb_grad, router_out = block_call(
        functools.partial(grad_join_body, layers, chips, n),
        [place, *pieces, *given],
        [(shape, F32) for shape in (qkv_shape, out_shape, *small_shapes)],
        grid=(1,),
        in_specs=[pl.BlockSpec(memory_space=pltpu.SMEM)]
        + [full_spec(pieces[0].shape)] * (2 * chips)
        + [pl.BlockSpec(memory_space=pl.ANY)] * len(given),
        out_specs=[
            pl.BlockSpec((1,) + shape[1:], lambda i: (0, 0, 0)) for shape in (qkv_shape, out_shape)
        ]
        + [full_spec(shape) for shape in small_shapes],
        scratch=[pltpu.VMEM((2 * half, model_width), F32)],
        vmem=24,
        aliases={1 + 2 * chips + i: i for i in range(len(given))},
        name="grad_join",
    )
    qkv_grad = qkv_grad.reshape(layers, 3, local_cols, model_width).transpose(0, 3, 1, 2)
    return (
        output.reshape(images, seq_len, model_width),
        grad_tokens.reshape(images, seq_len, model_width),
        gain_grad,
        shift_grad,
        qkv_grad,
        qv_grad,
        out_grad,
        outb_grad,
        router_out.transpose(0, 2, 1),
        g1[:, None],
        gb1,
        g2[:, None],
        gb2,
    )


def solution(mesh):
    n = mesh.shape["tensor"]
    groups = mesh.shape["dp"] * mesh.shape["expert"]
    return jax.shard_map(
        functools.partial(on_device, n, groups),
        mesh=mesh,
        in_specs=(
            P(("dp", "expert"), None, None),
            P(("dp", "expert"), None, None),
            P(None, ("dp", "expert"), None, None),
            P(),
            P(),
            P(None, None, None, "tensor"),
            P(None, None, "tensor"),
            P(None, "tensor", None),
            P(),
            P(),
            P(None, ("dp", "expert"), None, "tensor"),
            P(None, ("dp", "expert"), "tensor"),
            P(None, ("dp", "expert"), "tensor", None),
            P(None, ("dp", "expert"), None),
        ),
        out_specs=(
            P(("dp", "expert"), None, None),
            P(("dp", "expert"), None, None),
            P(),
            P(),
            P(None, None, None, "tensor"),
            P(None, None, "tensor"),
            P(None, "tensor", None),
            P(),
            P(),
            P(None, ("dp", "expert"), None, "tensor"),
            P(None, ("dp", "expert"), "tensor"),
            P(None, ("dp", "expert"), "tensor", None),
            P(None, ("dp", "expert"), None),
        ),
        check_vma=False,
    )
```
